32 devices in a mesh: ctx: 16 (over z, x, core), head: 2 (over y).
Axes of the slice: x: 2, y: 2, z: 4, core: 2. Of those that a mesh axis runs over, the one named last changes fastest.
Arguments:
- queries: bfloat16 [3120, 768], P('ctx', 'head'), may hold values from -6 to 6
- keys: bfloat16 [3120, 768], P('ctx', 'head'), may hold values from -6 to 6
- values: bfloat16 [3120, 768], P('ctx', 'head'), may hold values from -6 to 6
- rates: float32 [3120, 6], P('ctx', 'head'), may hold values from 0.1 to 1
- frame_update: int32 [16], P('ctx'), may hold values 0 or 1
- fast_weights: float32 [3, 6, 512, 128], P(None, 'head', 'ctx'), may hold values from -2 to 2
- gain: float32 [768], P('head'), may hold values from 0.5 to 1.5
Outputs:
- block_out: bfloat16 [3120, 768], P('ctx', 'head')
- new_weights: float32 [3, 6, 512, 128], P(None, 'head', 'ctx')
The draws below stay inside these ranges and needn't reach their ends.
All inputs are finite; a program needn't handle non-finite values. No bound on the sum of `frame_update` on one device may be relied on, other than what follows from the above.
Results may differ from the reference program's by a relative error of at most 0.0071.
Values may be sent and summed in bfloat16 or wider, within the bound.
No kernel may reach another device: no remote copies, remote signals or barrier semaphores. Data moves between devices by JAX's collectives and lax.ppermute only.
A program may use at most 64 MiB of HBM per device.

```python
import math
import jax
import jax.numpy as jnp
from jax import lax

HD = 128
HID = 512
FRAME = 195
NS_STEPS = 5
HEADS = 6
FRAMES = 16
TOKENS = 3120


def draw_queries(key, part):
    key = jax.random.fold_in(key, 5)
    base = jnp.clip(jax.random.normal(key, (TOKENS, HEADS * HD), jnp.float32), -6.0, 6.0)
    return base.astype(jnp.bfloat16)


def draw_keys(key, part):
    key = jax.random.fold_in(key, 7)
    base = jnp.clip(jax.random.normal(key, (TOKENS, HEADS * HD), jnp.float32), -6.0, 6.0)
    return base.astype(jnp.bfloat16)


def draw_fast_weights(key, part):
    key = jax.random.fold_in(key, 9)
    noise_key = jax.random.fold_in(key, 0)
    base = jnp.clip(jax.random.normal(noise_key, (3, HEADS, HID, HD), jnp.float32), -5.0, 5.0)
    rise = 3.0 ** (jnp.arange(HEADS, dtype=jnp.float32) / max(HEADS - 1, 1))
    ones_row = jnp.ones((HEADS,), jnp.float32)
    scale = jnp.stack([ones_row * HD ** (-0.5), ones_row * HD ** (-0.5), rise * HID ** (-0.5)])
    return jnp.clip(base * scale[:, :, None, None], -2.0, 2.0)


def with_ends(drawn, rng, smallest, top_value):
    index_at = [jax.random.randint(jax.random.fold_in(rng, axis), (), 0, length) for axis, length in enumerate(drawn.shape)]
    widest = drawn.shape.index(max(drawn.shape))
    beside = index_at[:widest] + [(index_at[widest] + 1) % drawn.shape[widest]] + index_at[widest + 1:]
    return drawn.at[tuple(index_at)].set(smallest).at[tuple(beside)].set(top_value)


def level_of(key, shape, pieces, least, high):
    def one(dim, shards_of):
        draws = jax.random.uniform(jax.random.fold_in(jax.random.fold_in(key, 6), dim), (shards_of,), jnp.float32, least / len(pieces), high / len(pieces))
        return jnp.repeat(jnp.exp(draws), shape[dim] // shards_of).reshape((-1,) + (1,) * (len(shape) - dim - 1))

    loudness = one(*pieces[0])
    for cut in pieces[1:]:
        loudness = loudness * one(*cut)
    return loudness


def gaussian(key, extent, scale, most, shards=(), held_as=jnp.bfloat16):
    entries = scale * jax.random.normal(key, extent, jnp.float32)
    if shards:
        entries = entries * level_of(key, extent, shards, -0.22, 0.18)
    return jnp.clip(entries, -most, most).astype(held_as)


def setup_inputs(seed: int = 0) -> dict:
    arg_keys = jax.random.split(jax.random.key(seed), 8)
    queries = draw_queries(jax.random.fold_in(arg_keys[7], 71), 0)
    keys = draw_keys(jax.random.fold_in(arg_keys[7], 71), 0)
    values = gaussian(arg_keys[2], (TOKENS, HEADS * HD), 1.0, 6.0, ((0, 16), (1, 2)))
    rates = jnp.clip(jnp.exp(math.log(1.0) - 2.3025851 * jax.random.uniform(arg_keys[3], (TOKENS, HEADS), jnp.float32) ** level_of(arg_keys[3], (TOKENS, HEADS), ((0, 16), (1, 2)), -0.2, 0.2)), 0.1, 1.0)
    frame_update = with_ends((jax.random.randint(arg_keys[4], (FRAMES,), 0, 4) < 3).astype(jnp.int32), jax.random.fold_in(arg_keys[4], 1), 0, 1)
    fast_weights = draw_fast_weights(jax.random.fold_in(arg_keys[7], 71), 0)
    gain = jnp.clip(1.0 + 0.1 * jax.random.normal(arg_keys[6], (HEADS * HD,), jnp.float32), 0.5, 1.5)
    return {"queries": queries, "keys": keys, "values": values, "rates": rates, "frame_update": frame_update, "fast_weights": fast_weights, "gain": gain}


epsilon = 1e-06
quintic_a = 3.4445
quintic_b = -4.775
quintic_c = 2.0315
highest = lax.Precision.HIGHEST

def frame_attention(queries, keys, values):
    frame_count = queries.shape[0] // FRAME
    head_count = queries.shape[1] // HD
    shaped_q = queries.reshape(frame_count, FRAME, head_count, HD)
    shaped_k = keys.reshape(frame_count, FRAME, head_count, HD)
    shaped_v = values.reshape(frame_count, FRAME, head_count, HD)
    before_k = jnp.concatenate([jnp.zeros_like(shaped_k[:1]), shaped_k[:-1]], axis=0)
    before_v = jnp.concatenate([jnp.zeros_like(shaped_v[:1]), shaped_v[:-1]], axis=0)
    frame_ids = jnp.arange(frame_count, dtype=jnp.int32)

    def one_frame(items):
        query_block, key_block, value_block, key_before, value_before, frame_id = items
        key_window = jnp.concatenate([key_before, key_block], axis=0).astype(jnp.float32)
        value_window = jnp.concatenate([value_before, value_block], axis=0).astype(jnp.float32)
        scores = jnp.einsum('qhd,khd->hqk', query_block.astype(jnp.float32), key_window) * HD ** (-0.5)
        valid = jnp.concatenate([jnp.full((FRAME,), frame_id > 0), jnp.ones((FRAME,), jnp.bool_)])
        scores = jnp.where(valid[None, None, :], scores, -1e+30)
        row_max = lax.optimization_barrier(jnp.max(scores, axis=2, keepdims=True))
        weights_exp = jnp.exp(scores - row_max)
        probs = (weights_exp / lax.optimization_barrier(jnp.sum(weights_exp, axis=2, keepdims=True))).astype(jnp.bfloat16)
        attended = jnp.einsum('hqk,khd->qhd', probs.astype(jnp.float32), value_window)
        return attended.reshape(FRAME, head_count * HD)
    blocks = lax.map(one_frame, (shaped_q, shaped_k, shaped_v, before_k, before_v, frame_ids))
    return blocks.reshape(frame_count * FRAME, head_count * HD)

def head_terms(items):
    query_h, key_h, value_h, rate_h, weights_h = items
    proj_one = jnp.dot(query_h, weights_h[0].T, preferred_element_type=jnp.float32)
    proj_three = jnp.dot(query_h, weights_h[1].T, preferred_element_type=jnp.float32)
    hidden_q = (jax.nn.silu(proj_one) * proj_three).astype(jnp.bfloat16)
    fast_out = jnp.dot(hidden_q, weights_h[2], preferred_element_type=jnp.float32)
    pre_one = jnp.dot(key_h, weights_h[0].T, preferred_element_type=jnp.float32)
    pre_three = jnp.dot(key_h, weights_h[1].T, preferred_element_type=jnp.float32)
    gate_act = jax.nn.silu(pre_one)
    act = (gate_act * pre_three).astype(jnp.bfloat16)
    target = (rate_h[:, None] * value_h.astype(jnp.float32)).astype(jnp.bfloat16)
    back = jnp.dot(target, weights_h[2].T, preferred_element_type=jnp.float32)
    sigmoid_pre = jax.nn.sigmoid(pre_one)
    delta_one = (back * pre_three * sigmoid_pre * (1.0 + pre_one * (1.0 - sigmoid_pre))).astype(jnp.bfloat16)
    delta_three = (back * gate_act).astype(jnp.bfloat16)
    grad_one = jnp.dot(delta_one.T, key_h, preferred_element_type=jnp.float32)
    grad_three = jnp.dot(delta_three.T, key_h, preferred_element_type=jnp.float32)
    grad_two = jnp.dot(act.T, target, preferred_element_type=jnp.float32)
    return (fast_out, jnp.stack([grad_one, grad_three, grad_two]))

def reference(queries, keys, values, rates, frame_update, fast_weights, gain):
    head_count = queries.shape[1] // HD
    tokens_all = queries.shape[0]
    low_weights = fast_weights.astype(jnp.bfloat16)
    attended = frame_attention(queries, keys, values)
    keep_token = jnp.repeat(frame_update.astype(jnp.float32), FRAME)
    split_q = queries.reshape(tokens_all, head_count, HD).transpose(1, 0, 2)
    split_k = keys.reshape(tokens_all, head_count, HD).transpose(1, 0, 2)
    split_v = values.reshape(tokens_all, head_count, HD).transpose(1, 0, 2)
    rate_heads = (rates * keep_token[:, None]).T
    fast_out, grads = lax.map(head_terms, (split_q, split_k, split_v, rate_heads, low_weights.transpose(1, 0, 2, 3)))
    fast_out = fast_out.transpose(1, 0, 2).reshape(tokens_all, head_count * HD)
    spread = lax.optimization_barrier(jnp.mean(fast_out * fast_out, axis=1, keepdims=True))
    block_out = (attended + fast_out * gain[None, :] * lax.rsqrt(spread + epsilon)).astype(jnp.bfloat16)
    grads = grads.transpose(1, 0, 2, 3)
    squares = lax.optimization_barrier(jnp.sum(grads * grads, axis=(2, 3), keepdims=True))
    ortho = grads * lax.rsqrt(squares + epsilon)
    for section_index in range(NS_STEPS):
        gram_matrix = jnp.einsum('mhjd,mhje->mhde', ortho, ortho, precision=highest)
        square_gram = jnp.einsum('mhde,mhef->mhdf', gram_matrix, gram_matrix, precision=highest)
        mix_matrix = quintic_b * gram_matrix + quintic_c * square_gram
        ortho = quintic_a * ortho + jnp.einsum('mhjd,mhde->mhje', ortho, mix_matrix, precision=highest)
    summed = fast_weights + ortho
    old_norm = jnp.sqrt(lax.optimization_barrier(jnp.sum(fast_weights * fast_weights, axis=3, keepdims=True)))
    new_weights = summed * old_norm * lax.rsqrt(lax.optimization_barrier(jnp.sum(summed * summed, axis=3, keepdims=True)) + epsilon)
    return (block_out, new_weights)
```

```python
import functools

import jax
import jax.numpy as jnp
import numpy as np
from jax import lax
from jax.experimental import pallas as pl
from jax.experimental.pallas import tpu as pltpu
from jax.sharding import Mesh, PartitionSpec as P

HD = 128
NS_STEPS = 5

epsilon = 1e-06
quintic_a = 3.4445
quintic_b = -4.775
quintic_c = 2.0315
highest = lax.Precision.HIGHEST
f32 = jnp.float32
bf16 = jnp.bfloat16
VMEM_LIMIT = 24 * 1024 * 1024
VMEM_MOST = 56 * 1024 * 1024


def dot(a, b, contract, precision=None):
    return lax.dot_general(
        a, b, ((contract[:1], contract[1:]), ((), ())),
        precision=precision, preferred_element_type=f32,
    )


def call(body, outs, scratch=(), in_specs=None, flops=1e8, **kw):
    given = {} if in_specs is None else {"in_specs": in_specs}
    return pl.pallas_call(
        body,
        out_shape=outs,
        **given,
        scratch_shapes=list(scratch),
        compiler_params=pltpu.CompilerParams(vmem_limit_bytes=VMEM_LIMIT),
        cost_estimate=pl.CostEstimate(flops=int(flops), bytes_accessed=1 << 20, transcendentals=0),
        **kw,
    )


smem = pl.BlockSpec(memory_space=pltpu.SMEM)
vmem = pl.BlockSpec(memory_space=pltpu.VMEM)


def sds(shape, dtype):
    return jax.ShapeDtypeStruct(shape, dtype)


def prep_body(heads, group, tokens, place, update, w_ref, k_ref, v_ref, q_ref, rate_ref, *outs):
    w_out, kv_out = outs[:2]
    token_outs = outs[2:]
    padded = kv_out.shape[0]
    slots = w_out.shape[0] // group
    for j in range(group):
        for m in range(3):
            low = w_ref[m, min(j, heads - 1)].astype(bf16)
            for z in range(slots):
                w_out[z * group + j, m] = low
    valid = lax.broadcasted_iota(jnp.int32, (padded, 1), 0) < tokens
    none = jnp.zeros((), bf16)
    keep = update[0].astype(f32)
    row = lax.broadcasted_iota(jnp.int32, (heads, HD), 0)
    for d in range(group):
        head = jnp.minimum(place[1] ^ d, heads - 1)
        cols = pl.ds(pl.multiple_of(head * HD, HD), HD)
        rate = dot(rate_ref[...], (row == head).astype(f32), (0, 0), highest)[:padded]
        target = ((rate * keep) * v_ref[:, cols].astype(f32)).astype(bf16)
        token_outs[d][:, :HD] = jnp.where(valid, k_ref[:, cols], none)
        token_outs[d][:, HD : 2 * HD] = jnp.where(valid, target, none)
        token_outs[d][:, 2 * HD :] = jnp.where(valid, q_ref[:, cols], none)
    kv_out[:, : heads * HD] = jnp.where(valid, k_ref[...], none)
    kv_out[:, heads * HD :] = jnp.where(valid, v_ref[...], none)


def grad_body(group, slots, place, *refs):
    token_refs, w_ref = refs[:group], refs[group]
    outs = refs[group + 1 : group + 1 + slots]
    k_all, t_all, grads = refs[group + 1 + slots :]
    padded = token_refs[0].shape[0]
    width = k_all.shape[0]
    for d in range(group):
        k_all[d * padded : (d + 1) * padded] = token_refs[d][:, :HD]
        t_all[d * padded : (d + 1) * padded] = token_refs[d][:, HD : 2 * HD]
    if width > group * padded:
        k_all[group * padded :] = jnp.zeros((width - group * padded, HD), bf16)
        t_all[group * padded :] = jnp.zeros((width - group * padded, HD), bf16)
    hidden = grads.shape[1]
    block = 128
    key, target = k_all[...], t_all[...]
    for start in range(0, hidden, block):
        rows = slice(start, start + block)
        w1, w3, w2 = (weight_rows(w_ref, m, start, block) for m in range(3))
        pre_one = dot(w1, key, (1, 1))
        pre_three = dot(w3, key, (1, 1))
        back = dot(w2, target, (1, 1))
        sig = jax.nn.sigmoid(pre_one)
        gate = pre_one * sig
        act = (gate * pre_three).astype(bf16)
        delta_one = (back * pre_three * sig * (1.0 + pre_one * (1.0 - sig))).astype(bf16)
        delta_three = (back * gate).astype(bf16)
        grads[0, rows] = dot(delta_one, key, (1, 0)).astype(bf16)
        grads[1, rows] = dot(delta_three, key, (1, 0)).astype(bf16)
        grads[2, rows] = dot(act, target, (1, 0)).astype(bf16)
    for d in range(slots):
        matrix = lax.rem((place[0] ^ d) - place[1] + group * slots, slots)
        chosen = grads[jnp.minimum(matrix, 2)]
        outs[d][...] = jnp.where(matrix < 3, chosen, jnp.zeros_like(chosen))


def weight_rows(w_ref, m, start, block):
    if len(w_ref.shape) == 3:
        return w_ref[m, start : start + block]
    rows = w_ref.shape[2]
    return w_ref[start // rows : (start + block) // rows, m].reshape(block, HD)


def apply_body(group, place, *refs):
    token_refs, w_ref, out = refs[:group], refs[group], refs[group + 1]
    hidden = w_ref.shape[1] if len(w_ref.shape) == 3 else w_ref.shape[0] * w_ref.shape[2]
    w1, w3, w2 = (weight_rows(w_ref, m, 0, hidden) for m in range(3))
    for d in range(group):
        query = token_refs[d][:, 2 * HD :]
        proj_one = dot(query, w1, (1, 1))
        proj_three = dot(query, w3, (1, 1))
        act = (proj_one * jax.nn.sigmoid(proj_one) * proj_three).astype(bf16)
        out[place[1] ^ d] = dot(act, w2, (1, 0)).astype(out.dtype)


def ortho_body(*refs):
    parts, out = refs[:-1], refs[-1]
    grads = parts[0][...].astype(f32)
    for part in parts[1:]:
        grads = grads + part[...].astype(f32)
    square = jnp.sum(jnp.sum(grads * grads, axis=0, keepdims=True), axis=1, keepdims=True)
    ortho = grads * lax.rsqrt(square + epsilon)
    gram = dot(ortho, ortho, (0, 0), highest)
    eye = (
        lax.broadcasted_iota(jnp.int32, (HD, HD), 0) == lax.broadcasted_iota(jnp.int32, (HD, HD), 1)
    ).astype(f32)
    total = None
    for step in range(NS_STEPS):
        square_gram = dot(gram, gram, (1, 0), highest)
        mix = quintic_a * eye + quintic_b * gram + quintic_c * square_gram
        if step < NS_STEPS - 1:
            gram = dot(dot(gram, mix, (1, 0), highest), mix, (1, 0), highest)
        total = mix if total is None else dot(total, mix, (1, 0), highest)
    out[...] = dot(ortho, total, (1, 0), highest).astype(out.dtype)


def finish_body(slots, group, w_ref, rows_ref, out):
    heads = w_ref.shape[1]
    for m in range(3):
        for h in range(heads):
            weights = w_ref[m, h]
            summed = weights + rows_ref[((m + h) % slots) * group + h].astype(f32)
            old = jnp.sqrt(jnp.sum(weights * weights, axis=1, keepdims=True))
            new = lax.rsqrt(jnp.sum(summed * summed, axis=1, keepdims=True) + epsilon)
            out[m, h] = summed * (old * new)


def attend_body(heads, tokens, place, q_ref, own_ref, back_ref, out):
    padded = own_ref.shape[0]
    span = heads * HD
    column = lax.broadcasted_iota(jnp.int32, (1, 2 * padded), 1)
    first = (place[0] == 0) & (place[1] == 0)
    stop = jnp.where(first, padded, padded + tokens)
    live = (column < tokens) | ((column >= padded) & (column < stop))
    for h in range(heads):
        cols = slice(h * HD, (h + 1) * HD)
        key = jnp.concatenate([own_ref[:, cols], back_ref[:, cols]], axis=0)
        vcols = slice(span + h * HD, span + (h + 1) * HD)
        value = jnp.concatenate([own_ref[:, vcols], back_ref[:, vcols]], axis=0)
        scores = dot(q_ref[:, cols], key, (1, 1)) * (HD ** (-0.5))
        scores = jnp.where(live, scores, -1e30)
        weights = jnp.exp(scores - jnp.max(scores, axis=1, keepdims=True))
        probs = (weights / jnp.sum(weights, axis=1, keepdims=True)).astype(bf16)
        out[:, cols] = dot(probs, value, (1, 0))


def assemble_body(heads, slots, out, squares):
    for h in range(heads):
        out[:, h * HD : (h + 1) * HD] = slots[h]
    fast = out[...].astype(f32)
    squares[...] = dot(jnp.ones((8, heads * HD), f32), fast * fast, (1, 1), highest)


def block_body(features, gain_ref, attended_ref, fast_ref, *refs):
    squares, out = refs[:-1], refs[-1]
    total = squares[0][...]
    for other in squares[1:]:
        total = total + other[...]
    pick = (lax.broadcasted_iota(jnp.int32, (8, HD), 0) == 0).astype(f32)
    spread = dot(total, pick, (0, 0), highest) * (1.0 / features)
    scale = lax.rsqrt(spread + epsilon)
    for h in range(fast_ref.shape[1] // HD):
        cols = slice(h * HD, (h + 1) * HD)
        out[:, cols] = (
            attended_ref[:, cols] + fast_ref[:, cols].astype(f32) * gain_ref[:, cols] * scale
        ).astype(bf16)


def on_device(queries, keys, values, rates, frame_update, fast_weights, gain):
    tokens = queries.shape[0]
    heads = queries.shape[1] // HD
    rows_local = fast_weights.shape[2]
    nz, group, nh = lax.axis_size("z"), lax.axis_size("grp"), lax.axis_size("head")
    count = nz * group
    hidden = count * rows_local
    place = jnp.stack([lax.axis_index("z"), lax.axis_index("grp")]).astype(jnp.int32)
    padded = -(-tokens // 16) * 16
    span = heads * HD

    def whole(*shape):
        return pl.BlockSpec(shape, lambda i: (0,) * len(shape))

    low_shape = (count, 3, rows_local, HD)
    prepared = pl.pallas_call(
        functools.partial(prep_body, heads, group, tokens),
        grid=(1,),
        out_shape=[sds(low_shape, bf16), sds((padded, 2 * span), bf16)]
        + [sds((padded, 3 * HD), bf16)] * group,
        in_specs=[smem, smem, whole(*fast_weights.shape)]
        + [whole(padded, span)] * 3
        + [whole(heads, -(-padded // 128) * 128)],
        out_specs=[whole(*low_shape), whole(padded, 2 * span)]
        + [whole(padded, 3 * HD)] * group,
        compiler_params=pltpu.CompilerParams(vmem_limit_bytes=VMEM_MOST),
    )(place, frame_update, fast_weights, keys, values, queries, rates.T)
    low, kv_own, token_slots = prepared[0], prepared[1], list(prepared[2:])

    weights = lax.all_to_all(low, ("z", "grp"), 0, 0, tiled=True)
    if rows_local % 16:
        weights = weights.transpose(1, 0, 2, 3).reshape(3, hidden, HD)
    for d in range(1, group):
        pairs = [(s, s ^ d) for s in range(group) if s ^ d < heads]
        token_slots[d] = lax.ppermute(token_slots[d], "grp", pairs)

    width = -(-group * padded // 128) * 128
    partials = list(
        call(
            functools.partial(grad_body, group, nz),
            [sds((hidden, HD), bf16)] * nz,
            scratch=[
                pltpu.VMEM((width, HD), bf16),
                pltpu.VMEM((width, HD), bf16),
                pltpu.VMEM((3, hidden, HD), bf16),
            ],
            in_specs=[smem] + [vmem] * (group + 1),
            flops=1e9,
        )(place, *token_slots, weights)
    )
    kv_own, weights, partials[0] = lax.optimization_barrier((kv_own, weights, partials[0]))
    for d in range(1, nz):
        pairs = []
        for z in range(nz):
            pairs += [
                (z * group + j, (z ^ d) * group + j)
                for j in range(heads)
                if ((z ^ d) - j) % nz < 3
            ]
        partials[d] = lax.ppermute(partials[d], ("z", "grp"), pairs)

    fast_slots = call(
        functools.partial(apply_body, group),
        sds((group, padded, HD), bf16),
        in_specs=[smem] + [vmem] * (group + 1),
        flops=5e8,
    )(place, *token_slots, weights)
    queries, fast_slots = lax.optimization_barrier((queries, fast_slots))
    fast_slots = lax.all_to_all(fast_slots, "grp", 0, 0, tiled=True)

    ring = [(i, i + 1) for i in range(count - 1)]
    kv_back = lax.ppermute(kv_own, ("z", "grp"), ring)
    attended = pl.pallas_call(
        functools.partial(attend_body, heads, tokens),
        grid=(1,),
        out_shape=sds((padded, span), f32),
        in_specs=[smem, whole(padded, span)] + [whole(padded, 2 * span)] * 2,
        out_specs=whole(padded, span),
        compiler_params=pltpu.CompilerParams(vmem_limit_bytes=VMEM_LIMIT),
    )(place, queries, kv_own, kv_back)
    attended, partials[0] = lax.optimization_barrier((attended, partials[0]))

    ortho = call(ortho_body, sds((hidden, HD), bf16), flops=1e9)(*partials)
    rows = lax.all_to_all(
        ortho.reshape(count, rows_local, HD), ("z", "grp"), 0, 0, tiled=True
    )
    new_weights = call(
        functools.partial(finish_body, nz, group), sds(fast_weights.shape, f32), flops=1e6
    )(fast_weights, rows)

    fast, squares = call(
        functools.partial(assemble_body, heads),
        [sds((padded, span), bf16), sds((8, padded), f32)],
        flops=1e7,
    )(fast_slots)
    all_squares = [squares] + [
        lax.ppermute(squares, "head", [(s, (s + d) % nh) for s in range(nh)]) for d in range(1, nh)
    ]
    block_out = pl.pallas_call(
        functools.partial(block_body, span * nh),
        grid=(1,),
        out_shape=sds((tokens, span), bf16),
        in_specs=[whole(1, span), whole(padded, span), whole(padded, span)]
        + [whole(8, padded)] * nh,
        out_specs=whole(padded, span),
        compiler_params=pltpu.CompilerParams(vmem_limit_bytes=VMEM_LIMIT),
    )(gain.reshape(1, span), attended, fast, *all_squares)
    return (block_out, new_weights)


def solution(mesh):
    group = 4
    nh = mesh.shape["head"]
    inner = Mesh(
        np.asarray(mesh.devices).reshape(mesh.shape["ctx"] // group, group, nh),
        ("z", "grp", "head"),
    )
    ctx = ("z", "grp")
    placed = (
        P(ctx, "head"),
        P(ctx, "head"),
        P(ctx, "head"),
        P(ctx, "head"),
        P(ctx),
        P(None, "head", ctx, None),
        P("head"),
    )
    return jax.shard_map(
        on_device,
        mesh=inner,
        in_specs=placed,
        out_specs=(P(ctx, "head"), P(None, "head", ctx, None)),
        check_vma=False,
    )
```

```python
import functools

import jax
import jax.numpy as jnp
import numpy as np
from jax import lax
from jax.experimental import pallas as pl
from jax.experimental.pallas import tpu as pltpu
from jax.sharding import Mesh, PartitionSpec as P

HD = 128
NS_STEPS = 5

epsilon = 1e-06
quintic_a = 3.4445
quintic_b = -4.775
quintic_c = 2.0315
highest = lax.Precision.HIGHEST
f32 = jnp.float32
bf16 = jnp.bfloat16
VMEM_LIMIT = 24 * 1024 * 1024
VMEM_MOST = 56 * 1024 * 1024


def dot(a, b, contract, precision=None):
    return lax.dot_general(
        a, b, ((contract[:1], contract[1:]), ((), ())),
        precision=precision, preferred_element_type=f32,
    )


def call(body, outs, scratch=(), in_specs=None, flops=1e8, moved=1 << 20, **kw):
    given = {} if in_specs is None else {"in_specs": in_specs}
    return pl.pallas_call(
        body,
        out_shape=outs,
        **given,
        scratch_shapes=list(scratch),
        compiler_params=pltpu.CompilerParams(vmem_limit_bytes=VMEM_LIMIT),
        cost_estimate=pl.CostEstimate(flops=int(flops), bytes_accessed=moved, transcendentals=0),
        **kw,
    )


def sds(shape, dtype):
    return jax.ShapeDtypeStruct(shape, dtype)


def served(n):
    return [0] + list(range(n - 1, 0, -1))


def position():
    return lax.axis_index("z"), lax.axis_index("grp")


def sigmoid(x):
    return 0.5 * jnp.tanh(0.5 * x) + 0.5


def prep_body(heads, group, tokens, update, w_ref, k_ref, v_ref, q_ref, rate_ref, *outs):
    w_out, kv_out = outs[:2]
    token_outs = outs[2:]
    padded = kv_out.shape[0]
    slots = w_out.shape[0] // group
    for j in range(group):
        for m in range(3):
            low = w_ref[m, min(j, heads - 1)].astype(bf16)
            for z in range(slots):
                w_out[z * group + j, m] = low
    place = position()
    valid = lax.broadcasted_iota(jnp.int32, (padded, 1), 0) < tokens
    none = jnp.zeros((), bf16)
    keep = update[...].astype(f32)
    row = lax.broadcasted_iota(jnp.int32, (heads, HD), 0)
    for d in range(group):
        head = jnp.minimum(place[1] ^ d, heads - 1)
        cols = pl.ds(pl.multiple_of(head * HD, HD), HD)
        rate = dot(rate_ref[...], (row == head).astype(f32), (0, 0), highest)[:padded]
        target = ((rate * keep) * v_ref[:, cols].astype(f32)).astype(bf16)
        token_outs[d][:, :HD] = jnp.where(valid, k_ref[:, cols], none)
        token_outs[d][:, HD : 2 * HD] = jnp.where(valid, target, none)
        token_outs[d][:, 2 * HD :] = jnp.where(valid, q_ref[:, cols], none)
    kv_out[:, : heads * HD] = jnp.where(valid, k_ref[...], none)
    kv_out[:, heads * HD :] = jnp.where(valid, v_ref[...], none)


def gradients(token_refs, w_ref, k_all, t_all, staged, deltas):
    padded = token_refs[0].shape[0]
    width = k_all.shape[0]
    filled = len(token_refs) * padded
    for i, ref in enumerate(token_refs):
        k_all[i * padded : (i + 1) * padded] = ref[:, :HD]
        t_all[i * padded : (i + 1) * padded] = ref[:, HD : 2 * HD]
    if width > filled:
        k_all[filled:] = jnp.zeros((width - filled, HD), bf16)
        t_all[filled:] = jnp.zeros((width - filled, HD), bf16)
    hidden = deltas.shape[1]
    w1, w3, w2 = (weight_rows(w_ref, m, 0, hidden) for m in range(3))
    tall = 64
    for left in range(0, width, staged.shape[3]):
        right = min(left + staged.shape[3], width)
        cols, used = slice(left, right), slice(0, right - left)
        stage = staged.at[(left // staged.shape[3]) % staged.shape[0]]
        stage[0, :, used] = dot(w1, k_all[cols], (1, 1))
        stage[1, :, used] = dot(w3, k_all[cols], (1, 1))
        stage[2, :, used] = dot(w2, t_all[cols], (1, 1))
        for start in range(0, hidden, tall):
            rows = slice(start, start + tall)
            pre_one, pre_three, back = (stage[i, rows, used] for i in range(3))
            sig = sigmoid(pre_one)
            gate = pre_one * sig
            deltas[2, rows, cols] = (gate * pre_three).astype(bf16)
            deltas[1, rows, cols] = (back * gate).astype(bf16)
            deltas[0, rows, cols] = (
                (back * pre_three) * (sig * (1.0 + pre_one * (1.0 - sig)))
            ).astype(bf16)
    return (
        dot(deltas[0], k_all[...], (1, 0)),
        dot(deltas[1], k_all[...], (1, 0)),
        dot(deltas[2], t_all[...], (1, 0)),
    )


def gradient_scratch(slots, padded, hidden):
    width = -(-slots * padded // 128) * 128
    return [
        pltpu.VMEM((width, HD), bf16),
        pltpu.VMEM((width, HD), bf16),
        pltpu.VMEM((2, 3, hidden, 256), f32),
        pltpu.VMEM((3, hidden, width), bf16),
    ]


def apply_tokens(token_ref, w_ref, stage, act):
    hidden = act.shape[1]
    tall = 16
    w1, w3, w2 = (weight_rows(w_ref, m, 0, hidden) for m in range(3))
    query = token_ref[:, 2 * HD :]
    stage[0] = dot(query, w1, (1, 1))
    stage[1] = dot(query, w3, (1, 1))
    for start in range(0, query.shape[0], tall):
        rows = slice(start, start + tall)
        proj = stage[0, rows]
        act[rows] = (proj * sigmoid(proj) * stage[1, rows]).astype(bf16)
    return dot(act[...], w2, (1, 0)).astype(bf16)


def apply_scratch(padded, hidden):
    return [pltpu.VMEM((2, 2, padded, hidden), f32), pltpu.VMEM((2, padded, hidden), bf16)]


def early_body(count, *refs):
    token_refs, w_ref = refs[:count], refs[count]
    grads, fast = refs[count + 1 : count + 3]
    scratch, (staged, acts) = refs[count + 3 : -2], refs[-2:]
    for m, grad in enumerate(gradients(token_refs, w_ref, *scratch)):
        grads[m] = grad
    for i, ref in enumerate(token_refs):
        fast[i] = apply_tokens(ref, w_ref, staged.at[i % 2], acts.at[i % 2])


def late_body(group, slots, token_ref, w_ref, early, *refs):
    place = position()
    outs, sums, scratch = refs[:slots], refs[slots], refs[slots + 1 :]
    for m, grad in enumerate(gradients([token_ref], w_ref, *scratch)):
        sums[m] = (early[m] + grad).astype(bf16)
    for d in range(slots):
        matrix = lax.rem((place[0] ^ d) - place[1] + group * slots, slots)
        chosen = sums[jnp.minimum(matrix, 2)]
        outs[d][...] = jnp.where(matrix < 3, chosen, jnp.zeros_like(chosen))


def late_apply_body(early_slots, last, token_ref, w_ref, early, out, staged, acts):
    place = position()
    for i, d in enumerate(early_slots):
        out[place[1] ^ d] = early[i]
    out[place[1] ^ last] = apply_tokens(token_ref, w_ref, staged.at[0], acts.at[0])


def weight_rows(w_ref, m, start, block):
    if len(w_ref.shape) == 3:
        return w_ref[m, start : start + block]
    rows = w_ref.shape[2]
    return w_ref[start // rows : (start + block) // rows, m].reshape(block, HD)


def parts_of(x):
    high = x.astype(bf16)
    return high, (x - high.astype(f32)).astype(bf16)


def left_of(x):
    high, low = parts_of(x)
    return jnp.concatenate([high, high, low], axis=1)


def right_of(x):
    high, low = parts_of(x)
    return jnp.concatenate([high, low, high], axis=0)


def ortho_body(*refs):
    parts, out = refs[:-1], refs[-1]
    grads = parts[0][...].astype(f32)
    for part in parts[1:]:
        grads = grads + part[...].astype(f32)
    eye = (
        lax.broadcasted_iota(jnp.int32, (HD, HD), 0) == lax.broadcasted_iota(jnp.int32, (HD, HD), 1)
    ).astype(f32)
    raw = dot(grads, grads, (0, 0), highest)
    square = jnp.sum(jnp.sum(raw * eye, axis=0, keepdims=True), axis=1, keepdims=True)
    scale = lax.rsqrt(square + epsilon)
    gram = raw * scale * scale
    total = None
    for step in range(NS_STEPS):
        square_gram = dot(left_of(gram), right_of(gram), (1, 0))
        mix = quintic_a * eye + quintic_b * gram + quintic_c * square_gram
        right = right_of(mix)
        if step < NS_STEPS - 1:
            gram = dot(left_of(dot(left_of(gram), right, (1, 0))), right, (1, 0))
        total = mix if total is None else dot(left_of(total), right, (1, 0))
    out[...] = dot(left_of(grads * scale), right_of(total), (1, 0)).astype(out.dtype)


def finish_body(slots, group, w_ref, rows_ref, out):
    heads = w_ref.shape[1]
    for m in range(3):
        for h in range(heads):
            weights = w_ref[m, h]
            summed = weights + rows_ref[((m + h) % slots) * group + h].astype(f32)
            old = jnp.sqrt(jnp.sum(weights * weights, axis=1, keepdims=True))
            new = lax.rsqrt(jnp.sum(summed * summed, axis=1, keepdims=True) + epsilon)
            out[m, h] = summed * (old * new)


def attend_body(heads, tokens, q_ref, own_ref, back_ref, out):
    padded = own_ref.shape[0]
    span = heads * HD
    column = lax.broadcasted_iota(jnp.int32, (1, 2 * padded), 1)
    place = position()
    first = (place[0] == 0) & (place[1] == 0)
    stop = jnp.where(first, padded, padded + tokens)
    live = (column < tokens) | ((column >= padded) & (column < stop))
    for h in range(heads):
        cols = slice(h * HD, (h + 1) * HD)
        key = jnp.concatenate([own_ref[:, cols], back_ref[:, cols]], axis=0)
        vcols = slice(span + h * HD, span + (h + 1) * HD)
        value = jnp.concatenate([own_ref[:, vcols], back_ref[:, vcols]], axis=0)
        scores = dot(q_ref[:, cols], key, (1, 1)) * (HD ** (-0.5))
        scores = jnp.where(live, scores, -1e30)
        weights = jnp.exp(scores - jnp.max(scores, axis=1, keepdims=True))
        probs = (weights / jnp.sum(weights, axis=1, keepdims=True)).astype(bf16)
        out[:, cols] = dot(probs, value, (1, 0))


def assemble_body(heads, slots, out, squares):
    for h in range(heads):
        out[:, h * HD : (h + 1) * HD] = slots[h]
    fast = out[...].astype(f32)
    squares[...] = dot(jnp.ones((8, heads * HD), f32), fast * fast, (1, 1), highest)


def block_body(features, gain_ref, attended_ref, fast_ref, *refs):
    squares, out = refs[:-1], refs[-1]
    total = squares[0][...]
    for other in squares[1:]:
        total = total + other[...]
    pick = (lax.broadcasted_iota(jnp.int32, (8, HD), 0) == 0).astype(f32)
    spread = dot(total, pick, (0, 0), highest) * (1.0 / features)
    scale = lax.rsqrt(spread + epsilon)
    for h in range(fast_ref.shape[1] // HD):
        cols = slice(h * HD, (h + 1) * HD)
        out[:, cols] = (
            attended_ref[:, cols] + fast_ref[:, cols].astype(f32) * gain_ref[:, cols] * scale
        ).astype(bf16)


def on_device(queries, keys, values, rates, frame_update, fast_weights, gain):
    tokens = queries.shape[0]
    heads = queries.shape[1] // HD
    rows_local = fast_weights.shape[2]
    nz, group, nh = lax.axis_size("z"), lax.axis_size("grp"), lax.axis_size("head")
    count = nz * group
    hidden = count * rows_local
    padded = -(-tokens // 16) * 16
    span = heads * HD

    def whole(*shape):
        return pl.BlockSpec(shape, lambda i: (0,) * len(shape))

    low_shape = (count, 3, rows_local, HD)
    prepared = pl.pallas_call(
        functools.partial(prep_body, heads, group, tokens),
        grid=(1,),
        out_shape=[sds(low_shape, bf16), sds((padded, 2 * span), bf16)]
        + [sds((padded, 3 * HD), bf16)] * group,
        in_specs=[whole(1, 1), whole(*fast_weights.shape)]
        + [whole(padded, span)] * 3
        + [whole(heads, -(-padded // 128) * 128)],
        out_specs=[whole(*low_shape), whole(padded, 2 * span)]
        + [whole(padded, 3 * HD)] * group,
        compiler_params=pltpu.CompilerParams(vmem_limit_bytes=VMEM_MOST),
    )(frame_update.reshape(1, 1), fast_weights, keys, values, queries, rates.T)
    low, kv_own, token_slots = prepared[0], prepared[1], list(prepared[2:])

    weights = lax.all_to_all(low, ("z", "grp"), 0, 0, tiled=True)
    if rows_local % 16:
        weights = weights.transpose(1, 0, 2, 3).reshape(3, hidden, HD)
    for d in served(group)[1:]:
        pairs = [(s, s ^ d) for s in range(group) if s ^ d < heads]
        token_slots[d] = lax.ppermute(token_slots[d], "grp", pairs)

    last = group // 2
    early_slots = [d for d in served(group) if d != last]
    early_grads, early_fast = call(
        functools.partial(early_body, len(early_slots)),
        [sds((3, hidden, HD), f32), sds((len(early_slots), padded, HD), bf16)],
        scratch=gradient_scratch(len(early_slots), padded, hidden) + apply_scratch(padded, hidden),
        flops=1e9,
    )(*(token_slots[d] for d in early_slots), weights)
    partials = list(
        call(
            functools.partial(late_body, group, nz),
            [sds((hidden, HD), bf16)] * nz,
            scratch=[pltpu.VMEM((3, hidden, HD), bf16)] + gradient_scratch(1, padded, hidden),
            flops=5e8,
        )(token_slots[last], weights, early_grads)
    )
    weights, partials[0] = lax.optimization_barrier((weights, partials[0]))
    for d in served(nz)[1:]:
        pairs = []
        for z in range(nz):
            pairs += [
                (z * group + j, (z ^ d) * group + j)
                for j in range(heads)
                if ((z ^ d) - j) % nz < 3
            ]
        partials[d] = lax.ppermute(partials[d], ("z", "grp"), pairs)

    fast_slots = call(
        functools.partial(late_apply_body, early_slots, last),
        sds((group, padded, HD), bf16),
        scratch=apply_scratch(padded, hidden),
        flops=1e3,
        moved=1024,
    )(token_slots[last], weights, early_fast)
    kv_own, partials[0], fast_slots = lax.optimization_barrier((kv_own, partials[0], fast_slots))
    fast_slots = lax.all_to_all(fast_slots, "grp", 0, 0, tiled=True)

    ring = [(i, i + 1) for i in range(count - 1)]
    kv_back = lax.ppermute(kv_own, ("z", "grp"), ring)

    ortho = call(ortho_body, sds((hidden, HD), bf16), flops=1e9)(
        *(partials[d] for d in served(nz))
    )
    queries, ortho = lax.optimization_barrier((queries, ortho))
    rows = lax.all_to_all(
        ortho.reshape(count, rows_local, HD), ("z", "grp"), 0, 0, tiled=True
    )
    new_weights = call(
        functools.partial(finish_body, nz, group), sds(fast_weights.shape, f32), flops=1e6
    )(fast_weights, rows)

    attended = pl.pallas_call(
        functools.partial(attend_body, heads, tokens),
        grid=(1,),
        out_shape=sds((padded, span), f32),
        in_specs=[whole(padded, span)] + [whole(padded, 2 * span)] * 2,
        out_specs=whole(padded, span),
        compiler_params=pltpu.CompilerParams(vmem_limit_bytes=VMEM_LIMIT),
    )(queries, kv_own, kv_back)
    fast, squares = call(
        functools.partial(assemble_body, heads),
        [sds((padded, span), bf16), sds((8, padded), f32)],
        flops=1e7,
    )(fast_slots)
    all_squares = [squares] + [
        lax.ppermute(squares, "head", [(s, (s + d) % nh) for s in range(nh)]) for d in range(1, nh)
    ]
    block_out = pl.pallas_call(
        functools.partial(block_body, span * nh),
        grid=(1,),
        out_shape=sds((tokens, span), bf16),
        in_specs=[whole(1, span), whole(padded, span), whole(padded, span)]
        + [whole(8, padded)] * nh,
        out_specs=whole(padded, span),
        compiler_params=pltpu.CompilerParams(vmem_limit_bytes=VMEM_LIMIT),
    )(gain.reshape(1, span), attended, fast, *all_squares)
    return (block_out, new_weights)


def solution(mesh):
    group = 4
    nh = mesh.shape["head"]
    inner = Mesh(
        np.asarray(mesh.devices).reshape(mesh.shape["ctx"] // group, group, nh),
        ("z", "grp", "head"),
    )
    ctx = ("z", "grp")
    placed = (
        P(ctx, "head"),
        P(ctx, "head"),
        P(ctx, "head"),
        P(ctx, "head"),
        P(ctx),
        P(None, "head", ctx, None),
        P("head"),
    )
    return jax.shard_map(
        on_device,
        mesh=inner,
        in_specs=placed,
        out_specs=(P(ctx, "head"), P(None, "head", ctx, None)),
        check_vma=False,
    )
```

```python
import functools

import jax
import jax.numpy as jnp
import numpy as np
from jax import lax
from jax.experimental import pallas as pl
from jax.experimental.pallas import tpu as pltpu
from jax.sharding import Mesh, PartitionSpec as P

HD = 128
NS_STEPS = 5

epsilon = 1e-06
quintic_a = 3.4445
quintic_b = -4.775
quintic_c = 2.0315
highest = lax.Precision.HIGHEST
f32 = jnp.float32
bf16 = jnp.bfloat16
VMEM_LIMIT = 24 * 1024 * 1024


def dot(a, b, contract, precision=None):
    return lax.dot_general(
        a, b, ((contract[:1], contract[1:]), ((), ())),
        precision=precision, preferred_element_type=f32,
    )


def call(body, outs, scratch=(), in_specs=None, flops=1e8, moved=1 << 20, **kw):
    given = {} if in_specs is None else {"in_specs": in_specs}
    return pl.pallas_call(
        body,
        out_shape=outs,
        **given,
        scratch_shapes=list(scratch),
        compiler_params=pltpu.CompilerParams(vmem_limit_bytes=VMEM_LIMIT),
        cost_estimate=pl.CostEstimate(flops=int(flops), bytes_accessed=moved, transcendentals=0),
        **kw,
    )


def sds(shape, dtype):
    return jax.ShapeDtypeStruct(shape, dtype)


def served(n):
    return [0] + list(range(n - 1, 0, -1))


def flip(z, group):
    return (z & 1) * (group // 2)


def position():
    return lax.axis_index("z"), lax.axis_index("grp")


def sigmoid(x):
    return 0.5 * jnp.tanh(0.5 * x) + 0.5


def cast_body(heads, group, w_ref, w_out):
    slots = w_out.shape[0] // group
    for head in range(heads):
        for m in range(3):
            low = w_ref[m, head].astype(bf16)
            for z in range(slots):
                for j in range(group):
                    if min(j ^ flip(z, group), heads - 1) == head:
                        w_out[z * group + j, m] = low


def prep_body(
    heads, group, tokens, last, after, update, k_ref, v_ref, q_ref, rate_ref, kv_out, *outs
):
    token_outs, (late_out, targets) = outs[:-2], outs[-2:]
    padded = kv_out.shape[0]
    place = position()
    valid = lax.broadcasted_iota(jnp.int32, (padded, 1), 0) < tokens
    none = jnp.zeros((), bf16)
    keep = update[...].astype(f32)
    lane_head = lax.broadcasted_iota(jnp.int32, (heads, heads * HD), 1) // HD
    row = lax.broadcasted_iota(jnp.int32, (heads, heads * HD), 0)
    rate = dot(rate_ref[...], (row == lane_head).astype(f32), (0, 0), highest)[:padded]
    targets[...] = jnp.where(valid, ((rate * keep) * v_ref[...].astype(f32)).astype(bf16), none)
    for d in range(group):
        head = jnp.minimum(place[1] ^ d ^ flip(place[0], group), heads - 1)
        cols = pl.ds(pl.multiple_of(head * HD, HD), HD)
        token_outs[d][:, :HD] = jnp.where(valid, k_ref[:, cols], none)
        token_outs[d][:, HD : 2 * HD] = targets[:, cols]
        query = jnp.where(valid, q_ref[:, cols], none)
        if d == last:
            late_out[...] = query
        else:
            token_outs[d][:, 2 * HD :] = query
    kv_out[:, : heads * HD] = jnp.where(valid, k_ref[...], none)
    kv_out[:, heads * HD :] = jnp.where(valid, v_ref[...], none)


def gradients(token_refs, w_ref, k_all, t_all, staged, deltas):
    padded = token_refs[0].shape[0]
    width = k_all.shape[0]
    filled = len(token_refs) * padded
    for i, ref in enumerate(token_refs):
        k_all[i * padded : (i + 1) * padded] = ref[:, :HD]
        t_all[i * padded : (i + 1) * padded] = ref[:, HD : 2 * HD]
    if width > filled:
        k_all[filled:] = jnp.zeros((width - filled, HD), bf16)
        t_all[filled:] = jnp.zeros((width - filled, HD), bf16)
    hidden = deltas.shape[1]
    w1, w3, w2 = (weight_rows(w_ref, m, 0, hidden) for m in range(3))
    tall = 64
    for left in range(0, width, staged.shape[3]):
        right = min(left + staged.shape[3], width)
        cols, used = slice(left, right), slice(0, right - left)
        stage = staged.at[(left // staged.shape[3]) % staged.shape[0]]
        stage[0, :, used] = dot(w1, k_all[cols], (1, 1))
        stage[1, :, used] = dot(w3, k_all[cols], (1, 1))
        stage[2, :, used] = dot(w2, t_all[cols], (1, 1))
        for start in range(0, hidden, tall):
            rows = slice(start, start + tall)
            pre_one, pre_three, back = (stage[i, rows, used] for i in range(3))
            sig = sigmoid(pre_one)
            gate = pre_one * sig
            deltas[2, rows, cols] = (gate * pre_three).astype(bf16)
            deltas[1, rows, cols] = (back * gate).astype(bf16)
            deltas[0, rows, cols] = (
                (back * pre_three) * (sig * (1.0 + pre_one * (1.0 - sig)))
            ).astype(bf16)
    return (
        dot(deltas[0], k_all[...], (1, 0)),
        dot(deltas[1], k_all[...], (1, 0)),
        dot(deltas[2], t_all[...], (1, 0)),
    )


def gradient_scratch(slots, padded, hidden):
    width = -(-slots * padded // 128) * 128
    return [
        pltpu.VMEM((width, HD), bf16),
        pltpu.VMEM((width, HD), bf16),
        pltpu.VMEM((2, 3, hidden, 256), f32),
        pltpu.VMEM((3, hidden, width), bf16),
    ]


def apply_tokens(query, w_ref, stage, act):
    hidden = act.shape[1]
    tall = 16
    w1, w3, w2 = (weight_rows(w_ref, m, 0, hidden) for m in range(3))
    stage[0] = dot(query, w1, (1, 1))
    stage[1] = dot(query, w3, (1, 1))
    for start in range(0, query.shape[0], tall):
        rows = slice(start, start + tall)
        proj = stage[0, rows]
        act[rows] = (proj * sigmoid(proj) * stage[1, rows]).astype(bf16)
    return dot(act[...], w2, (1, 0)).astype(bf16)


def apply_scratch(padded, hidden):
    return [pltpu.VMEM((2, 2, padded, hidden), f32), pltpu.VMEM((2, padded, hidden), bf16)]


def early_body(count, *refs):
    token_refs, w_ref = refs[:count], refs[count]
    grads, fast = refs[count + 1 : count + 3]
    scratch, (staged, acts) = refs[count + 3 : -2], refs[-2:]
    for m, grad in enumerate(gradients(token_refs, w_ref, *scratch)):
        grads[m] = grad
    for i, ref in enumerate(token_refs):
        fast[i] = apply_tokens(ref[:, 2 * HD :], w_ref, staged.at[i % 2], acts.at[i % 2])


def late_body(group, slots, token_ref, w_ref, early, *refs):
    place = position()
    outs, sums, scratch = refs[:slots], refs[slots], refs[slots + 1 :]
    for m, grad in enumerate(gradients([token_ref], w_ref, *scratch)):
        sums[m] = (early[m] + grad).astype(bf16)
    head = place[1] ^ flip(place[0], group)
    for d in range(slots):
        matrix = lax.rem((place[0] ^ d) - head + group * slots, slots)
        chosen = sums[jnp.minimum(matrix, 2)]
        outs[d][...] = jnp.where(matrix < 3, chosen, jnp.zeros_like(chosen))


def late_apply_body(early_slots, last, query_ref, w_ref, early, out, staged, acts):
    place = position()
    for i, d in enumerate(early_slots):
        out[place[1] ^ d] = early[i]
    out[place[1] ^ last] = apply_tokens(query_ref[...], w_ref, staged.at[0], acts.at[0])


def weight_rows(w_ref, m, start, block):
    if len(w_ref.shape) == 3:
        return w_ref[m, start : start + block]
    rows = w_ref.shape[2]
    return w_ref[start // rows : (start + block) // rows, m].reshape(block, HD)


def parts_of(x):
    high = x.astype(bf16)
    return high, (x - high.astype(f32)).astype(bf16)


def left_of(x):
    high, low = parts_of(x)
    return jnp.concatenate([high, high, low], axis=1)


def right_of(x):
    high, low = parts_of(x)
    return jnp.concatenate([high, low, high], axis=0)


def ortho_body(*refs):
    parts, out = refs[:-1], refs[-1]
    grads = parts[0][...].astype(f32)
    for part in parts[1:]:
        grads = grads + part[...].astype(f32)
    eye = (
        lax.broadcasted_iota(jnp.int32, (HD, HD), 0) == lax.broadcasted_iota(jnp.int32, (HD, HD), 1)
    ).astype(f32)
    both = jnp.concatenate(parts_of(grads), axis=1)
    blocks = dot(both, both, (0, 0))
    raw = (blocks[:HD, HD:] + blocks[HD:, :HD]) + blocks[:HD, :HD]
    square = jnp.sum(jnp.sum(raw * eye, axis=0, keepdims=True), axis=1, keepdims=True)
    scale = lax.rsqrt(square + epsilon)
    gram = raw * scale * scale
    total = None
    for step in range(NS_STEPS):
        square_gram = dot(left_of(gram), right_of(gram), (1, 0))
        mix = quintic_a * eye + quintic_b * gram + quintic_c * square_gram
        right = right_of(mix)
        if step < NS_STEPS - 1:
            gram = dot(left_of(dot(left_of(gram), right, (1, 0))), right, (1, 0))
            total = mix if total is None else dot(left_of(total), right, (1, 0))
    ortho = dot(left_of(grads * scale), right_of(total), (1, 0))
    out[...] = dot(left_of(ortho), right, (1, 0)).astype(out.dtype)


def finish_body(slots, group, w_ref, rows_ref, out):
    heads = w_ref.shape[1]

    def at(m, h):
        z = (m + h) % slots
        return z * group + (h ^ flip(z, group))

    for m in range(3):
        for h in range(heads):
            weights = w_ref[m, h]
            summed = weights + rows_ref[at(m, h)].astype(f32)
            old = jnp.sqrt(jnp.sum(weights * weights, axis=1, keepdims=True))
            new = lax.rsqrt(jnp.sum(summed * summed, axis=1, keepdims=True) + epsilon)
            out[m, h] = summed * (old * new)


def attend_body(heads, tokens, q_ref, own_ref, back_ref, out):
    padded = own_ref.shape[0]
    span = heads * HD
    column = lax.broadcasted_iota(jnp.int32, (1, 2 * padded), 1)
    place = position()
    first = (place[0] == 0) & (place[1] == 0)
    stop = jnp.where(first, padded, padded + tokens)
    live = (column < tokens) | ((column >= padded) & (column < stop))
    for h in range(heads):
        cols = slice(h * HD, (h + 1) * HD)
        key = jnp.concatenate([own_ref[:, cols], back_ref[:, cols]], axis=0)
        vcols = slice(span + h * HD, span + (h + 1) * HD)
        value = jnp.concatenate([own_ref[:, vcols], back_ref[:, vcols]], axis=0)
        scores = dot(q_ref[:, cols], key, (1, 1)) * (HD ** (-0.5))
        scores = jnp.where(live, scores, -1e30)
        weights = jnp.exp(scores - jnp.max(scores, axis=1, keepdims=True))
        probs = (weights / jnp.sum(weights, axis=1, keepdims=True)).astype(bf16)
        out[:, cols] = dot(probs, value, (1, 0))


def assemble_body(heads, slots, out, squares):
    side = flip(position()[0], slots.shape[0])
    for h in range(heads):
        out[:, h * HD : (h + 1) * HD] = slots[h ^ side]
    fast = out[...].astype(f32)
    squares[...] = dot(jnp.ones((8, heads * HD), f32), fast * fast, (1, 1), highest)


def block_body(features, gain_ref, attended_ref, fast_ref, *refs):
    squares, out = refs[:-1], refs[-1]
    total = squares[0][...]
    for other in squares[1:]:
        total = total + other[...]
    pick = (lax.broadcasted_iota(jnp.int32, (8, HD), 0) == 0).astype(f32)
    spread = dot(total, pick, (0, 0), highest) * (1.0 / features)
    scale = lax.rsqrt(spread + epsilon)
    for h in range(fast_ref.shape[1] // HD):
        cols = slice(h * HD, (h + 1) * HD)
        out[:, cols] = (
            attended_ref[:, cols] + fast_ref[:, cols].astype(f32) * gain_ref[:, cols] * scale
        ).astype(bf16)


def on_device(queries, keys, values, rates, frame_update, fast_weights, gain):
    tokens = queries.shape[0]
    heads = queries.shape[1] // HD
    rows_local = fast_weights.shape[2]
    nz, group, nh = lax.axis_size("z"), lax.axis_size("grp"), lax.axis_size("head")
    count = nz * group
    hidden = count * rows_local
    padded = -(-tokens // 16) * 16
    span = heads * HD

    def whole(*shape):
        return pl.BlockSpec(shape, lambda i: (0,) * len(shape))

    low_shape = (count, 3, rows_local, HD)
    last = group // 2
    widths = [2 * HD if d == last else 3 * HD for d in range(group)] + [HD]
    low = call(
        functools.partial(cast_body, heads, group), sds(low_shape, bf16), flops=1e6
    )(fast_weights)
    prepared = pl.pallas_call(
        functools.partial(prep_body, heads, group, tokens, last),
        grid=(1,),
        out_shape=[sds((padded, 2 * span), bf16)]
        + [sds((padded, width), bf16) for width in widths],
        in_specs=[pl.BlockSpec(memory_space=pl.ANY), whole(1, 1)]
        + [whole(padded, span)] * 3
        + [whole(heads, -(-padded // 128) * 128)],
        out_specs=[whole(padded, 2 * span)] + [whole(padded, width) for width in widths],
        scratch_shapes=[pltpu.VMEM((padded, span), bf16)],
        compiler_params=pltpu.CompilerParams(vmem_limit_bytes=VMEM_LIMIT),
    )(low, frame_update.reshape(1, 1), keys, values, queries, rates.T)
    kv_own, *token_slots, late_queries = prepared

    weights = lax.all_to_all(low, ("z", "grp"), 0, 0, tiled=True)
    if rows_local % 16:
        weights = weights.transpose(1, 0, 2, 3).reshape(3, hidden, HD)
    for d in served(group)[1:]:
        pairs = [
            (z * group + s, z * group + (s ^ d))
            for z in range(nz)
            for s in range(group)
            if s ^ d ^ flip(z, group) < heads
        ]
        token_slots[d] = lax.ppermute(token_slots[d], ("z", "grp"), pairs)
        if d == last:
            late_queries = lax.ppermute(late_queries, ("z", "grp"), pairs)

    early_slots = [d for d in served(group) if d != last]
    early_grads, early_fast = call(
        functools.partial(early_body, len(early_slots)),
        [sds((3, hidden, HD), f32), sds((len(early_slots), padded, HD), bf16)],
        scratch=gradient_scratch(len(early_slots), padded, hidden) + apply_scratch(padded, hidden),
        flops=1e9,
    )(*(token_slots[d] for d in early_slots), weights)
    partials = list(
        call(
            functools.partial(late_body, group, nz),
            [sds((hidden, HD), bf16)] * nz,
            scratch=[pltpu.VMEM((3, hidden, HD), bf16)] + gradient_scratch(1, padded, hidden),
            flops=5e8,
        )(token_slots[last], weights, early_grads)
    )
    weights, partials[0] = lax.optimization_barrier((weights, partials[0]))
    late_queries, partials[1] = lax.optimization_barrier((late_queries, partials[1]))
    for d in served(nz)[1:]:
        pairs = [
            (z * group + (h ^ flip(z, group)), (z ^ d) * group + (h ^ flip(z ^ d, group)))
            for z in range(nz)
            for h in range(heads)
            if ((z ^ d) - h) % nz < 3
        ]
        partials[d] = lax.ppermute(partials[d], ("z", "grp"), pairs)

    fast_slots = call(
        functools.partial(late_apply_body, early_slots, last),
        sds((group, padded, HD), bf16),
        scratch=apply_scratch(padded, hidden),
        flops=1e3,
        moved=1024,
    )(late_queries, weights, early_fast)
    kv_own, partials[0], fast_slots = lax.optimization_barrier((kv_own, partials[0], fast_slots))
    fast_slots = lax.all_to_all(fast_slots, "grp", 0, 0, tiled=True)

    ring = [(i, i + 1) for i in range(count - 1)]
    kv_back = lax.ppermute(kv_own, ("z", "grp"), ring)

    ortho = call(ortho_body, sds((hidden, HD), bf16), flops=1e9)(
        *(partials[d] for d in served(nz))
    )
    queries, ortho = lax.optimization_barrier((queries, ortho))
    rows = lax.all_to_all(
        ortho.reshape(count, rows_local, HD), ("z", "grp"), 0, 0, tiled=True
    )
    new_weights = call(
        functools.partial(finish_body, nz, group), sds(fast_weights.shape, f32), flops=1e6
    )(fast_weights, rows)

    attended = pl.pallas_call(
        functools.partial(attend_body, heads, tokens),
        grid=(1,),
        out_shape=sds((padded, span), f32),
        in_specs=[whole(padded, span)] + [whole(padded, 2 * span)] * 2,
        out_specs=whole(padded, span),
        compiler_params=pltpu.CompilerParams(vmem_limit_bytes=VMEM_LIMIT),
    )(queries, kv_own, kv_back)
    fast, squares = call(
        functools.partial(assemble_body, heads),
        [sds((padded, span), bf16), sds((8, padded), f32)],
        flops=1e7,
    )(fast_slots)
    all_squares = [squares] + [
        lax.ppermute(squares, "head", [(s, (s + d) % nh) for s in range(nh)]) for d in range(1, nh)
    ]
    block_out = pl.pallas_call(
        functools.partial(block_body, span * nh),
        grid=(1,),
        out_shape=sds((tokens, span), bf16),
        in_specs=[whole(1, span), whole(padded, span), whole(padded, span)]
        + [whole(8, padded)] * nh,
        out_specs=whole(padded, span),
        compiler_params=pltpu.CompilerParams(vmem_limit_bytes=VMEM_LIMIT),
    )(gain.reshape(1, span), attended, fast, *all_squares)
    return (block_out, new_weights)


def solution(mesh):
    group = 4
    nh = mesh.shape["head"]
    inner = Mesh(
        np.asarray(mesh.devices).reshape(mesh.shape["ctx"] // group, group, nh),
        ("z", "grp", "head"),
    )
    ctx = ("z", "grp")
    placed = (
        P(ctx, "head"),
        P(ctx, "head"),
        P(ctx, "head"),
        P(ctx, "head"),
        P(ctx),
        P(None, "head", ctx, None),
        P("head"),
    )
    return jax.shard_map(
        on_device,
        mesh=inner,
        in_specs=placed,
        out_specs=(P(ctx, "head"), P(None, "head", ctx, None)),
        check_vma=False,
    )
```

```python
import functools

import jax
import jax.numpy as jnp
import numpy as np
from jax import lax
from jax.experimental import pallas as pl
from jax.experimental.pallas import tpu as pltpu
from jax.sharding import Mesh, PartitionSpec as P

HD = 128
NS_STEPS = 5

epsilon = 1e-06
quintic_a = 3.4445
quintic_b = -4.775
quintic_c = 2.0315
highest = lax.Precision.HIGHEST
f32 = jnp.float32
bf16 = jnp.bfloat16
VMEM_LIMIT = 24 * 1024 * 1024


def dot(a, b, contract, precision=None):
    return lax.dot_general(
        a, b, ((contract[:1], contract[1:]), ((), ())),
        precision=precision, preferred_element_type=f32,
    )


def call(body, outs, scratch=(), in_specs=None, flops=1e8, moved=1 << 20, **kw):
    given = {} if in_specs is None else {"in_specs": in_specs}
    return pl.pallas_call(
        body,
        out_shape=outs,
        **given,
        scratch_shapes=list(scratch),
        compiler_params=pltpu.CompilerParams(vmem_limit_bytes=VMEM_LIMIT),
        cost_estimate=pl.CostEstimate(flops=int(flops), bytes_accessed=moved, transcendentals=0),
        **kw,
    )


def sds(shape, dtype):
    return jax.ShapeDtypeStruct(shape, dtype)


def served(n):
    return [0] + list(range(n - 1, 0, -1))


def position():
    return lax.axis_index("z"), lax.axis_index("grp")


def sigmoid(x):
    return 0.5 * jnp.tanh(0.5 * x) + 0.5


def cast_body(heads, group, w_ref, w_out):
    slots = w_out.shape[0] // group
    for j in range(group):
        for m in range(3):
            low = w_ref[m, min(j, heads - 1)].astype(bf16)
            for z in range(slots):
                w_out[z * group + j, m] = low


def prep_body(
    heads, group, tokens, after, update, rate_ref, k_ref, v_ref, q_ref, kv_out, *outs
):
    token_outs, targets = outs[:-1], outs[-1]
    padded = kv_out.shape[0]
    place = position()
    valid = lax.broadcasted_iota(jnp.int32, (padded, 1), 0) < tokens
    none = jnp.zeros((), bf16)
    keep = update[...].astype(f32)
    lane_head = lax.broadcasted_iota(jnp.int32, (heads, heads * HD), 1) // HD
    row = lax.broadcasted_iota(jnp.int32, (heads, heads * HD), 0)
    rate = dot(rate_ref[...], (row == lane_head).astype(f32), (0, 0), highest)[:padded]
    targets[...] = jnp.where(valid, ((rate * keep) * v_ref[...].astype(f32)).astype(bf16), none)
    for d in range(group):
        head = jnp.minimum(place[1] ^ d, heads - 1)
        cols = pl.ds(pl.multiple_of(head * HD, HD), HD)
        token_outs[d][:, :HD] = jnp.where(valid, k_ref[:, cols], none)
        token_outs[d][:, HD : 2 * HD] = targets[:, cols]
        token_outs[d][:, 2 * HD :] = jnp.where(valid, q_ref[:, cols], none)
    kv_out[:, : heads * HD] = jnp.where(valid, k_ref[...], none)
    kv_out[:, heads * HD :] = jnp.where(valid, v_ref[...], none)


def gradients(token_refs, w_ref, k_all, t_all, staged, deltas):
    padded = token_refs[0].shape[0]
    width = k_all.shape[0]
    filled = len(token_refs) * padded
    for i, ref in enumerate(token_refs):
        k_all[i * padded : (i + 1) * padded] = ref[:, :HD]
        t_all[i * padded : (i + 1) * padded] = ref[:, HD : 2 * HD]
    if width > filled:
        k_all[filled:] = jnp.zeros((width - filled, HD), bf16)
        t_all[filled:] = jnp.zeros((width - filled, HD), bf16)
    hidden = deltas.shape[1]
    w1, w3, w2 = (weight_rows(w_ref, m, 0, hidden) for m in range(3))
    tall = 64
    for left in range(0, width, staged.shape[3]):
        right = min(left + staged.shape[3], width)
        cols, used = slice(left, right), slice(0, right - left)
        stage = staged.at[(left // staged.shape[3]) % staged.shape[0]]
        stage[0, :, used] = dot(w1, k_all[cols], (1, 1))
        stage[1, :, used] = dot(w3, k_all[cols], (1, 1))
        stage[2, :, used] = dot(w2, t_all[cols], (1, 1))
        for start in range(0, hidden, tall):
            rows = slice(start, start + tall)
            pre_one, pre_three, back = (stage[i, rows, used] for i in range(3))
            sig = sigmoid(pre_one)
            gate = pre_one * sig
            deltas[2, rows, cols] = (gate * pre_three).astype(bf16)
            deltas[1, rows, cols] = (back * gate).astype(bf16)
            deltas[0, rows, cols] = (
                (back * pre_three) * (sig * (1.0 + pre_one * (1.0 - sig)))
            ).astype(bf16)
    return (
        dot(deltas[0], k_all[...], (1, 0)),
        dot(deltas[1], k_all[...], (1, 0)),
        dot(deltas[2], t_all[...], (1, 0)),
    )


def gradient_scratch(slots, padded, hidden):
    width = -(-slots * padded // 128) * 128
    return [
        pltpu.VMEM((width, HD), bf16),
        pltpu.VMEM((width, HD), bf16),
        pltpu.VMEM((2, 3, hidden, 256), f32),
        pltpu.VMEM((3, hidden, width), bf16),
    ]


def apply_tokens(query, w_ref, stage, act):
    hidden = act.shape[1]
    tall = 16
    w1, w3, w2 = (weight_rows(w_ref, m, 0, hidden) for m in range(3))
    stage[0] = dot(query, w1, (1, 1))
    stage[1] = dot(query, w3, (1, 1))
    for start in range(0, query.shape[0], tall):
        rows = slice(start, start + tall)
        proj = stage[0, rows]
        act[rows] = (proj * sigmoid(proj) * stage[1, rows]).astype(bf16)
    return dot(act[...], w2, (1, 0)).astype(bf16)


def apply_scratch(padded, hidden):
    return [pltpu.VMEM((2, 2, padded, hidden), f32), pltpu.VMEM((2, padded, hidden), bf16)]


def early_body(count, *refs):
    token_refs, w_ref = refs[:count], refs[count]
    grads, fast = refs[count + 1 : count + 3]
    scratch, (staged, acts) = refs[count + 3 : -2], refs[-2:]
    for m, grad in enumerate(gradients(token_refs, w_ref, *scratch)):
        grads[m] = grad
    for i, ref in enumerate(token_refs):
        fast[i] = apply_tokens(ref[:, 2 * HD :], w_ref, staged.at[i % 2], acts.at[i % 2])


def late_body(group, slots, token_ref, w_ref, early, *refs):
    place = position()
    outs, sums, scratch = refs[:slots], refs[slots], refs[slots + 1 :]
    for m, grad in enumerate(gradients([token_ref], w_ref, *scratch)):
        sums[m] = (early[m] + grad).astype(bf16)
    for d in range(slots):
        matrix = lax.rem((place[0] ^ d) - place[1] + group * slots, slots)
        chosen = sums[jnp.minimum(matrix, 2)]
        outs[d][...] = jnp.where(matrix < 3, chosen, jnp.zeros_like(chosen))


def late_apply_body(early_slots, last, token_ref, w_ref, early, out, staged, acts):
    place = position()
    for i, d in enumerate(early_slots):
        out[place[1] ^ d] = early[i]
    out[place[1] ^ last] = apply_tokens(
        token_ref[:, 2 * HD :], w_ref, staged.at[0], acts.at[0]
    )


def weight_rows(w_ref, m, start, block):
    if len(w_ref.shape) == 3:
        return w_ref[m, start : start + block]
    rows = w_ref.shape[2]
    return w_ref[start // rows : (start + block) // rows, m].reshape(block, HD)


def parts_of(x):
    high = x.astype(bf16)
    return high, (x - high.astype(f32)).astype(bf16)


def left_of(x):
    high, low = parts_of(x)
    return jnp.concatenate([high, high, low], axis=1)


def right_of(x):
    high, low = parts_of(x)
    return jnp.concatenate([high, low, high], axis=0)


def ortho_body(heads, slots, *refs):
    place = position()
    matrix = lax.rem(place[0] - place[1] + heads * slots, slots)
    owner = (place[1] < heads) & (matrix < 3)

    @pl.when(owner)
    def _():
        orthogonalize(refs[:-1], refs[-1])

    @pl.when(jnp.logical_not(owner))
    def _():
        refs[-1][...] = jnp.zeros(refs[-1].shape, refs[-1].dtype)


def orthogonalize(parts, out):
    grads = parts[0][...].astype(f32)
    for part in parts[1:]:
        grads = grads + part[...].astype(f32)
    eye = (
        lax.broadcasted_iota(jnp.int32, (HD, HD), 0) == lax.broadcasted_iota(jnp.int32, (HD, HD), 1)
    ).astype(f32)
    both = jnp.concatenate(parts_of(grads), axis=1)
    blocks = dot(both, both, (0, 0))
    raw = (blocks[:HD, HD:] + blocks[HD:, :HD]) + blocks[:HD, :HD]
    square = jnp.sum(jnp.sum(raw * eye, axis=0, keepdims=True), axis=1, keepdims=True)
    scale = lax.rsqrt(square + epsilon)
    gram = raw * scale * scale
    total = None
    for step in range(NS_STEPS):
        square_gram = dot(left_of(gram), right_of(gram), (1, 0))
        mix = quintic_a * eye + quintic_b * gram + quintic_c * square_gram
        right = right_of(mix)
        if step < NS_STEPS - 1:
            gram = dot(left_of(dot(left_of(gram), right, (1, 0))), right, (1, 0))
            total = mix if total is None else dot(left_of(total), right, (1, 0))
    ortho = dot(left_of(grads * scale), right_of(total), (1, 0))
    out[...] = dot(left_of(ortho), right, (1, 0)).astype(out.dtype)


def finish_body(slots, group, w_ref, rows_ref, out):
    heads = w_ref.shape[1]
    for m in range(3):
        for h in range(heads):
            weights = w_ref[m, h]
            summed = weights + rows_ref[((m + h) % slots) * group + h].astype(f32)
            old = jnp.sqrt(jnp.sum(weights * weights, axis=1, keepdims=True))
            new = lax.rsqrt(jnp.sum(summed * summed, axis=1, keepdims=True) + epsilon)
            out[m, h] = summed * (old * new)


def attend_body(heads, tokens, q_ref, own_ref, back_ref, out):
    padded = own_ref.shape[0]
    span = heads * HD
    column = lax.broadcasted_iota(jnp.int32, (1, 2 * padded), 1)
    place = position()
    first = (place[0] == 0) & (place[1] == 0)
    stop = jnp.where(first, padded, padded + tokens)
    live = (column < tokens) | ((column >= padded) & (column < stop))
    for h in range(heads):
        cols = slice(h * HD, (h + 1) * HD)
        key = jnp.concatenate([own_ref[:, cols], back_ref[:, cols]], axis=0)
        vcols = slice(span + h * HD, span + (h + 1) * HD)
        value = jnp.concatenate([own_ref[:, vcols], back_ref[:, vcols]], axis=0)
        scores = dot(q_ref[:, cols], key, (1, 1)) * (HD ** (-0.5))
        scores = jnp.where(live, scores, -1e30)
        weights = jnp.exp(scores - jnp.max(scores, axis=1, keepdims=True))
        probs = (weights / jnp.sum(weights, axis=1, keepdims=True)).astype(bf16)
        out[:, cols] = dot(probs, value, (1, 0))


def assemble_body(heads, slots, out, squares):
    for h in range(heads):
        out[:, h * HD : (h + 1) * HD] = slots[h]
    fast = out[...].astype(f32)
    squares[...] = dot(jnp.ones((8, heads * HD), f32), fast * fast, (1, 1), highest)


def block_body(features, gain_ref, attended_ref, fast_ref, *refs):
    squares, out = refs[:-1], refs[-1]
    total = squares[0][...]
    for other in squares[1:]:
        total = total + other[...]
    pick = (lax.broadcasted_iota(jnp.int32, (8, HD), 0) == 0).astype(f32)
    spread = dot(total, pick, (0, 0), highest) * (1.0 / features)
    scale = lax.rsqrt(spread + epsilon)
    for h in range(fast_ref.shape[1] // HD):
        cols = slice(h * HD, (h + 1) * HD)
        out[:, cols] = (
            attended_ref[:, cols] + fast_ref[:, cols].astype(f32) * gain_ref[:, cols] * scale
        ).astype(bf16)


def on_device(queries, keys, values, rates, frame_update, fast_weights, gain):
    tokens = queries.shape[0]
    heads = queries.shape[1] // HD
    rows_local = fast_weights.shape[2]
    nz, group, nh = lax.axis_size("z"), lax.axis_size("grp"), lax.axis_size("head")
    count = nz * group
    hidden = count * rows_local
    padded = -(-tokens // 16) * 16
    span = heads * HD

    def whole(*shape):
        return pl.BlockSpec(shape, lambda i: (0,) * len(shape))

    low_shape = (count, 3, rows_local, HD)
    low = call(
        functools.partial(cast_body, heads, group), sds(low_shape, bf16), flops=1e6
    )(fast_weights)
    prepared = pl.pallas_call(
        functools.partial(prep_body, heads, group, tokens),
        grid=(1,),
        out_shape=[sds((padded, 2 * span), bf16)]
        + [sds((padded, 3 * HD), bf16)] * group,
        in_specs=[pl.BlockSpec(memory_space=pl.ANY), whole(1, 1)]
        + [whole(heads, -(-padded // 128) * 128)]
        + [whole(padded, span)] * 3,
        out_specs=[whole(padded, 2 * span)] + [whole(padded, 3 * HD)] * group,
        scratch_shapes=[pltpu.VMEM((padded, span), bf16)],
        compiler_params=pltpu.CompilerParams(vmem_limit_bytes=VMEM_LIMIT),
    )(low, frame_update.reshape(1, 1), rates.T, keys, values, queries)
    kv_own, *token_slots = prepared

    weights = lax.all_to_all(low, ("z", "grp"), 0, 0, tiled=True)
    if rows_local % 16:
        weights = weights.transpose(1, 0, 2, 3).reshape(3, hidden, HD)
    for d in served(group)[1:]:
        pairs = [(s, s ^ d) for s in range(group) if s ^ d < heads]
        token_slots[d] = lax.ppermute(token_slots[d], "grp", pairs)

    last = group // 2
    early_slots = [d for d in served(group) if d != last]
    early_grads, early_fast = call(
        functools.partial(early_body, len(early_slots)),
        [sds((3, hidden, HD), f32), sds((len(early_slots), padded, HD), bf16)],
        scratch=gradient_scratch(len(early_slots), padded, hidden) + apply_scratch(padded, hidden),
        flops=1e9,
    )(*(token_slots[d] for d in early_slots), weights)
    partials = list(
        call(
            functools.partial(late_body, group, nz),
            [sds((hidden, HD), bf16)] * nz,
            scratch=[pltpu.VMEM((3, hidden, HD), bf16)] + gradient_scratch(1, padded, hidden),
            flops=5e8,
        )(token_slots[last], weights, early_grads)
    )
    weights, partials[0] = lax.optimization_barrier((weights, partials[0]))
    for d in served(nz)[1:]:
        pairs = []
        for z in range(nz):
            pairs += [
                (z * group + j, (z ^ d) * group + j)
                for j in range(heads)
                if ((z ^ d) - j) % nz < 3
            ]
        partials[d] = lax.ppermute(partials[d], ("z", "grp"), pairs)

    fast_slots = call(
        functools.partial(late_apply_body, early_slots, last),
        sds((group, padded, HD), bf16),
        scratch=apply_scratch(padded, hidden),
        flops=1e3,
        moved=1024,
    )(token_slots[last], weights, early_fast)
    kv_own, partials[0], fast_slots = lax.optimization_barrier((kv_own, partials[0], fast_slots))
    fast_slots = lax.all_to_all(fast_slots, "grp", 0, 0, tiled=True)

    ring = [(i, i + 1) for i in range(count - 1)]
    kv_back = lax.ppermute(kv_own, ("z", "grp"), ring)

    ortho = call(functools.partial(ortho_body, heads, nz), sds((hidden, HD), bf16), flops=1e9)(
        *(partials[d] for d in served(nz))
    )
    queries, ortho = lax.optimization_barrier((queries, ortho))
    rows = lax.all_to_all(
        ortho.reshape(count, rows_local, HD), ("z", "grp"), 0, 0, tiled=True
    )
    new_weights = call(
        functools.partial(finish_body, nz, group), sds(fast_weights.shape, f32), flops=1e6
    )(fast_weights, rows)

    attended = pl.pallas_call(
        functools.partial(attend_body, heads, tokens),
        grid=(1,),
        out_shape=sds((padded, span), f32),
        in_specs=[whole(padded, span)] + [whole(padded, 2 * span)] * 2,
        out_specs=whole(padded, span),
        compiler_params=pltpu.CompilerParams(vmem_limit_bytes=VMEM_LIMIT),
    )(queries, kv_own, kv_back)
    fast, squares = call(
        functools.partial(assemble_body, heads),
        [sds((padded, span), bf16), sds((8, padded), f32)],
        flops=1e7,
    )(fast_slots)
    all_squares = [squares] + [
        lax.ppermute(squares, "head", [(s, (s + d) % nh) for s in range(nh)]) for d in range(1, nh)
    ]
    block_out = pl.pallas_call(
        functools.partial(block_body, span * nh),
        grid=(1,),
        out_shape=sds((tokens, span), bf16),
        in_specs=[whole(1, span), whole(padded, span), whole(padded, span)]
        + [whole(8, padded)] * nh,
        out_specs=whole(padded, span),
        compiler_params=pltpu.CompilerParams(vmem_limit_bytes=VMEM_LIMIT),
    )(gain.reshape(1, span), attended, fast, *all_squares)
    return (block_out, new_weights)


def solution(mesh):
    group = 4
    nh = mesh.shape["head"]
    inner = Mesh(
        np.asarray(mesh.devices).reshape(mesh.shape["ctx"] // group, group, nh),
        ("z", "grp", "head"),
    )
    ctx = ("z", "grp")
    placed = (
        P(ctx, "head"),
        P(ctx, "head"),
        P(ctx, "head"),
        P(ctx, "head"),
        P(ctx),
        P(None, "head", ctx, None),
        P("head"),
    )
    return jax.shard_map(
        on_device,
        mesh=inner,
        in_specs=placed,
        out_specs=(P(ctx, "head"), P(None, "head", ctx, None)),
        check_vma=False,
    )
```

```python
import functools

import jax
import jax.numpy as jnp
import numpy as np
from jax import lax
from jax.experimental import pallas as pl
from jax.experimental.pallas import tpu as pltpu
from jax.sharding import Mesh, PartitionSpec as P

HD = 128
NS_STEPS = 5

epsilon = 1e-06
quintic_a = 3.4445
quintic_b = -4.775
quintic_c = 2.0315
highest = lax.Precision.HIGHEST
f32 = jnp.float32
bf16 = jnp.bfloat16
VMEM_LIMIT = 24 * 1024 * 1024


def dot(a, b, contract, precision=None):
    return lax.dot_general(
        a, b, ((contract[:1], contract[1:]), ((), ())),
        precision=precision, preferred_element_type=f32,
    )


def call(body, outs, scratch=(), in_specs=None, flops=1e8, moved=1 << 20, **kw):
    given = {} if in_specs is None else {"in_specs": in_specs}
    return pl.pallas_call(
        body,
        out_shape=outs,
        **given,
        scratch_shapes=list(scratch),
        compiler_params=pltpu.CompilerParams(vmem_limit_bytes=VMEM_LIMIT),
        cost_estimate=pl.CostEstimate(flops=int(flops), bytes_accessed=moved, transcendentals=0),
        **kw,
    )


def sds(shape, dtype):
    return jax.ShapeDtypeStruct(shape, dtype)


def served(n):
    return [0] + list(range(n - 1, 0, -1))


def position():
    return lax.axis_index("z"), lax.axis_index("grp")


def sigmoid(x):
    return 0.5 * jnp.tanh(0.5 * x) + 0.5


def cast_body(heads, group, w_ref, w_out):
    slots = w_out.shape[0] // group
    for j in range(group):
        for m in range(3):
            low = w_ref[m, min(j, heads - 1)].astype(bf16)
            for z in range(slots):
                w_out[z * group + j, m] = low


def prep_body(
    heads, group, tokens, after, update, rate_ref, k_ref, v_ref, q_ref, kv_out, *outs
):
    token_outs, targets = outs[:-1], outs[-1]
    padded = kv_out.shape[0]
    place = position()
    valid = lax.broadcasted_iota(jnp.int32, (padded, 1), 0) < tokens
    none = jnp.zeros((), bf16)
    keep = update[...].astype(f32)
    lane_head = lax.broadcasted_iota(jnp.int32, (heads, heads * HD), 1) // HD
    row = lax.broadcasted_iota(jnp.int32, (heads, heads * HD), 0)
    rate = dot(rate_ref[...], (row == lane_head).astype(f32), (0, 0), highest)[:padded]
    targets[...] = jnp.where(valid, ((rate * keep) * v_ref[...].astype(f32)).astype(bf16), none)
    for d in range(group):
        head = jnp.minimum(place[1] ^ d, heads - 1)
        cols = pl.ds(pl.multiple_of(head * HD, HD), HD)
        token_outs[d][:, :HD] = jnp.where(valid, k_ref[:, cols], none)
        token_outs[d][:, HD : 2 * HD] = targets[:, cols]
        token_outs[d][:, 2 * HD :] = jnp.where(valid, q_ref[:, cols], none)
    kv_out[:, : heads * HD] = jnp.where(valid, k_ref[...], none)
    kv_out[:, heads * HD :] = jnp.where(valid, v_ref[...], none)


def gradients(token_refs, w_ref, k_all, t_all, staged, deltas):
    padded = token_refs[0].shape[0]
    width = k_all.shape[0]
    filled = len(token_refs) * padded
    for i, ref in enumerate(token_refs):
        k_all[i * padded : (i + 1) * padded] = ref[:, :HD]
        t_all[i * padded : (i + 1) * padded] = ref[:, HD : 2 * HD]
    if width > filled:
        k_all[filled:] = jnp.zeros((width - filled, HD), bf16)
        t_all[filled:] = jnp.zeros((width - filled, HD), bf16)
    hidden = deltas.shape[1]
    w1, w3, w2 = (weight_rows(w_ref, m, 0, hidden) for m in range(3))
    tall = 64
    for left in range(0, width, staged.shape[3]):
        right = min(left + staged.shape[3], width)
        cols, used = slice(left, right), slice(0, right - left)
        stage = staged.at[(left // staged.shape[3]) % staged.shape[0]]
        stage[0, :, used] = dot(w1, k_all[cols], (1, 1))
        stage[1, :, used] = dot(w3, k_all[cols], (1, 1))
        stage[2, :, used] = dot(w2, t_all[cols], (1, 1))
        for start in range(0, hidden, tall):
            rows = slice(start, start + tall)
            pre_one, pre_three, back = (stage[i, rows, used] for i in range(3))
            sig = sigmoid(pre_one)
            gate = pre_one * sig
            deltas[2, rows, cols] = (gate * pre_three).astype(bf16)
            deltas[1, rows, cols] = (back * gate).astype(bf16)
            deltas[0, rows, cols] = (
                (back * pre_three) * (sig * (1.0 + pre_one * (1.0 - sig)))
            ).astype(bf16)
    return (
        dot(deltas[0], k_all[...], (1, 0)),
        dot(deltas[1], k_all[...], (1, 0)),
        dot(deltas[2], t_all[...], (1, 0)),
    )


def gradient_scratch(slots, padded, hidden):
    width = -(-slots * padded // 128) * 128
    return [
        pltpu.VMEM((width, HD), bf16),
        pltpu.VMEM((width, HD), bf16),
        pltpu.VMEM((2, 3, hidden, 256), f32),
        pltpu.VMEM((3, hidden, width), bf16),
    ]


def apply_tokens(query, w_ref, stage, act):
    hidden = act.shape[1]
    tall = 16
    w1, w3, w2 = (weight_rows(w_ref, m, 0, hidden) for m in range(3))
    stage[0] = dot(query, w1, (1, 1))
    stage[1] = dot(query, w3, (1, 1))
    for start in range(0, query.shape[0], tall):
        rows = slice(start, start + tall)
        proj = stage[0, rows]
        act[rows] = (proj * sigmoid(proj) * stage[1, rows]).astype(bf16)
    return dot(act[...], w2, (1, 0)).astype(bf16)


def apply_scratch(padded, hidden):
    return [pltpu.VMEM((2, 2, padded, hidden), f32), pltpu.VMEM((2, padded, hidden), bf16)]


def early_body(count, *refs):
    token_refs, w_ref = refs[:count], refs[count]
    grads, fast = refs[count + 1 : count + 3]
    scratch, (staged, acts) = refs[count + 3 : -2], refs[-2:]
    for m, grad in enumerate(gradients(token_refs, w_ref, *scratch)):
        grads[m] = grad
    for i, ref in enumerate(token_refs):
        fast[i] = apply_tokens(ref[:, 2 * HD :], w_ref, staged.at[i % 2], acts.at[i % 2])


def late_body(group, slots, token_ref, w_ref, early, *refs):
    place = position()
    outs, sums, scratch = refs[:slots], refs[slots], refs[slots + 1 :]
    for m, grad in enumerate(gradients([token_ref], w_ref, *scratch)):
        sums[m] = (early[m] + grad).astype(bf16)
    for d in range(slots):
        matrix = lax.rem((place[0] ^ d) - place[1] + group * slots, slots)
        chosen = sums[jnp.minimum(matrix, 2)]
        outs[d][...] = jnp.where(matrix < 3, chosen, jnp.zeros_like(chosen))


def late_apply_body(early_slots, last, token_ref, w_ref, early, out, staged, acts):
    place = position()
    for i, d in enumerate(early_slots):
        out[place[1] ^ d] = early[i]
    out[place[1] ^ last] = apply_tokens(
        token_ref[:, 2 * HD :], w_ref, staged.at[0], acts.at[0]
    )


def weight_rows(w_ref, m, start, block):
    if len(w_ref.shape) == 3:
        return w_ref[m, start : start + block]
    rows = w_ref.shape[2]
    return w_ref[start // rows : (start + block) // rows, m].reshape(block, HD)


def parts_of(x):
    high = x.astype(bf16)
    return high, (x - high.astype(f32)).astype(bf16)


def left_of(x):
    high, low = parts_of(x)
    return jnp.concatenate([high, high, low], axis=1)


def right_of(x):
    high, low = parts_of(x)
    return jnp.concatenate([high, low, high], axis=0)


def ortho_body(heads, slots, *refs):
    place = position()
    matrix = lax.rem(place[0] - place[1] + heads * slots, slots)
    owner = (place[1] < heads) & (matrix < 3)

    @pl.when(owner)
    def _():
        orthogonalize(refs[:-1], refs[-1])

    @pl.when(jnp.logical_not(owner))
    def _():
        refs[-1][...] = jnp.zeros(refs[-1].shape, refs[-1].dtype)


def orthogonalize(parts, out):
    grads = parts[0][...].astype(f32)
    for part in parts[1:]:
        grads = grads + part[...].astype(f32)
    eye = (
        lax.broadcasted_iota(jnp.int32, (HD, HD), 0) == lax.broadcasted_iota(jnp.int32, (HD, HD), 1)
    ).astype(f32)
    both = jnp.concatenate(parts_of(grads), axis=1)
    blocks = dot(both, both, (0, 0))
    raw = (blocks[:HD, HD:] + blocks[HD:, :HD]) + blocks[:HD, :HD]
    square = jnp.sum(jnp.sum(raw * eye, axis=0, keepdims=True), axis=1, keepdims=True)
    scale = lax.rsqrt(square + epsilon)
    gram = raw * scale * scale
    total = None
    for step in range(NS_STEPS):
        square_gram = dot(left_of(gram), right_of(gram), (1, 0))
        mix = quintic_a * eye + quintic_b * gram + quintic_c * square_gram
        right = right_of(mix)
        if step < NS_STEPS - 1:
            gram = dot(left_of(dot(left_of(gram), right, (1, 0))), right, (1, 0))
            total = mix if total is None else dot(left_of(total), right, (1, 0))
    ortho = dot(left_of(grads * scale), right_of(total), (1, 0))
    out[...] = dot(left_of(ortho), right, (1, 0)).astype(out.dtype)


def finish_body(slots, group, w_ref, rows_ref, out):
    heads = w_ref.shape[1]
    for m in range(3):
        for h in range(heads):
            weights = w_ref[m, h]
            summed = weights + rows_ref[((m + h) % slots) * group + h].astype(f32)
            old = jnp.sqrt(jnp.sum(weights * weights, axis=1, keepdims=True))
            new = lax.rsqrt(jnp.sum(summed * summed, axis=1, keepdims=True) + epsilon)
            out[m, h] = summed * (old * new)


def attend_body(heads, tokens, q_ref, own_ref, back_ref, out):
    padded = own_ref.shape[0]
    span = heads * HD
    column = lax.broadcasted_iota(jnp.int32, (1, 2 * padded), 1)
    place = position()
    first = (place[0] == 0) & (place[1] == 0)
    stop = jnp.where(first, padded, padded + tokens)
    live = (column < tokens) | ((column >= padded) & (column < stop))
    for h in range(heads):
        cols = slice(h * HD, (h + 1) * HD)
        key = jnp.concatenate([own_ref[:, cols], back_ref[:, cols]], axis=0)
        vcols = slice(span + h * HD, span + (h + 1) * HD)
        value = jnp.concatenate([own_ref[:, vcols], back_ref[:, vcols]], axis=0)
        scores = dot(q_ref[:, cols], key, (1, 1)) * (HD ** (-0.5))
        scores = jnp.where(live, scores, -1e30)
        weights = jnp.exp(scores - jnp.max(scores, axis=1, keepdims=True))
        probs = (weights / jnp.sum(weights, axis=1, keepdims=True)).astype(bf16)
        out[:, cols] = dot(probs, value, (1, 0))


def assemble_body(heads, slots, out, squares):
    for h in range(heads):
        out[:, h * HD : (h + 1) * HD] = slots[h]
    fast = out[...].astype(f32)
    squares[...] = dot(jnp.ones((8, heads * HD), f32), fast * fast, (1, 1), highest)


def block_body(features, gain_ref, attended_ref, fast_ref, *refs):
    squares, out = refs[:-1], refs[-1]
    total = squares[0][...]
    for other in squares[1:]:
        total = total + other[...]
    pick = (lax.broadcasted_iota(jnp.int32, (8, HD), 0) == 0).astype(f32)
    spread = dot(total, pick, (0, 0), highest) * (1.0 / features)
    scale = lax.rsqrt(spread + epsilon)
    for h in range(fast_ref.shape[1] // HD):
        cols = slice(h * HD, (h + 1) * HD)
        out[:, cols] = (
            attended_ref[:, cols] + fast_ref[:, cols].astype(f32) * gain_ref[:, cols] * scale
        ).astype(bf16)


def on_device(queries, keys, values, rates, frame_update, fast_weights, gain):
    tokens = queries.shape[0]
    heads = queries.shape[1] // HD
    rows_local = fast_weights.shape[2]
    nz, group, nh = lax.axis_size("z"), lax.axis_size("grp"), lax.axis_size("head")
    count = nz * group
    hidden = count * rows_local
    padded = -(-tokens // 16) * 16
    span = heads * HD

    def whole(*shape):
        return pl.BlockSpec(shape, lambda i: (0,) * len(shape))

    low_shape = (count, 3, rows_local, HD)
    low = call(
        functools.partial(cast_body, heads, group), sds(low_shape, bf16), flops=1e6
    )(fast_weights)
    prepared = pl.pallas_call(
        functools.partial(prep_body, heads, group, tokens),
        grid=(1,),
        out_shape=[sds((padded, 2 * span), bf16)]
        + [sds((padded, 3 * HD), bf16)] * group,
        in_specs=[pl.BlockSpec(memory_space=pl.ANY), whole(1, 1)]
        + [whole(heads, -(-padded // 128) * 128)]
        + [whole(padded, span)] * 3,
        out_specs=[whole(padded, 2 * span)] + [whole(padded, 3 * HD)] * group,
        scratch_shapes=[pltpu.VMEM((padded, span), bf16)],
        compiler_params=pltpu.CompilerParams(vmem_limit_bytes=VMEM_LIMIT),
    )(low, frame_update.reshape(1, 1), rates.T, keys, values, queries)
    kv_own, *token_slots = prepared

    weights = lax.all_to_all(low, ("z", "grp"), 0, 0, tiled=True)
    if rows_local % 16:
        weights = weights.transpose(1, 0, 2, 3).reshape(3, hidden, HD)
    for d in served(group)[1:]:
        pairs = [(s, s ^ d) for s in range(group) if s ^ d < heads]
        token_slots[d] = lax.ppermute(token_slots[d], "grp", pairs)

    last = group // 2
    early_slots = [d for d in served(group) if d != last]
    early_grads, early_fast = call(
        functools.partial(early_body, len(early_slots)),
        [sds((3, hidden, HD), f32), sds((len(early_slots), padded, HD), bf16)],
        scratch=gradient_scratch(len(early_slots), padded, hidden) + apply_scratch(padded, hidden),
        flops=1e9,
    )(*(token_slots[d] for d in early_slots), weights)
    partials = list(
        call(
            functools.partial(late_body, group, nz),
            [sds((hidden, HD), bf16)] * nz,
            scratch=[pltpu.VMEM((3, hidden, HD), bf16)] + gradient_scratch(1, padded, hidden),
            flops=5e8,
        )(token_slots[last], weights, early_grads)
    )
    weights, partials[0] = lax.optimization_barrier((weights, partials[0]))
    def summed(d, partial):
        pairs = []
        for z in range(nz):
            pairs += [
                (z * group + j, (z ^ d) * group + j)
                for j in range(heads)
                if ((z ^ d) - j) % nz < 3
            ]
        return lax.ppermute(partial, ("z", "grp"), pairs)

    for d in served(nz)[1:-1]:
        partials[d] = summed(d, partials[d])

    fast_slots = call(
        functools.partial(late_apply_body, early_slots, last),
        sds((group, padded, HD), bf16),
        scratch=apply_scratch(padded, hidden),
        flops=1e3,
        moved=1024,
    )(token_slots[last], weights, early_fast)
    kv_own, partials[1], fast_slots = lax.optimization_barrier((kv_own, partials[1], fast_slots))
    partials[1] = summed(1, partials[1])
    fast_slots = lax.all_to_all(fast_slots, "grp", 0, 0, tiled=True)

    ring = [(i, i + 1) for i in range(count - 1)]
    kv_back = lax.ppermute(kv_own, ("z", "grp"), ring)

    ortho = call(functools.partial(ortho_body, heads, nz), sds((hidden, HD), bf16), flops=1e9)(
        *(partials[d] for d in served(nz))
    )
    queries, ortho = lax.optimization_barrier((queries, ortho))
    rows = lax.all_to_all(
        ortho.reshape(count, rows_local, HD), ("z", "grp"), 0, 0, tiled=True
    )
    new_weights = call(
        functools.partial(finish_body, nz, group), sds(fast_weights.shape, f32), flops=1e6
    )(fast_weights, rows)

    attended = pl.pallas_call(
        functools.partial(attend_body, heads, tokens),
        grid=(1,),
        out_shape=sds((padded, span), f32),
        in_specs=[whole(padded, span)] + [whole(padded, 2 * span)] * 2,
        out_specs=whole(padded, span),
        compiler_params=pltpu.CompilerParams(vmem_limit_bytes=VMEM_LIMIT),
    )(queries, kv_own, kv_back)
    fast, squares = call(
        functools.partial(assemble_body, heads),
        [sds((padded, span), bf16), sds((8, padded), f32)],
        flops=1e7,
    )(fast_slots)
    all_squares = [squares] + [
        lax.ppermute(squares, "head", [(s, (s + d) % nh) for s in range(nh)]) for d in range(1, nh)
    ]
    block_out = pl.pallas_call(
        functools.partial(block_body, span * nh),
        grid=(1,),
        out_shape=sds((tokens, span), bf16),
        in_specs=[whole(1, span), whole(padded, span), whole(padded, span)]
        + [whole(8, padded)] * nh,
        out_specs=whole(padded, span),
        compiler_params=pltpu.CompilerParams(vmem_limit_bytes=VMEM_LIMIT),
    )(gain.reshape(1, span), attended, fast, *all_squares)
    return (block_out, new_weights)


def solution(mesh):
    group = 4
    nh = mesh.shape["head"]
    inner = Mesh(
        np.asarray(mesh.devices).reshape(mesh.shape["ctx"] // group, group, nh),
        ("z", "grp", "head"),
    )
    ctx = ("z", "grp")
    placed = (
        P(ctx, "head"),
        P(ctx, "head"),
        P(ctx, "head"),
        P(ctx, "head"),
        P(ctx),
        P(None, "head", ctx, None),
        P("head"),
    )
    return jax.shard_map(
        on_device,
        mesh=inner,
        in_specs=placed,
        out_specs=(P(ctx, "head"), P(None, "head", ctx, None)),
        check_vma=False,
    )
```

```python
import functools

import jax
import jax.numpy as jnp
import numpy as np
from jax import lax
from jax.experimental import pallas as pl
from jax.experimental.pallas import tpu as pltpu
from jax.sharding import Mesh, PartitionSpec as P

HD = 128
NS_STEPS = 5

epsilon = 1e-06
quintic_a = 3.4445
quintic_b = -4.775
quintic_c = 2.0315
highest = lax.Precision.HIGHEST
f32 = jnp.float32
bf16 = jnp.bfloat16
VMEM_LIMIT = 24 * 1024 * 1024


def dot(a, b, contract, precision=None):
    return lax.dot_general(
        a, b, ((contract[:1], contract[1:]), ((), ())),
        precision=precision, preferred_element_type=f32,
    )


def call(body, outs, scratch=(), in_specs=None, flops=1e8, moved=1 << 20, **kw):
    given = {} if in_specs is None else {"in_specs": in_specs}
    return pl.pallas_call(
        body,
        out_shape=outs,
        **given,
        scratch_shapes=list(scratch),
        compiler_params=pltpu.CompilerParams(vmem_limit_bytes=VMEM_LIMIT),
        cost_estimate=pl.CostEstimate(flops=int(flops), bytes_accessed=moved, transcendentals=0),
        **kw,
    )


def sds(shape, dtype):
    return jax.ShapeDtypeStruct(shape, dtype)


def served(n):
    return [0] + list(range(n - 1, 0, -1))


def first_owner(h):
    return h & 1


def position():
    return lax.axis_index("z"), lax.axis_index("grp")


def sigmoid(x):
    return 0.5 * jnp.tanh(0.5 * x) + 0.5


def cast_body(heads, group, w_ref, w_out):
    slots = w_out.shape[0] // group
    for j in range(group):
        for m in range(3):
            low = w_ref[m, min(j, heads - 1)].astype(bf16)
            for z in range(slots):
                w_out[z * group + j, m] = low


def prep_body(
    heads, group, tokens, after, update, rate_ref, k_ref, v_ref, q_ref, kv_out, *outs
):
    token_outs, targets = outs[:-1], outs[-1]
    padded = kv_out.shape[0]
    place = position()
    valid = lax.broadcasted_iota(jnp.int32, (padded, 1), 0) < tokens
    none = jnp.zeros((), bf16)
    keep = update[...].astype(f32)
    lane_head = lax.broadcasted_iota(jnp.int32, (heads, heads * HD), 1) // HD
    row = lax.broadcasted_iota(jnp.int32, (heads, heads * HD), 0)
    rate = dot(rate_ref[...], (row == lane_head).astype(f32), (0, 0), highest)[:padded]
    targets[...] = ((rate * keep) * v_ref[...].astype(f32)).astype(bf16)
    for d in range(group):
        head = jnp.minimum(place[1] ^ d, heads - 1)
        cols = pl.ds(pl.multiple_of(head * HD, HD), HD)
        for i, source in enumerate((k_ref, targets, q_ref)):
            token_outs[d][:, i * HD : (i + 1) * HD] = source[:tokens, cols]
    kv_out[:, : heads * HD] = jnp.where(valid, k_ref[...], none)
    kv_out[:, heads * HD :] = jnp.where(valid, v_ref[...], none)


def gradients(token_refs, w_ref, k_all, t_all, staged, deltas):
    tokens = token_refs[0].shape[0]
    padded = -(-tokens // 16) * 16
    width = k_all.shape[0]
    filled = len(token_refs) * padded
    for i, ref in enumerate(token_refs):
        for part, rows in enumerate((k_all, t_all)):
            rows[(i + 1) * padded - 16 : (i + 1) * padded] = jnp.zeros((16, HD), bf16)
            rows[i * padded : i * padded + tokens] = ref[:, part * HD : (part + 1) * HD]
    if width > filled:
        k_all[filled:] = jnp.zeros((width - filled, HD), bf16)
        t_all[filled:] = jnp.zeros((width - filled, HD), bf16)
    hidden = deltas.shape[1]
    w1, w3, w2 = (weight_rows(w_ref, m, 0, hidden) for m in range(3))
    tall = 64
    for left in range(0, width, staged.shape[3]):
        right = min(left + staged.shape[3], width)
        cols, used = slice(left, right), slice(0, right - left)
        stage = staged.at[(left // staged.shape[3]) % staged.shape[0]]
        stage[0, :, used] = dot(w1, k_all[cols], (1, 1))
        stage[1, :, used] = dot(w3, k_all[cols], (1, 1))
        stage[2, :, used] = dot(w2, t_all[cols], (1, 1))
        for start in range(0, hidden, tall):
            rows = slice(start, start + tall)
            pre_one, pre_three, back = (stage[i, rows, used] for i in range(3))
            sig = sigmoid(pre_one)
            gate = pre_one * sig
            deltas[2, rows, cols] = (gate * pre_three).astype(bf16)
            deltas[1, rows, cols] = (back * gate).astype(bf16)
            deltas[0, rows, cols] = (
                (back * pre_three) * (sig * (1.0 + pre_one * (1.0 - sig)))
            ).astype(bf16)
    return (
        dot(deltas[0], k_all[...], (1, 0)),
        dot(deltas[1], k_all[...], (1, 0)),
        dot(deltas[2], t_all[...], (1, 0)),
    )


def gradient_scratch(slots, padded, hidden):
    width = -(-slots * padded // 128) * 128
    return [
        pltpu.VMEM((width, HD), bf16),
        pltpu.VMEM((width, HD), bf16),
        pltpu.VMEM((2, 3, hidden, 256), f32),
        pltpu.VMEM((3, hidden, width), bf16),
    ]


def apply_tokens(token_ref, w_ref, stage, act, held):
    hidden = act.shape[1]
    tall = 16
    w1, w3, w2 = (weight_rows(w_ref, m, 0, hidden) for m in range(3))
    held[held.shape[0] - 16 :] = jnp.zeros((16, HD), bf16)
    held[: token_ref.shape[0]] = token_ref[:, 2 * HD :]
    query = held[...]
    stage[0] = dot(query, w1, (1, 1))
    stage[1] = dot(query, w3, (1, 1))
    for start in range(0, query.shape[0], tall):
        rows = slice(start, start + tall)
        proj = stage[0, rows]
        act[rows] = (proj * sigmoid(proj) * stage[1, rows]).astype(bf16)
    return dot(act[...], w2, (1, 0)).astype(bf16)


def apply_scratch(padded, hidden):
    return [
        pltpu.VMEM((2, 2, padded, hidden), f32),
        pltpu.VMEM((2, padded, hidden), bf16),
        pltpu.VMEM((2, padded, HD), bf16),
    ]


def early_body(count, *refs):
    token_refs, w_ref = refs[:count], refs[count]
    grads, fast = refs[count + 1 : count + 3]
    scratch, (staged, acts, held) = refs[count + 3 : -3], refs[-3:]
    for m, grad in enumerate(gradients(token_refs, w_ref, *scratch)):
        grads[m] = grad
    for i, ref in enumerate(token_refs):
        fast[i] = apply_tokens(ref, w_ref, *(buffer.at[i % 2] for buffer in (staged, acts, held)))


def late_body(group, slots, token_ref, w_ref, early, *refs):
    place = position()
    outs, sums, scratch = refs[:slots], refs[slots], refs[slots + 1 :]
    for m, grad in enumerate(gradients([token_ref], w_ref, *scratch)):
        sums[m] = (early[m] + grad).astype(bf16)
    for d in range(slots):
        matrix = lax.rem((place[0] ^ d) - first_owner(place[1]) + slots, slots)
        chosen = sums[jnp.minimum(matrix, 2)]
        outs[d][...] = jnp.where(matrix < 3, chosen, jnp.zeros_like(chosen))


def late_apply_body(early_slots, last, token_ref, w_ref, early, out, staged, acts, held):
    place = position()
    for i, d in enumerate(early_slots):
        out[place[1] ^ d] = early[i]
    out[place[1] ^ last] = apply_tokens(
        token_ref, w_ref, staged.at[0], acts.at[0], held.at[0]
    )


def weight_rows(w_ref, m, start, block):
    if len(w_ref.shape) == 3:
        return w_ref[m, start : start + block]
    rows = w_ref.shape[2]
    return w_ref[start // rows : (start + block) // rows, m].reshape(block, HD)


def parts_of(x):
    high = x.astype(bf16)
    return high, (x - high.astype(f32)).astype(bf16)


def left_of(x):
    high, low = parts_of(x)
    return jnp.concatenate([high, high, low], axis=1)


def right_of(x):
    high, low = parts_of(x)
    return jnp.concatenate([high, low, high], axis=0)


def ortho_body(heads, slots, *refs):
    place = position()
    matrix = lax.rem(place[0] - first_owner(place[1]) + slots, slots)
    owner = (place[1] < heads) & (matrix < 3)

    @pl.when(owner)
    def _():
        orthogonalize(refs[:-1], refs[-1])

    @pl.when(jnp.logical_not(owner))
    def _():
        refs[-1][...] = jnp.zeros(refs[-1].shape, refs[-1].dtype)


def orthogonalize(parts, out):
    grads = parts[0][...].astype(f32)
    for part in parts[1:]:
        grads = grads + part[...].astype(f32)
    eye = (
        lax.broadcasted_iota(jnp.int32, (HD, HD), 0) == lax.broadcasted_iota(jnp.int32, (HD, HD), 1)
    ).astype(f32)
    both = jnp.concatenate(parts_of(grads), axis=1)
    blocks = dot(both, both, (0, 0))
    raw = (blocks[:HD, HD:] + blocks[HD:, :HD]) + blocks[:HD, :HD]
    square = jnp.sum(jnp.sum(raw * eye, axis=0, keepdims=True), axis=1, keepdims=True)
    scale = lax.rsqrt(square + epsilon)
    gram = raw * scale * scale
    total = None
    for step in range(NS_STEPS):
        square_gram = dot(left_of(gram), right_of(gram), (1, 0))
        mix = quintic_a * eye + quintic_b * gram + quintic_c * square_gram
        right = right_of(mix)
        if step < NS_STEPS - 1:
            gram = dot(left_of(dot(left_of(gram), right, (1, 0))), right, (1, 0))
            total = mix if total is None else dot(left_of(total), right, (1, 0))
    ortho = dot(left_of(grads * scale), right_of(total), (1, 0))
    out[...] = dot(left_of(ortho), right, (1, 0)).astype(out.dtype)


def finish_body(slots, group, w_ref, rows_ref, out):
    heads = w_ref.shape[1]
    for m in range(3):
        for h in range(heads):
            weights = w_ref[m, h]
            summed = weights + rows_ref[((m + first_owner(h)) % slots) * group + h].astype(f32)
            old = jnp.sqrt(jnp.sum(weights * weights, axis=1, keepdims=True))
            new = lax.rsqrt(jnp.sum(summed * summed, axis=1, keepdims=True) + epsilon)
            out[m, h] = summed * (old * new)


def attend_body(heads, tokens, q_ref, own_ref, back_ref, out):
    padded = own_ref.shape[0]
    span = heads * HD
    column = lax.broadcasted_iota(jnp.int32, (1, 2 * padded), 1)
    place = position()
    first = (place[0] == 0) & (place[1] == 0)
    stop = jnp.where(first, padded, padded + tokens)
    live = (column < tokens) | ((column >= padded) & (column < stop))
    for h in range(heads):
        cols = slice(h * HD, (h + 1) * HD)
        key = jnp.concatenate([own_ref[:, cols], back_ref[:, cols]], axis=0)
        vcols = slice(span + h * HD, span + (h + 1) * HD)
        value = jnp.concatenate([own_ref[:, vcols], back_ref[:, vcols]], axis=0)
        scores = dot(q_ref[:, cols], key, (1, 1)) * (HD ** (-0.5))
        scores = jnp.where(live, scores, -1e30)
        weights = jnp.exp(scores - jnp.max(scores, axis=1, keepdims=True))
        probs = (weights / jnp.sum(weights, axis=1, keepdims=True)).astype(bf16)
        out[:, cols] = dot(probs, value, (1, 0))


def assemble_body(heads, slots, out, squares):
    for h in range(heads):
        out[:, h * HD : (h + 1) * HD] = slots[h]
    fast = out[...].astype(f32)
    squares[...] = dot(jnp.ones((8, heads * HD), f32), fast * fast, (1, 1), highest)


def block_body(features, gain_ref, attended_ref, fast_ref, *refs):
    squares, out = refs[:-1], refs[-1]
    total = squares[0][...]
    for other in squares[1:]:
        total = total + other[...]
    pick = (lax.broadcasted_iota(jnp.int32, (8, HD), 0) == 0).astype(f32)
    spread = dot(total, pick, (0, 0), highest) * (1.0 / features)
    scale = lax.rsqrt(spread + epsilon)
    for h in range(fast_ref.shape[1] // HD):
        cols = slice(h * HD, (h + 1) * HD)
        out[:, cols] = (
            attended_ref[:, cols] + fast_ref[:, cols].astype(f32) * gain_ref[:, cols] * scale
        ).astype(bf16)


def on_device(queries, keys, values, rates, frame_update, fast_weights, gain):
    tokens = queries.shape[0]
    heads = queries.shape[1] // HD
    rows_local = fast_weights.shape[2]
    nz, group, nh = lax.axis_size("z"), lax.axis_size("grp"), lax.axis_size("head")
    count = nz * group
    hidden = count * rows_local
    padded = -(-tokens // 16) * 16
    span = heads * HD

    def whole(*shape):
        return pl.BlockSpec(shape, lambda i: (0,) * len(shape))

    low_shape = (count, 3, rows_local, HD)
    low = call(
        functools.partial(cast_body, heads, group), sds(low_shape, bf16), flops=1e6
    )(fast_weights)
    prepared = pl.pallas_call(
        functools.partial(prep_body, heads, group, tokens),
        grid=(1,),
        out_shape=[sds((padded, 2 * span), bf16)]
        + [sds((tokens, 3 * HD), bf16)] * group,
        in_specs=[pl.BlockSpec(memory_space=pl.ANY), whole(1, 1)]
        + [whole(heads, -(-padded // 128) * 128)]
        + [whole(padded, span)] * 3,
        out_specs=[whole(padded, 2 * span)] + [whole(tokens, 3 * HD)] * group,
        scratch_shapes=[pltpu.VMEM((padded, span), bf16)],
        compiler_params=pltpu.CompilerParams(vmem_limit_bytes=VMEM_LIMIT),
    )(low, frame_update.reshape(1, 1), rates.T, keys, values, queries)
    kv_own, *token_slots = prepared

    weights = lax.all_to_all(low, ("z", "grp"), 0, 0, tiled=True)
    if rows_local % 16:
        weights = weights.transpose(1, 0, 2, 3).reshape(3, hidden, HD)
    for d in served(group)[1:]:
        pairs = [(s, s ^ d) for s in range(group) if s ^ d < heads]
        token_slots[d] = lax.ppermute(token_slots[d], "grp", pairs)

    last = group // 2
    early_slots = [d for d in served(group) if d != last]
    early_grads, early_fast = call(
        functools.partial(early_body, len(early_slots)),
        [sds((3, hidden, HD), f32), sds((len(early_slots), padded, HD), bf16)],
        scratch=gradient_scratch(len(early_slots), padded, hidden) + apply_scratch(padded, hidden),
        flops=1e9,
    )(*(token_slots[d] for d in early_slots), weights)
    partials = list(
        call(
            functools.partial(late_body, group, nz),
            [sds((hidden, HD), bf16)] * nz,
            scratch=[pltpu.VMEM((3, hidden, HD), bf16)] + gradient_scratch(1, padded, hidden),
            flops=5e8,
        )(token_slots[last], weights, early_grads)
    )
    weights, partials[0] = lax.optimization_barrier((weights, partials[0]))
    for d in served(nz)[1:]:
        pairs = []
        for z in range(nz):
            pairs += [
                (z * group + j, (z ^ d) * group + j)
                for j in range(heads)
                if ((z ^ d) - first_owner(j)) % nz < 3
            ]
        partials[d] = lax.ppermute(partials[d], ("z", "grp"), pairs)

    fast_slots = call(
        functools.partial(late_apply_body, early_slots, last),
        sds((group, padded, HD), bf16),
        scratch=apply_scratch(padded, hidden),
        flops=1e3,
        moved=1024,
    )(token_slots[last], weights, early_fast)
    kv_own, partials[0], fast_slots = lax.optimization_barrier((kv_own, partials[0], fast_slots))
    fast_slots = lax.all_to_all(fast_slots, "grp", 0, 0, tiled=True)

    ring = [(i, i + 1) for i in range(count - 1)]
    kv_back = lax.ppermute(kv_own, ("z", "grp"), ring)

    ortho = call(functools.partial(ortho_body, heads, nz), sds((hidden, HD), bf16), flops=1e9)(
        *(partials[d] for d in served(nz))
    )
    queries, ortho = lax.optimization_barrier((queries, ortho))
    rows = lax.all_to_all(
        ortho.reshape(count, rows_local, HD), ("z", "grp"), 0, 0, tiled=True
    )
    new_weights = call(
        functools.partial(finish_body, nz, group), sds(fast_weights.shape, f32), flops=1e6
    )(fast_weights, rows)

    attended = pl.pallas_call(
        functools.partial(attend_body, heads, tokens),
        grid=(1,),
        out_shape=sds((padded, span), f32),
        in_specs=[whole(padded, span)] + [whole(padded, 2 * span)] * 2,
        out_specs=whole(padded, span),
        compiler_params=pltpu.CompilerParams(vmem_limit_bytes=VMEM_LIMIT),
    )(queries, kv_own, kv_back)
    fast, squares = call(
        functools.partial(assemble_body, heads),
        [sds((padded, span), bf16), sds((8, padded), f32)],
        flops=1e7,
    )(fast_slots)
    all_squares = [squares] + [
        lax.ppermute(squares, "head", [(s, (s + d) % nh) for s in range(nh)]) for d in range(1, nh)
    ]
    block_out = pl.pallas_call(
        functools.partial(block_body, span * nh),
        grid=(1,),
        out_shape=sds((tokens, span), bf16),
        in_specs=[whole(1, span), whole(padded, span), whole(padded, span)]
        + [whole(8, padded)] * nh,
        out_specs=whole(padded, span),
        compiler_params=pltpu.CompilerParams(vmem_limit_bytes=VMEM_LIMIT),
    )(gain.reshape(1, span), attended, fast, *all_squares)
    return (block_out, new_weights)


def solution(mesh):
    group = 4
    nh = mesh.shape["head"]
    inner = Mesh(
        np.asarray(mesh.devices).reshape(mesh.shape["ctx"] // group, group, nh),
        ("z", "grp", "head"),
    )
    ctx = ("z", "grp")
    placed = (
        P(ctx, "head"),
        P(ctx, "head"),
        P(ctx, "head"),
        P(ctx, "head"),
        P(ctx),
        P(None, "head", ctx, None),
        P("head"),
    )
    return jax.shard_map(
        on_device,
        mesh=inner,
        in_specs=placed,
        out_specs=(P(ctx, "head"), P(None, "head", ctx, None)),
        check_vma=False,
    )
```

```python
import functools

import jax
import jax.numpy as jnp
import numpy as np
from jax import lax
from jax.experimental import pallas as pl
from jax.experimental.pallas import tpu as pltpu
from jax.sharding import Mesh, PartitionSpec as P

HD = 128
NS_STEPS = 5

epsilon = 1e-06
quintic_a = 3.4445
quintic_b = -4.775
quintic_c = 2.0315
highest = lax.Precision.HIGHEST
f32 = jnp.float32
bf16 = jnp.bfloat16
VMEM_LIMIT = 24 * 1024 * 1024


def dot(a, b, contract, precision=None):
    return lax.dot_general(
        a, b, ((contract[:1], contract[1:]), ((), ())),
        precision=precision, preferred_element_type=f32,
    )


def call(body, outs, scratch=(), in_specs=None, flops=1e8, moved=1 << 20, **kw):
    given = {} if in_specs is None else {"in_specs": in_specs}
    return pl.pallas_call(
        body,
        out_shape=outs,
        **given,
        scratch_shapes=list(scratch),
        compiler_params=pltpu.CompilerParams(vmem_limit_bytes=VMEM_LIMIT),
        cost_estimate=pl.CostEstimate(flops=int(flops), bytes_accessed=moved, transcendentals=0),
        **kw,
    )


def sds(shape, dtype):
    return jax.ShapeDtypeStruct(shape, dtype)


def served(n):
    return [0] + list(range(n - 1, 0, -1))


def summed_order(n):
    return [0] + list(range(n // 2, n)) + list(range(1, n // 2))


def first_owner(h):
    return h & 1


def position():
    return lax.axis_index("z"), lax.axis_index("grp")


def sigmoid(x):
    return 0.5 * jnp.tanh(0.5 * x) + 0.5


def cast_body(heads, group, w_ref, w_out):
    slots = w_out.shape[0] // group
    for j in range(group):
        for m in range(3):
            low = w_ref[m, min(j, heads - 1)].astype(bf16)
            for z in range(slots):
                w_out[z * group + j, m] = low


def prep_body(
    heads, group, tokens, after, update, rate_ref, k_ref, v_ref, q_ref, kv_out, *outs
):
    token_outs, targets = outs[:-1], outs[-1]
    padded = kv_out.shape[0]
    place = position()
    valid = lax.broadcasted_iota(jnp.int32, (padded, 1), 0) < tokens
    none = jnp.zeros((), bf16)
    keep = update[...].astype(f32)
    lane_head = lax.broadcasted_iota(jnp.int32, (heads, heads * HD), 1) // HD
    row = lax.broadcasted_iota(jnp.int32, (heads, heads * HD), 0)
    rate = dot(rate_ref[...], (row == lane_head).astype(f32), (0, 0), highest)[:padded]
    targets[...] = ((rate * keep) * v_ref[...].astype(f32)).astype(bf16)
    for d in range(group):
        head = jnp.minimum(place[1] ^ d, heads - 1)
        cols = pl.ds(pl.multiple_of(head * HD, HD), HD)
        for i, source in enumerate((k_ref, targets, q_ref)):
            token_outs[d][:, i * HD : (i + 1) * HD] = source[:tokens, cols]
    kv_out[:, : heads * HD] = jnp.where(valid, k_ref[...], none)
    kv_out[:, heads * HD :] = jnp.where(valid, v_ref[...], none)


def gradients(token_refs, w_ref, k_all, t_all, staged, deltas):
    tokens = token_refs[0].shape[0]
    padded = -(-tokens // 16) * 16
    width = k_all.shape[0]
    filled = len(token_refs) * padded
    for i, ref in enumerate(token_refs):
        for part, rows in enumerate((k_all, t_all)):
            rows[(i + 1) * padded - 16 : (i + 1) * padded] = jnp.zeros((16, HD), bf16)
            rows[i * padded : i * padded + tokens] = ref[:, part * HD : (part + 1) * HD]
    if width > filled:
        k_all[filled:] = jnp.zeros((width - filled, HD), bf16)
        t_all[filled:] = jnp.zeros((width - filled, HD), bf16)
    hidden = deltas.shape[1]
    w1, w3, w2 = (weight_rows(w_ref, m, 0, hidden) for m in range(3))
    tall = 64
    for left in range(0, width, staged.shape[3]):
        right = min(left + staged.shape[3], width)
        cols, used = slice(left, right), slice(0, right - left)
        stage = staged.at[(left // staged.shape[3]) % staged.shape[0]]
        stage[0, :, used] = dot(w1, k_all[cols], (1, 1))
        stage[1, :, used] = dot(w3, k_all[cols], (1, 1))
        stage[2, :, used] = dot(w2, t_all[cols], (1, 1))
        for start in range(0, hidden, tall):
            rows = slice(start, start + tall)
            pre_one, pre_three, back = (stage[i, rows, used] for i in range(3))
            sig = sigmoid(pre_one)
            gate = pre_one * sig
            deltas[2, rows, cols] = (gate * pre_three).astype(bf16)
            deltas[1, rows, cols] = (back * gate).astype(bf16)
            deltas[0, rows, cols] = (
                (back * pre_three) * (sig * (1.0 + pre_one * (1.0 - sig)))
            ).astype(bf16)
    return (
        dot(deltas[0], k_all[...], (1, 0)),
        dot(deltas[1], k_all[...], (1, 0)),
        dot(deltas[2], t_all[...], (1, 0)),
    )


def gradient_scratch(slots, padded, hidden):
    width = -(-slots * padded // 128) * 128
    return [
        pltpu.VMEM((width, HD), bf16),
        pltpu.VMEM((width, HD), bf16),
        pltpu.VMEM((2, 3, hidden, 256), f32),
        pltpu.VMEM((3, hidden, width), bf16),
    ]


def apply_tokens(token_ref, w_ref, stage, act, held):
    hidden = act.shape[1]
    tall = 16
    w1, w3, w2 = (weight_rows(w_ref, m, 0, hidden) for m in range(3))
    held[held.shape[0] - 16 :] = jnp.zeros((16, HD), bf16)
    held[: token_ref.shape[0]] = token_ref[:, 2 * HD :]
    query = held[...]
    stage[0] = dot(query, w1, (1, 1))
    stage[1] = dot(query, w3, (1, 1))
    for start in range(0, query.shape[0], tall):
        rows = slice(start, start + tall)
        proj = stage[0, rows]
        act[rows] = (proj * sigmoid(proj) * stage[1, rows]).astype(bf16)
    return dot(act[...], w2, (1, 0)).astype(bf16)


def apply_scratch(padded, hidden):
    return [
        pltpu.VMEM((2, 2, padded, hidden), f32),
        pltpu.VMEM((2, padded, hidden), bf16),
        pltpu.VMEM((2, padded, HD), bf16),
    ]


def early_body(count, *refs):
    token_refs, w_ref = refs[:count], refs[count]
    grads, fast = refs[count + 1 : count + 3]
    scratch, (staged, acts, held) = refs[count + 3 : -3], refs[-3:]
    for m, grad in enumerate(gradients(token_refs, w_ref, *scratch)):
        grads[m] = grad
    for i, ref in enumerate(token_refs):
        fast[i] = apply_tokens(ref, w_ref, *(buffer.at[i % 2] for buffer in (staged, acts, held)))


def late_body(group, slots, token_ref, w_ref, early, *refs):
    place = position()
    outs, sums, scratch = refs[:slots], refs[slots], refs[slots + 1 :]
    for m, grad in enumerate(gradients([token_ref], w_ref, *scratch)):
        sums[m] = (early[m] + grad).astype(bf16)
    for d in range(slots):
        matrix = lax.rem((place[0] ^ d) - first_owner(place[1]) + slots, slots)
        chosen = sums[jnp.minimum(matrix, 2)]
        outs[d][...] = jnp.where(matrix < 3, chosen, jnp.zeros_like(chosen))


def late_apply_body(early_slots, last, token_ref, w_ref, early, out, staged, acts, held):
    place = position()
    for i, d in enumerate(early_slots):
        out[place[1] ^ d] = early[i]
    out[place[1] ^ last] = apply_tokens(
        token_ref, w_ref, staged.at[0], acts.at[0], held.at[0]
    )


def weight_rows(w_ref, m, start, block):
    if len(w_ref.shape) == 3:
        return w_ref[m, start : start + block]
    rows = w_ref.shape[2]
    return w_ref[start // rows : (start + block) // rows, m].reshape(block, HD)


def parts_of(x):
    high = x.astype(bf16)
    return high, (x - high.astype(f32)).astype(bf16)


def left_of(x):
    high, low = parts_of(x)
    return jnp.concatenate([high, high, low], axis=1)


def right_of(x):
    high, low = parts_of(x)
    return jnp.concatenate([high, low, high], axis=0)


def ortho_body(heads, slots, *refs):
    place = position()
    matrix = lax.rem(place[0] - first_owner(place[1]) + slots, slots)
    owner = (place[1] < heads) & (matrix < 3)

    @pl.when(owner)
    def _():
        orthogonalize(refs[:-1], refs[-1])

    @pl.when(jnp.logical_not(owner))
    def _():
        refs[-1][...] = jnp.zeros(refs[-1].shape, refs[-1].dtype)


def orthogonalize(parts, out):
    grads = parts[0][...].astype(f32)
    for part in parts[1:]:
        grads = grads + part[...].astype(f32)
    eye = (
        lax.broadcasted_iota(jnp.int32, (HD, HD), 0) == lax.broadcasted_iota(jnp.int32, (HD, HD), 1)
    ).astype(f32)
    both = jnp.concatenate(parts_of(grads), axis=1)
    blocks = dot(both, both, (0, 0))
    raw = (blocks[:HD, HD:] + blocks[HD:, :HD]) + blocks[:HD, :HD]
    square = jnp.sum(jnp.sum(raw * eye, axis=0, keepdims=True), axis=1, keepdims=True)
    scale = lax.rsqrt(square + epsilon)
    gram = raw * scale * scale
    total = None
    for step in range(NS_STEPS):
        square_gram = dot(left_of(gram), right_of(gram), (1, 0))
        mix = quintic_a * eye + quintic_b * gram + quintic_c * square_gram
        right = right_of(mix)
        if step < NS_STEPS - 1:
            gram = dot(left_of(dot(left_of(gram), right, (1, 0))), right, (1, 0))
            total = mix if total is None else dot(left_of(total), right, (1, 0))
    ortho = dot(left_of(grads * scale), right_of(total), (1, 0))
    out[...] = dot(left_of(ortho), right, (1, 0)).astype(out.dtype)


def finish_body(slots, group, w_ref, rows_ref, out):
    heads = w_ref.shape[1]
    for m in range(3):
        for h in range(heads):
            weights = w_ref[m, h]
            summed = weights + rows_ref[((m + first_owner(h)) % slots) * group + h].astype(f32)
            old = jnp.sqrt(jnp.sum(weights * weights, axis=1, keepdims=True))
            new = lax.rsqrt(jnp.sum(summed * summed, axis=1, keepdims=True) + epsilon)
            out[m, h] = summed * (old * new)


def attend_body(heads, tokens, q_ref, own_ref, back_ref, out):
    padded = own_ref.shape[0]
    span = heads * HD
    column = lax.broadcasted_iota(jnp.int32, (1, 2 * padded), 1)
    place = position()
    first = (place[0] == 0) & (place[1] == 0)
    stop = jnp.where(first, padded, padded + tokens)
    live = (column < tokens) | ((column >= padded) & (column < stop))
    for h in range(heads):
        cols = slice(h * HD, (h + 1) * HD)
        key = jnp.concatenate([own_ref[:, cols], back_ref[:, cols]], axis=0)
        vcols = slice(span + h * HD, span + (h + 1) * HD)
        value = jnp.concatenate([own_ref[:, vcols], back_ref[:, vcols]], axis=0)
        scores = dot(q_ref[:, cols], key, (1, 1)) * (HD ** (-0.5))
        scores = jnp.where(live, scores, -1e30)
        weights = jnp.exp(scores - jnp.max(scores, axis=1, keepdims=True))
        probs = (weights / jnp.sum(weights, axis=1, keepdims=True)).astype(bf16)
        out[:, cols] = dot(probs, value, (1, 0))


def assemble_body(heads, slots, out, squares):
    for h in range(heads):
        out[:, h * HD : (h + 1) * HD] = slots[h]
    fast = out[...].astype(f32)
    squares[...] = dot(jnp.ones((8, heads * HD), f32), fast * fast, (1, 1), highest)


def block_body(features, gain_ref, attended_ref, fast_ref, *refs):
    squares, out = refs[:-1], refs[-1]
    total = squares[0][...]
    for other in squares[1:]:
        total = total + other[...]
    pick = (lax.broadcasted_iota(jnp.int32, (8, HD), 0) == 0).astype(f32)
    spread = dot(total, pick, (0, 0), highest) * (1.0 / features)
    scale = lax.rsqrt(spread + epsilon)
    for h in range(fast_ref.shape[1] // HD):
        cols = slice(h * HD, (h + 1) * HD)
        out[:, cols] = (
            attended_ref[:, cols] + fast_ref[:, cols].astype(f32) * gain_ref[:, cols] * scale
        ).astype(bf16)


def on_device(queries, keys, values, rates, frame_update, fast_weights, gain):
    tokens = queries.shape[0]
    heads = queries.shape[1] // HD
    rows_local = fast_weights.shape[2]
    nz, group, nh = lax.axis_size("z"), lax.axis_size("grp"), lax.axis_size("head")
    count = nz * group
    hidden = count * rows_local
    padded = -(-tokens // 16) * 16
    span = heads * HD

    def whole(*shape):
        return pl.BlockSpec(shape, lambda i: (0,) * len(shape))

    low_shape = (count, 3, rows_local, HD)
    low = call(
        functools.partial(cast_body, heads, group), sds(low_shape, bf16), flops=1e6
    )(fast_weights)
    prepared = pl.pallas_call(
        functools.partial(prep_body, heads, group, tokens),
        grid=(1,),
        out_shape=[sds((padded, 2 * span), bf16)]
        + [sds((tokens, 3 * HD), bf16)] * group,
        in_specs=[pl.BlockSpec(memory_space=pl.ANY), whole(1, 1)]
        + [whole(heads, -(-padded // 128) * 128)]
        + [whole(padded, span)] * 3,
        out_specs=[whole(padded, 2 * span)] + [whole(tokens, 3 * HD)] * group,
        scratch_shapes=[pltpu.VMEM((padded, span), bf16)],
        compiler_params=pltpu.CompilerParams(vmem_limit_bytes=VMEM_LIMIT),
    )(low, frame_update.reshape(1, 1), rates.T, keys, values, queries)
    kv_own, *token_slots = prepared

    weights = lax.all_to_all(low, ("z", "grp"), 0, 0, tiled=True)
    if rows_local % 16:
        weights = weights.transpose(1, 0, 2, 3).reshape(3, hidden, HD)
    for d in served(group)[1:]:
        pairs = [(s, s ^ d) for s in range(group) if s ^ d < heads]
        token_slots[d] = lax.ppermute(token_slots[d], "grp", pairs)

    last = group // 2
    early_slots = [d for d in served(group) if d != last]
    early_grads, early_fast = call(
        functools.partial(early_body, len(early_slots)),
        [sds((3, hidden, HD), f32), sds((len(early_slots), padded, HD), bf16)],
        scratch=gradient_scratch(len(early_slots), padded, hidden) + apply_scratch(padded, hidden),
        flops=1e9,
    )(*(token_slots[d] for d in early_slots), weights)
    partials = list(
        call(
            functools.partial(late_body, group, nz),
            [sds((hidden, HD), bf16)] * nz,
            scratch=[pltpu.VMEM((3, hidden, HD), bf16)] + gradient_scratch(1, padded, hidden),
            flops=5e8,
        )(token_slots[last], weights, early_grads)
    )
    weights, partials[0] = lax.optimization_barrier((weights, partials[0]))
    for d in summed_order(nz)[1:]:
        pairs = []
        for z in range(nz):
            pairs += [
                (z * group + j, (z ^ d) * group + j)
                for j in range(heads)
                if ((z ^ d) - first_owner(j)) % nz < 3
            ]
        partials[d] = lax.ppermute(partials[d], ("z", "grp"), pairs)

    fast_slots = call(
        functools.partial(late_apply_body, early_slots, last),
        sds((group, padded, HD), bf16),
        scratch=apply_scratch(padded, hidden),
        flops=1e3,
        moved=1024,
    )(token_slots[last], weights, early_fast)
    kv_own, partials[0], fast_slots = lax.optimization_barrier((kv_own, partials[0], fast_slots))
    fast_slots = lax.all_to_all(fast_slots, "grp", 0, 0, tiled=True)

    ring = [(i, i + 1) for i in range(count - 1)]
    kv_back = lax.ppermute(kv_own, ("z", "grp"), ring)

    ortho = call(functools.partial(ortho_body, heads, nz), sds((hidden, HD), bf16), flops=1e9)(
        *(partials[d] for d in summed_order(nz))
    )
    queries, ortho = lax.optimization_barrier((queries, ortho))
    rows = lax.all_to_all(
        ortho.reshape(count, rows_local, HD), ("z", "grp"), 0, 0, tiled=True
    )
    new_weights = call(
        functools.partial(finish_body, nz, group), sds(fast_weights.shape, f32), flops=1e6
    )(fast_weights, rows)

    attended = pl.pallas_call(
        functools.partial(attend_body, heads, tokens),
        grid=(1,),
        out_shape=sds((padded, span), f32),
        in_specs=[whole(padded, span)] + [whole(padded, 2 * span)] * 2,
        out_specs=whole(padded, span),
        compiler_params=pltpu.CompilerParams(vmem_limit_bytes=VMEM_LIMIT),
    )(queries, kv_own, kv_back)
    fast, squares = call(
        functools.partial(assemble_body, heads),
        [sds((padded, span), bf16), sds((8, padded), f32)],
        flops=1e7,
    )(fast_slots)
    all_squares = [squares] + [
        lax.ppermute(squares, "head", [(s, (s + d) % nh) for s in range(nh)]) for d in range(1, nh)
    ]
    block_out = pl.pallas_call(
        functools.partial(block_body, span * nh),
        grid=(1,),
        out_shape=sds((tokens, span), bf16),
        in_specs=[whole(1, span), whole(padded, span), whole(padded, span)]
        + [whole(8, padded)] * nh,
        out_specs=whole(padded, span),
        compiler_params=pltpu.CompilerParams(vmem_limit_bytes=VMEM_LIMIT),
    )(gain.reshape(1, span), attended, fast, *all_squares)
    return (block_out, new_weights)


def solution(mesh):
    group = 4
    nh = mesh.shape["head"]
    inner = Mesh(
        np.asarray(mesh.devices).reshape(mesh.shape["ctx"] // group, group, nh),
        ("z", "grp", "head"),
    )
    ctx = ("z", "grp")
    placed = (
        P(ctx, "head"),
        P(ctx, "head"),
        P(ctx, "head"),
        P(ctx, "head"),
        P(ctx),
        P(None, "head", ctx, None),
        P("head"),
    )
    return jax.shard_map(
        on_device,
        mesh=inner,
        in_specs=placed,
        out_specs=(P(ctx, "head"), P(None, "head", ctx, None)),
        check_vma=False,
    )
```

```python
import functools

import jax
import jax.numpy as jnp
import numpy as np
from jax import lax
from jax.experimental import pallas as pl
from jax.experimental.pallas import tpu as pltpu
from jax.sharding import Mesh, PartitionSpec as P

HD = 128
NS_STEPS = 5

epsilon = 1e-06
quintic_a = 3.4445
quintic_b = -4.775
quintic_c = 2.0315
highest = lax.Precision.HIGHEST
f32 = jnp.float32
bf16 = jnp.bfloat16
VMEM_LIMIT = 24 * 1024 * 1024


def dot(a, b, contract, precision=None):
    return lax.dot_general(
        a, b, ((contract[:1], contract[1:]), ((), ())),
        precision=precision, preferred_element_type=f32,
    )


def call(body, outs, scratch=(), in_specs=None, flops=1e8, moved=1 << 20, **kw):
    given = {} if in_specs is None else {"in_specs": in_specs}
    return pl.pallas_call(
        body,
        out_shape=outs,
        **given,
        scratch_shapes=list(scratch),
        compiler_params=pltpu.CompilerParams(vmem_limit_bytes=VMEM_LIMIT),
        cost_estimate=pl.CostEstimate(flops=int(flops), bytes_accessed=moved, transcendentals=0),
        **kw,
    )


def sds(shape, dtype):
    return jax.ShapeDtypeStruct(shape, dtype)


def served(n):
    return [0] + list(range(n - 1, 0, -1))


def first_owner(h):
    return h & 1


def position():
    return lax.axis_index("z"), lax.axis_index("grp")


def sigmoid(x):
    return 0.5 * jnp.tanh(0.5 * x) + 0.5


def cast_body(heads, group, w_ref, w_out):
    slots = w_out.shape[0] // group
    for j in range(group):
        for m in range(3):
            low = w_ref[m, min(j, heads - 1)].astype(bf16)
            for z in range(slots):
                w_out[z * group + j, m] = low


def prep_body(
    heads, group, tokens, after, update, rate_ref, k_ref, v_ref, q_ref, kv_out, *outs
):
    token_outs, targets = outs[:-1], outs[-1]
    padded = kv_out.shape[0]
    place = position()
    valid = lax.broadcasted_iota(jnp.int32, (padded, 1), 0) < tokens
    none = jnp.zeros((), bf16)
    keep = update[...].astype(f32)
    lane_head = lax.broadcasted_iota(jnp.int32, (heads, heads * HD), 1) // HD
    row = lax.broadcasted_iota(jnp.int32, (heads, heads * HD), 0)
    rate = dot(rate_ref[...], (row == lane_head).astype(f32), (0, 0), highest)[:padded]
    targets[...] = ((rate * keep) * v_ref[...].astype(f32)).astype(bf16)
    for d in range(group):
        head = jnp.minimum(place[1] ^ d, heads - 1)
        cols = pl.ds(pl.multiple_of(head * HD, HD), HD)
        for i, source in enumerate((k_ref, targets, q_ref)):
            token_outs[d][:, i * HD : (i + 1) * HD] = source[:tokens, cols]
    kv_out[:, : heads * HD] = jnp.where(valid, k_ref[...], none)
    kv_out[:, heads * HD :] = jnp.where(valid, v_ref[...], none)


def gradients(token_refs, w_ref, k_all, t_all, staged, deltas):
    tokens = token_refs[0].shape[0]
    padded = -(-tokens // 16) * 16
    width = k_all.shape[0]
    filled = len(token_refs) * padded
    for i, ref in enumerate(token_refs):
        for part, rows in enumerate((k_all, t_all)):
            rows[(i + 1) * padded - 16 : (i + 1) * padded] = jnp.zeros((16, HD), bf16)
            rows[i * padded : i * padded + tokens] = ref[:, part * HD : (part + 1) * HD]
    if width > filled:
        k_all[filled:] = jnp.zeros((width - filled, HD), bf16)
        t_all[filled:] = jnp.zeros((width - filled, HD), bf16)
    hidden = deltas.shape[1]
    w1, w3, w2 = (weight_rows(w_ref, m, 0, hidden) for m in range(3))
    tall = 64
    for left in range(0, width, staged.shape[3]):
        right = min(left + staged.shape[3], width)
        cols, used = slice(left, right), slice(0, right - left)
        stage = staged.at[(left // staged.shape[3]) % staged.shape[0]]
        stage[0, :, used] = dot(w1, k_all[cols], (1, 1))
        stage[1, :, used] = dot(w3, k_all[cols], (1, 1))
        stage[2, :, used] = dot(w2, t_all[cols], (1, 1))
        for start in range(0, hidden, tall):
            rows = slice(start, start + tall)
            pre_one, pre_three, back = (stage[i, rows, used] for i in range(3))
            sig = sigmoid(pre_one)
            gate = pre_one * sig
            deltas[2, rows, cols] = (gate * pre_three).astype(bf16)
            deltas[1, rows, cols] = (back * gate).astype(bf16)
            deltas[0, rows, cols] = (
                (back * pre_three) * (sig * (1.0 + pre_one * (1.0 - sig)))
            ).astype(bf16)
    return (
        dot(deltas[0], k_all[...], (1, 0)),
        dot(deltas[1], k_all[...], (1, 0)),
        dot(deltas[2], t_all[...], (1, 0)),
    )


def gradient_scratch(slots, padded, hidden):
    width = -(-slots * padded // 128) * 128
    return [
        pltpu.VMEM((width, HD), bf16),
        pltpu.VMEM((width, HD), bf16),
        pltpu.VMEM((2, 3, hidden, 256), f32),
        pltpu.VMEM((3, hidden, width), bf16),
    ]


def apply_tokens(token_ref, w_ref, stage, act, held):
    hidden = act.shape[1]
    tall = 16
    w1, w3, w2 = (weight_rows(w_ref, m, 0, hidden) for m in range(3))
    held[held.shape[0] - 16 :] = jnp.zeros((16, HD), bf16)
    held[: token_ref.shape[0]] = token_ref[:, 2 * HD :]
    query = held[...]
    stage[0] = dot(query, w1, (1, 1))
    stage[1] = dot(query, w3, (1, 1))
    for start in range(0, query.shape[0], tall):
        rows = slice(start, start + tall)
        proj = stage[0, rows]
        act[rows] = (proj * sigmoid(proj) * stage[1, rows]).astype(bf16)
    return dot(act[...], w2, (1, 0)).astype(bf16)


def apply_scratch(padded, hidden):
    return [
        pltpu.VMEM((2, 2, padded, hidden), f32),
        pltpu.VMEM((2, padded, hidden), bf16),
        pltpu.VMEM((2, padded, HD), bf16),
    ]


def early_body(count, *refs):
    token_refs, w_ref = refs[:count], refs[count]
    grads, fast = refs[count + 1 : count + 3]
    scratch, (staged, acts, held) = refs[count + 3 : -3], refs[-3:]
    for m, grad in enumerate(gradients(token_refs, w_ref, *scratch)):
        grads[m] = grad
    for i, ref in enumerate(token_refs):
        fast[i] = apply_tokens(ref, w_ref, *(buffer.at[i % 2] for buffer in (staged, acts, held)))


def late_body(group, slots, token_ref, w_ref, early, *refs):
    place = position()
    outs, sums, scratch = refs[:slots], refs[slots], refs[slots + 1 :]
    for m, grad in enumerate(gradients([token_ref], w_ref, *scratch)):
        sums[m] = (early[m] + grad).astype(bf16)
    for d in range(slots):
        matrix = lax.rem((place[0] ^ d) - first_owner(place[1]) + slots, slots)
        chosen = sums[jnp.minimum(matrix, 2)]
        outs[d][...] = jnp.where(matrix < 3, chosen, jnp.zeros_like(chosen))


def late_apply_body(early_slots, last, token_ref, w_ref, early, out, staged, acts, held):
    place = position()
    for i, d in enumerate(early_slots):
        out[place[1] ^ d] = early[i]
    out[place[1] ^ last] = apply_tokens(
        token_ref, w_ref, staged.at[0], acts.at[0], held.at[0]
    )


def weight_rows(w_ref, m, start, block):
    if len(w_ref.shape) == 3:
        return w_ref[m, start : start + block]
    rows = w_ref.shape[2]
    return w_ref[start // rows : (start + block) // rows, m].reshape(block, HD)


def parts_of(x):
    high = x.astype(bf16)
    return high, (x - high.astype(f32)).astype(bf16)


def left_of(x):
    high, low = parts_of(x)
    return jnp.concatenate([high, high, low], axis=1)


def right_of(x):
    high, low = parts_of(x)
    return jnp.concatenate([high, low, high], axis=0)


def ortho_body(heads, slots, *refs):
    place = position()
    matrix = lax.rem(place[0] - first_owner(place[1]) + slots, slots)
    owner = (place[1] < heads) & (matrix < 3)

    @pl.when(owner)
    def _():
        orthogonalize(refs[:-1], refs[-1])

    @pl.when(jnp.logical_not(owner))
    def _():
        refs[-1][...] = jnp.zeros(refs[-1].shape, refs[-1].dtype)


def orthogonalize(parts, out):
    grads = parts[0][...].astype(f32)
    for part in parts[1:]:
        grads = grads + part[...].astype(f32)
    eye = (
        lax.broadcasted_iota(jnp.int32, (HD, HD), 0) == lax.broadcasted_iota(jnp.int32, (HD, HD), 1)
    ).astype(f32)
    both = jnp.concatenate(parts_of(grads), axis=1)
    blocks = dot(both, both, (0, 0))
    raw = (blocks[:HD, HD:] + blocks[HD:, :HD]) + blocks[:HD, :HD]
    square = jnp.sum(jnp.sum(raw * eye, axis=0, keepdims=True), axis=1, keepdims=True)
    scale = lax.rsqrt(square + epsilon)
    gram = raw * scale * scale
    total = None
    for step in range(NS_STEPS):
        square_gram = dot(left_of(gram), right_of(gram), (1, 0))
        mix = quintic_a * eye + quintic_b * gram + quintic_c * square_gram
        right = right_of(mix)
        if step < NS_STEPS - 1:
            gram = dot(left_of(dot(left_of(gram), right, (1, 0))), right, (1, 0))
            total = mix if total is None else dot(left_of(total), right, (1, 0))
    ortho = dot(left_of(grads * scale), right_of(total), (1, 0))
    out[...] = dot(left_of(ortho), right, (1, 0)).astype(out.dtype)


def finish_body(slots, group, w_ref, rows_ref, out):
    heads = w_ref.shape[1]
    for m in range(3):
        for h in range(heads):
            weights = w_ref[m, h]
            summed = weights + rows_ref[((m + first_owner(h)) % slots) * group + h].astype(f32)
            old = jnp.sqrt(jnp.sum(weights * weights, axis=1, keepdims=True))
            new = lax.rsqrt(jnp.sum(summed * summed, axis=1, keepdims=True) + epsilon)
            out[m, h] = summed * (old * new)


def attend_body(heads, tokens, q_ref, own_ref, inside_ref, behind_ref, out):
    padded = own_ref.shape[0]
    span = heads * HD
    column = lax.broadcasted_iota(jnp.int32, (1, 2 * padded), 1)
    place = position()
    first = (place[0] == 0) & (place[1] == 0)
    stop = jnp.where(first, padded, padded + tokens)
    live = (column < tokens) | ((column >= padded) & (column < stop))

    def back(cols):
        return inside_ref[:, cols] + behind_ref[:, cols]

    for h in range(heads):
        cols = slice(h * HD, (h + 1) * HD)
        key = jnp.concatenate([own_ref[:, cols], back(cols)], axis=0)
        vcols = slice(span + h * HD, span + (h + 1) * HD)
        value = jnp.concatenate([own_ref[:, vcols], back(vcols)], axis=0)
        scores = dot(q_ref[:, cols], key, (1, 1)) * (HD ** (-0.5))
        scores = jnp.where(live, scores, -1e30)
        weights = jnp.exp(scores - jnp.max(scores, axis=1, keepdims=True))
        probs = (weights / jnp.sum(weights, axis=1, keepdims=True)).astype(bf16)
        out[:, cols] = dot(probs, value, (1, 0))


def assemble_body(heads, slots, out, squares):
    for h in range(heads):
        out[:, h * HD : (h + 1) * HD] = slots[h]
    fast = out[...].astype(f32)
    squares[...] = dot(jnp.ones((8, heads * HD), f32), fast * fast, (1, 1), highest)


def block_body(features, gain_ref, attended_ref, fast_ref, *refs):
    squares, out = refs[:-1], refs[-1]
    total = squares[0][...]
    for other in squares[1:]:
        total = total + other[...]
    pick = (lax.broadcasted_iota(jnp.int32, (8, HD), 0) == 0).astype(f32)
    spread = dot(total, pick, (0, 0), highest) * (1.0 / features)
    scale = lax.rsqrt(spread + epsilon)
    for h in range(fast_ref.shape[1] // HD):
        cols = slice(h * HD, (h + 1) * HD)
        out[:, cols] = (
            attended_ref[:, cols] + fast_ref[:, cols].astype(f32) * gain_ref[:, cols] * scale
        ).astype(bf16)


def on_device(queries, keys, values, rates, frame_update, fast_weights, gain):
    tokens = queries.shape[0]
    heads = queries.shape[1] // HD
    rows_local = fast_weights.shape[2]
    nz, group, nh = lax.axis_size("z"), lax.axis_size("grp"), lax.axis_size("head")
    count = nz * group
    hidden = count * rows_local
    padded = -(-tokens // 16) * 16
    span = heads * HD

    def whole(*shape):
        return pl.BlockSpec(shape, lambda i: (0,) * len(shape))

    low_shape = (count, 3, rows_local, HD)
    low = call(
        functools.partial(cast_body, heads, group), sds(low_shape, bf16), flops=1e6
    )(fast_weights)
    prepared = pl.pallas_call(
        functools.partial(prep_body, heads, group, tokens),
        grid=(1,),
        out_shape=[sds((padded, 2 * span), bf16)]
        + [sds((tokens, 3 * HD), bf16)] * group,
        in_specs=[pl.BlockSpec(memory_space=pl.ANY), whole(1, 1)]
        + [whole(heads, -(-padded // 128) * 128)]
        + [whole(padded, span)] * 3,
        out_specs=[whole(padded, 2 * span)] + [whole(tokens, 3 * HD)] * group,
        scratch_shapes=[pltpu.VMEM((padded, span), bf16)],
        compiler_params=pltpu.CompilerParams(vmem_limit_bytes=VMEM_LIMIT),
    )(low, frame_update.reshape(1, 1), rates.T, keys, values, queries)
    kv_own, *token_slots = prepared

    weights = lax.all_to_all(low, ("z", "grp"), 0, 0, tiled=True)
    if rows_local % 16:
        weights = weights.transpose(1, 0, 2, 3).reshape(3, hidden, HD)
    for d in served(group)[1:]:
        pairs = [(s, s ^ d) for s in range(group) if s ^ d < heads]
        token_slots[d] = lax.ppermute(token_slots[d], "grp", pairs)

    inside = lax.ppermute(kv_own, "grp", [(j, j + 1) for j in range(group - 1)])

    last = group // 2
    early_slots = [d for d in served(group) if d != last]
    early_grads, early_fast = call(
        functools.partial(early_body, len(early_slots)),
        [sds((3, hidden, HD), f32), sds((len(early_slots), padded, HD), bf16)],
        scratch=gradient_scratch(len(early_slots), padded, hidden) + apply_scratch(padded, hidden),
        flops=1e9,
    )(*(token_slots[d] for d in early_slots), weights)
    partials = list(
        call(
            functools.partial(late_body, group, nz),
            [sds((hidden, HD), bf16)] * nz,
            scratch=[pltpu.VMEM((3, hidden, HD), bf16)] + gradient_scratch(1, padded, hidden),
            flops=5e8,
        )(token_slots[last], weights, early_grads)
    )
    weights, inside, partials[0] = lax.optimization_barrier((weights, inside, partials[0]))
    for d in served(nz)[1:]:
        pairs = []
        for z in range(nz):
            pairs += [
                (z * group + j, (z ^ d) * group + j)
                for j in range(heads)
                if ((z ^ d) - first_owner(j)) % nz < 3
            ]
        partials[d] = lax.ppermute(partials[d], ("z", "grp"), pairs)

    fast_slots = call(
        functools.partial(late_apply_body, early_slots, last),
        sds((group, padded, HD), bf16),
        scratch=apply_scratch(padded, hidden),
        flops=1e3,
        moved=1024,
    )(token_slots[last], weights, early_fast)
    kv_own, partials[0], fast_slots = lax.optimization_barrier((kv_own, partials[0], fast_slots))
    fast_slots = lax.all_to_all(fast_slots, "grp", 0, 0, tiled=True)

    behind = lax.ppermute(
        kv_own, ("z", "grp"), [((z + 1) * group - 1, (z + 1) * group) for z in range(nz - 1)]
    )

    ortho = call(functools.partial(ortho_body, heads, nz), sds((hidden, HD), bf16), flops=1e9)(
        *(partials[d] for d in served(nz))
    )
    queries, ortho = lax.optimization_barrier((queries, ortho))
    rows = lax.all_to_all(
        ortho.reshape(count, rows_local, HD), ("z", "grp"), 0, 0, tiled=True
    )
    new_weights = call(
        functools.partial(finish_body, nz, group), sds(fast_weights.shape, f32), flops=1e6
    )(fast_weights, rows)

    attended = pl.pallas_call(
        functools.partial(attend_body, heads, tokens),
        grid=(1,),
        out_shape=sds((padded, span), f32),
        in_specs=[whole(padded, span)] + [whole(padded, 2 * span)] * 3,
        out_specs=whole(padded, span),
        compiler_params=pltpu.CompilerParams(vmem_limit_bytes=VMEM_LIMIT),
    )(queries, kv_own, inside, behind)
    fast, squares = call(
        functools.partial(assemble_body, heads),
        [sds((padded, span), bf16), sds((8, padded), f32)],
        flops=1e7,
    )(fast_slots)
    all_squares = [squares] + [
        lax.ppermute(squares, "head", [(s, (s + d) % nh) for s in range(nh)]) for d in range(1, nh)
    ]
    block_out = pl.pallas_call(
        functools.partial(block_body, span * nh),
        grid=(1,),
        out_shape=sds((tokens, span), bf16),
        in_specs=[whole(1, span), whole(padded, span), whole(padded, span)]
        + [whole(8, padded)] * nh,
        out_specs=whole(padded, span),
        compiler_params=pltpu.CompilerParams(vmem_limit_bytes=VMEM_LIMIT),
    )(gain.reshape(1, span), attended, fast, *all_squares)
    return (block_out, new_weights)


def solution(mesh):
    group = 4
    nh = mesh.shape["head"]
    inner = Mesh(
        np.asarray(mesh.devices).reshape(mesh.shape["ctx"] // group, group, nh),
        ("z", "grp", "head"),
    )
    ctx = ("z", "grp")
    placed = (
        P(ctx, "head"),
        P(ctx, "head"),
        P(ctx, "head"),
        P(ctx, "head"),
        P(ctx),
        P(None, "head", ctx, None),
        P("head"),
    )
    return jax.shard_map(
        on_device,
        mesh=inner,
        in_specs=placed,
        out_specs=(P(ctx, "head"), P(None, "head", ctx, None)),
        check_vma=False,
    )
```

```python
import functools

import jax
import jax.numpy as jnp
import numpy as np
from jax import lax
from jax.experimental import pallas as pl
from jax.experimental.pallas import tpu as pltpu
from jax.sharding import Mesh, PartitionSpec as P

HD = 128
NS_STEPS = 5

epsilon = 1e-06
quintic_a = 3.4445
quintic_b = -4.775
quintic_c = 2.0315
highest = lax.Precision.HIGHEST
f32 = jnp.float32
bf16 = jnp.bfloat16
VMEM_LIMIT = 24 * 1024 * 1024


def dot(a, b, contract, precision=None):
    return lax.dot_general(
        a, b, ((contract[:1], contract[1:]), ((), ())),
        precision=precision, preferred_element_type=f32,
    )


def call(body, outs, scratch=(), in_specs=None, flops=1e8, moved=1 << 20, **kw):
    given = {} if in_specs is None else {"in_specs": in_specs}
    return pl.pallas_call(
        body,
        out_shape=outs,
        **given,
        scratch_shapes=list(scratch),
        compiler_params=pltpu.CompilerParams(vmem_limit_bytes=VMEM_LIMIT),
        cost_estimate=pl.CostEstimate(flops=int(flops), bytes_accessed=moved, transcendentals=0),
        **kw,
    )


def sds(shape, dtype):
    return jax.ShapeDtypeStruct(shape, dtype)


def served(n):
    return [0] + list(range(n - 1, 0, -1))


def first_owner(h):
    return h & 1


def position():
    return lax.axis_index("z"), lax.axis_index("grp")


def sigmoid(x):
    return 0.5 * jnp.tanh(0.5 * x) + 0.5


def cast_body(heads, group, w_ref, w_out):
    slots = w_out.shape[0] // group
    for j in range(group):
        for m in range(3):
            low = w_ref[m, min(j, heads - 1)].astype(bf16)
            for z in range(slots):
                w_out[j * slots + z, m] = low


def prep_body(
    heads, group, tokens, after, update, rate_ref, k_ref, v_ref, q_ref, kv_out, *outs
):
    token_outs, targets = outs[:-1], outs[-1]
    padded = kv_out.shape[0]
    place = position()
    valid = lax.broadcasted_iota(jnp.int32, (padded, 1), 0) < tokens
    none = jnp.zeros((), bf16)
    keep = update[...].astype(f32)
    lane_head = lax.broadcasted_iota(jnp.int32, (heads, heads * HD), 1) // HD
    row = lax.broadcasted_iota(jnp.int32, (heads, heads * HD), 0)
    rate = dot(rate_ref[...], (row == lane_head).astype(f32), (0, 0), highest)[:padded]
    targets[...] = ((rate * keep) * v_ref[...].astype(f32)).astype(bf16)
    for d in range(group):
        head = jnp.minimum(place[1] ^ d, heads - 1)
        cols = pl.ds(pl.multiple_of(head * HD, HD), HD)
        for i, source in enumerate((k_ref, targets, q_ref)):
            token_outs[d][:, i * HD : (i + 1) * HD] = source[:tokens, cols]
    kv_out[:, : heads * HD] = jnp.where(valid, k_ref[...], none)
    kv_out[:, heads * HD :] = jnp.where(valid, v_ref[...], none)


def gradients(token_refs, w_ref, k_all, t_all, staged, deltas):
    tokens = token_refs[0].shape[0]
    padded = -(-tokens // 16) * 16
    width = k_all.shape[0]
    filled = len(token_refs) * padded
    for i, ref in enumerate(token_refs):
        for part, rows in enumerate((k_all, t_all)):
            rows[(i + 1) * padded - 16 : (i + 1) * padded] = jnp.zeros((16, HD), bf16)
            rows[i * padded : i * padded + tokens] = ref[:, part * HD : (part + 1) * HD]
    if width > filled:
        k_all[filled:] = jnp.zeros((width - filled, HD), bf16)
        t_all[filled:] = jnp.zeros((width - filled, HD), bf16)
    hidden = deltas.shape[1]
    w1, w3, w2 = (weight_rows(w_ref, m, 0, hidden) for m in range(3))
    tall = 64
    for left in range(0, width, staged.shape[3]):
        right = min(left + staged.shape[3], width)
        cols, used = slice(left, right), slice(0, right - left)
        stage = staged.at[(left // staged.shape[3]) % staged.shape[0]]
        stage[0, :, used] = dot(w1, k_all[cols], (1, 1))
        stage[1, :, used] = dot(w3, k_all[cols], (1, 1))
        stage[2, :, used] = dot(w2, t_all[cols], (1, 1))
        for start in range(0, hidden, tall):
            rows = slice(start, start + tall)
            pre_one, pre_three, back = (stage[i, rows, used] for i in range(3))
            sig = sigmoid(pre_one)
            gate = pre_one * sig
            deltas[2, rows, cols] = (gate * pre_three).astype(bf16)
            deltas[1, rows, cols] = (back * gate).astype(bf16)
            deltas[0, rows, cols] = (
                (back * pre_three) * (sig * (1.0 + pre_one * (1.0 - sig)))
            ).astype(bf16)
    return (
        dot(deltas[0], k_all[...], (1, 0)),
        dot(deltas[1], k_all[...], (1, 0)),
        dot(deltas[2], t_all[...], (1, 0)),
    )


def gradient_scratch(slots, padded, hidden):
    width = -(-slots * padded // 128) * 128
    return [
        pltpu.VMEM((width, HD), bf16),
        pltpu.VMEM((width, HD), bf16),
        pltpu.VMEM((2, 3, hidden, 256), f32),
        pltpu.VMEM((3, hidden, width), bf16),
    ]


def apply_tokens(token_ref, w_ref, stage, act, held):
    hidden = act.shape[1]
    tall = 16
    w1, w3, w2 = (weight_rows(w_ref, m, 0, hidden) for m in range(3))
    held[held.shape[0] - 16 :] = jnp.zeros((16, HD), bf16)
    held[: token_ref.shape[0]] = token_ref[:, 2 * HD :]
    query = held[...]
    stage[0] = dot(query, w1, (1, 1))
    stage[1] = dot(query, w3, (1, 1))
    for start in range(0, query.shape[0], tall):
        rows = slice(start, start + tall)
        proj = stage[0, rows]
        act[rows] = (proj * sigmoid(proj) * stage[1, rows]).astype(bf16)
    return dot(act[...], w2, (1, 0)).astype(bf16)


def apply_scratch(padded, hidden):
    return [
        pltpu.VMEM((2, 2, padded, hidden), f32),
        pltpu.VMEM((2, padded, hidden), bf16),
        pltpu.VMEM((2, padded, HD), bf16),
    ]


def early_body(count, *refs):
    token_refs, w_ref = refs[:count], refs[count]
    grads, fast = refs[count + 1 : count + 3]
    scratch, (staged, acts, held) = refs[count + 3 : -3], refs[-3:]
    for m, grad in enumerate(gradients(token_refs, w_ref, *scratch)):
        grads[m] = grad
    for i, ref in enumerate(token_refs):
        fast[i] = apply_tokens(ref, w_ref, *(buffer.at[i % 2] for buffer in (staged, acts, held)))


def late_body(group, slots, token_ref, w_ref, early, *refs):
    place = position()
    outs, sums, scratch = refs[:slots], refs[slots], refs[slots + 1 :]
    for m, grad in enumerate(gradients([token_ref], w_ref, *scratch)):
        sums[m] = (early[m] + grad).astype(bf16)
    for d in range(slots):
        matrix = lax.rem((place[0] ^ d) - first_owner(place[1]) + slots, slots)
        chosen = sums[jnp.minimum(matrix, 2)]
        outs[d][...] = jnp.where(matrix < 3, chosen, jnp.zeros_like(chosen))


def late_apply_body(early_slots, last, token_ref, w_ref, early, out, staged, acts, held):
    place = position()
    for i, d in enumerate(early_slots):
        out[place[1] ^ d] = early[i]
    out[place[1] ^ last] = apply_tokens(
        token_ref, w_ref, staged.at[0], acts.at[0], held.at[0]
    )


def weight_rows(w_ref, m, start, block):
    if len(w_ref.shape) == 3:
        return w_ref[m, start : start + block]
    rows = w_ref.shape[2]
    return w_ref[start // rows : (start + block) // rows, m].reshape(block, HD)


def parts_of(x):
    high = x.astype(bf16)
    return high, (x - high.astype(f32)).astype(bf16)


def left_of(x):
    high, low = parts_of(x)
    return jnp.concatenate([high, high, low], axis=1)


def right_of(x):
    high, low = parts_of(x)
    return jnp.concatenate([high, low, high], axis=0)


def ortho_body(heads, slots, *refs):
    place = position()
    matrix = lax.rem(place[0] - first_owner(place[1]) + slots, slots)
    owner = (place[1] < heads) & (matrix < 3)

    @pl.when(owner)
    def _():
        orthogonalize(refs[:-1], refs[-1])

    @pl.when(jnp.logical_not(owner))
    def _():
        refs[-1][...] = jnp.zeros(refs[-1].shape, refs[-1].dtype)


def orthogonalize(parts, out):
    grads = parts[0][...].astype(f32)
    for part in parts[1:]:
        grads = grads + part[...].astype(f32)
    eye = (
        lax.broadcasted_iota(jnp.int32, (HD, HD), 0) == lax.broadcasted_iota(jnp.int32, (HD, HD), 1)
    ).astype(f32)
    both = jnp.concatenate(parts_of(grads), axis=1)
    blocks = dot(both, both, (0, 0))
    raw = (blocks[:HD, HD:] + blocks[HD:, :HD]) + blocks[:HD, :HD]
    square = jnp.sum(jnp.sum(raw * eye, axis=0, keepdims=True), axis=1, keepdims=True)
    scale = lax.rsqrt(square + epsilon)
    gram = raw * scale * scale
    total = None
    for step in range(NS_STEPS):
        square_gram = dot(left_of(gram), right_of(gram), (1, 0))
        mix = quintic_a * eye + quintic_b * gram + quintic_c * square_gram
        right = right_of(mix)
        if step < NS_STEPS - 1:
            gram = dot(left_of(dot(left_of(gram), right, (1, 0))), right, (1, 0))
            total = mix if total is None else dot(left_of(total), right, (1, 0))
    ortho = dot(left_of(grads * scale), right_of(total), (1, 0))
    out[...] = dot(left_of(ortho), right, (1, 0)).astype(out.dtype)


def finish_body(slots, group, w_ref, rows_ref, out):
    heads = w_ref.shape[1]
    for m in range(3):
        for h in range(heads):
            weights = w_ref[m, h]
            summed = weights + rows_ref[h * slots + (m + first_owner(h)) % slots].astype(f32)
            old = jnp.sqrt(jnp.sum(weights * weights, axis=1, keepdims=True))
            new = lax.rsqrt(jnp.sum(summed * summed, axis=1, keepdims=True) + epsilon)
            out[m, h] = summed * (old * new)


def attend_body(heads, tokens, q_ref, own_ref, back_ref, out):
    padded = own_ref.shape[0]
    span = heads * HD
    column = lax.broadcasted_iota(jnp.int32, (1, 2 * padded), 1)
    place = position()
    first = (place[0] == 0) & (place[1] == 0)
    stop = jnp.where(first, padded, padded + tokens)
    live = (column < tokens) | ((column >= padded) & (column < stop))
    for h in range(heads):
        cols = slice(h * HD, (h + 1) * HD)
        key = jnp.concatenate([own_ref[:, cols], back_ref[:, cols]], axis=0)
        vcols = slice(span + h * HD, span + (h + 1) * HD)
        value = jnp.concatenate([own_ref[:, vcols], back_ref[:, vcols]], axis=0)
        scores = dot(q_ref[:, cols], key, (1, 1)) * (HD ** (-0.5))
        scores = jnp.where(live, scores, -1e30)
        weights = jnp.exp(scores - jnp.max(scores, axis=1, keepdims=True))
        probs = (weights / jnp.sum(weights, axis=1, keepdims=True)).astype(bf16)
        out[:, cols] = dot(probs, value, (1, 0))


def assemble_body(heads, slots, out, squares):
    for h in range(heads):
        out[:, h * HD : (h + 1) * HD] = slots[h]
    fast = out[...].astype(f32)
    squares[...] = dot(jnp.ones((8, heads * HD), f32), fast * fast, (1, 1), highest)


def block_body(features, gain_ref, attended_ref, fast_ref, *refs):
    squares, out = refs[:-1], refs[-1]
    total = squares[0][...]
    for other in squares[1:]:
        total = total + other[...]
    pick = (lax.broadcasted_iota(jnp.int32, (8, HD), 0) == 0).astype(f32)
    spread = dot(total, pick, (0, 0), highest) * (1.0 / features)
    scale = lax.rsqrt(spread + epsilon)
    for h in range(fast_ref.shape[1] // HD):
        cols = slice(h * HD, (h + 1) * HD)
        out[:, cols] = (
            attended_ref[:, cols] + fast_ref[:, cols].astype(f32) * gain_ref[:, cols] * scale
        ).astype(bf16)


def on_device(queries, keys, values, rates, frame_update, fast_weights, gain):
    tokens = queries.shape[0]
    heads = queries.shape[1] // HD
    rows_local = fast_weights.shape[2]
    nz, group, nh = lax.axis_size("z"), lax.axis_size("grp"), lax.axis_size("head")
    count = nz * group
    hidden = count * rows_local
    padded = -(-tokens // 16) * 16
    span = heads * HD

    def whole(*shape):
        return pl.BlockSpec(shape, lambda i: (0,) * len(shape))

    low_shape = (count, 3, rows_local, HD)
    low = call(
        functools.partial(cast_body, heads, group), sds(low_shape, bf16), flops=1e6
    )(fast_weights)
    prepared = pl.pallas_call(
        functools.partial(prep_body, heads, group, tokens),
        grid=(1,),
        out_shape=[sds((padded, 2 * span), bf16)]
        + [sds((tokens, 3 * HD), bf16)] * group,
        in_specs=[pl.BlockSpec(memory_space=pl.ANY), whole(1, 1)]
        + [whole(heads, -(-padded // 128) * 128)]
        + [whole(padded, span)] * 3,
        out_specs=[whole(padded, 2 * span)] + [whole(tokens, 3 * HD)] * group,
        scratch_shapes=[pltpu.VMEM((padded, span), bf16)],
        compiler_params=pltpu.CompilerParams(vmem_limit_bytes=VMEM_LIMIT),
    )(low, frame_update.reshape(1, 1), rates.T, keys, values, queries)
    kv_own, *token_slots = prepared

    weights = lax.all_to_all(low, ("grp", "z"), 0, 0, tiled=True)
    if rows_local % 16:
        weights = weights.transpose(1, 0, 2, 3).reshape(3, hidden, HD)
    for d in served(group)[1:]:
        pairs = [(s, s ^ d) for s in range(group) if s ^ d < heads]
        token_slots[d] = lax.ppermute(token_slots[d], "grp", pairs)

    last = group // 2
    early_slots = [d for d in served(group) if d != last]
    early_grads, early_fast = call(
        functools.partial(early_body, len(early_slots)),
        [sds((3, hidden, HD), f32), sds((len(early_slots), padded, HD), bf16)],
        scratch=gradient_scratch(len(early_slots), padded, hidden) + apply_scratch(padded, hidden),
        flops=1e9,
    )(*(token_slots[d] for d in early_slots), weights)
    partials = list(
        call(
            functools.partial(late_body, group, nz),
            [sds((hidden, HD), bf16)] * nz,
            scratch=[pltpu.VMEM((3, hidden, HD), bf16)] + gradient_scratch(1, padded, hidden),
            flops=5e8,
        )(token_slots[last], weights, early_grads)
    )
    weights, partials[0] = lax.optimization_barrier((weights, partials[0]))
    for d in served(nz)[1:]:
        pairs = []
        for z in range(nz):
            pairs += [
                (z * group + j, (z ^ d) * group + j)
                for j in range(heads)
                if ((z ^ d) - first_owner(j)) % nz < 3
            ]
        partials[d] = lax.ppermute(partials[d], ("z", "grp"), pairs)

    fast_slots = call(
        functools.partial(late_apply_body, early_slots, last),
        sds((group, padded, HD), bf16),
        scratch=apply_scratch(padded, hidden),
        flops=1e3,
        moved=1024,
    )(token_slots[last], weights, early_fast)
    kv_own, partials[0], fast_slots = lax.optimization_barrier((kv_own, partials[0], fast_slots))
    fast_slots = lax.all_to_all(fast_slots, "grp", 0, 0, tiled=True)

    ring = [(i, i + 1) for i in range(count - 1)]
    kv_back = lax.ppermute(kv_own, ("z", "grp"), ring)

    ortho = call(functools.partial(ortho_body, heads, nz), sds((hidden, HD), bf16), flops=1e9)(
        *(partials[d] for d in served(nz))
    )
    queries, ortho = lax.optimization_barrier((queries, ortho))
    rows = lax.all_to_all(
        ortho.reshape(count, rows_local, HD), ("grp", "z"), 0, 0, tiled=True
    )
    new_weights = call(
        functools.partial(finish_body, nz, group), sds(fast_weights.shape, f32), flops=1e6
    )(fast_weights, rows)

    attended = pl.pallas_call(
        functools.partial(attend_body, heads, tokens),
        grid=(1,),
        out_shape=sds((padded, span), f32),
        in_specs=[whole(padded, span)] + [whole(padded, 2 * span)] * 2,
        out_specs=whole(padded, span),
        compiler_params=pltpu.CompilerParams(vmem_limit_bytes=VMEM_LIMIT),
    )(queries, kv_own, kv_back)
    fast, squares = call(
        functools.partial(assemble_body, heads),
        [sds((padded, span), bf16), sds((8, padded), f32)],
        flops=1e7,
    )(fast_slots)
    all_squares = [squares] + [
        lax.ppermute(squares, "head", [(s, (s + d) % nh) for s in range(nh)]) for d in range(1, nh)
    ]
    block_out = pl.pallas_call(
        functools.partial(block_body, span * nh),
        grid=(1,),
        out_shape=sds((tokens, span), bf16),
        in_specs=[whole(1, span), whole(padded, span), whole(padded, span)]
        + [whole(8, padded)] * nh,
        out_specs=whole(padded, span),
        compiler_params=pltpu.CompilerParams(vmem_limit_bytes=VMEM_LIMIT),
    )(gain.reshape(1, span), attended, fast, *all_squares)
    return (block_out, new_weights)


def solution(mesh):
    group = 4
    nh = mesh.shape["head"]
    inner = Mesh(
        np.asarray(mesh.devices).reshape(mesh.shape["ctx"] // group, group, nh),
        ("z", "grp", "head"),
    )
    ctx = ("z", "grp")
    placed = (
        P(ctx, "head"),
        P(ctx, "head"),
        P(ctx, "head"),
        P(ctx, "head"),
        P(ctx),
        P(None, "head", ctx, None),
        P("head"),
    )
    return jax.shard_map(
        on_device,
        mesh=inner,
        in_specs=placed,
        out_specs=(P(ctx, "head"), P(None, "head", ctx, None)),
        check_vma=False,
    )
```

```python
import functools

import jax
import jax.numpy as jnp
import numpy as np
from jax import lax
from jax.experimental import pallas as pl
from jax.experimental.pallas import tpu as pltpu
from jax.sharding import Mesh, PartitionSpec as P

HD = 128
NS_STEPS = 5

epsilon = 1e-06
quintic_a = 3.4445
quintic_b = -4.775
quintic_c = 2.0315
highest = lax.Precision.HIGHEST
f32 = jnp.float32
bf16 = jnp.bfloat16
VMEM_LIMIT = 24 * 1024 * 1024


def dot(a, b, contract, precision=None):
    return lax.dot_general(
        a, b, ((contract[:1], contract[1:]), ((), ())),
        precision=precision, preferred_element_type=f32,
    )


def call(body, outs, scratch=(), in_specs=None, flops=1e8, moved=1 << 20, **kw):
    given = {} if in_specs is None else {"in_specs": in_specs}
    return pl.pallas_call(
        body,
        out_shape=outs,
        **given,
        scratch_shapes=list(scratch),
        compiler_params=pltpu.CompilerParams(vmem_limit_bytes=VMEM_LIMIT),
        cost_estimate=pl.CostEstimate(flops=int(flops), bytes_accessed=moved, transcendentals=0),
        **kw,
    )


def sds(shape, dtype):
    return jax.ShapeDtypeStruct(shape, dtype)


def served(n):
    return [0] + list(range(n - 1, 0, -1))


def first_owner(h):
    return h & 1


GROUP = ("x", "core")
ORDER = ("core", "x", "z")


def position():
    return lax.axis_index("z"), lax.axis_index("x") * 2 + lax.axis_index("core")


def index_of(z, j, slots):
    index = 0
    for name in ORDER:
        size, at = {"z": (slots, z), "x": (2, j // 2), "core": (2, j % 2)}[name]
        index = index * size + at
    return index


def sigmoid(x):
    return 0.5 * jnp.tanh(0.5 * x) + 0.5


def cast_body(heads, group, w_ref, w_out):
    slots = w_out.shape[0] // group
    for j in range(group):
        for m in range(3):
            low = w_ref[m, min(j, heads - 1)].astype(bf16)
            for z in range(slots):
                w_out[index_of(z, j, slots), m] = low


def prep_body(
    heads, group, tokens, after, update, rate_ref, k_ref, v_ref, q_ref, kv_out, *outs
):
    token_outs, targets = outs[:-1], outs[-1]
    padded = kv_out.shape[0]
    place = position()
    valid = lax.broadcasted_iota(jnp.int32, (padded, 1), 0) < tokens
    none = jnp.zeros((), bf16)
    keep = update[...].astype(f32)
    lane_head = lax.broadcasted_iota(jnp.int32, (heads, heads * HD), 1) // HD
    row = lax.broadcasted_iota(jnp.int32, (heads, heads * HD), 0)
    rate = dot(rate_ref[...], (row == lane_head).astype(f32), (0, 0), highest)[:padded]
    targets[...] = ((rate * keep) * v_ref[...].astype(f32)).astype(bf16)
    for d in range(group):
        head = jnp.minimum(place[1] ^ d, heads - 1)
        cols = pl.ds(pl.multiple_of(head * HD, HD), HD)
        for i, source in enumerate((k_ref, targets, q_ref)):
            token_outs[d][:, i * HD : (i + 1) * HD] = source[:tokens, cols]
    kv_out[:, : heads * HD] = jnp.where(valid, k_ref[...], none)
    kv_out[:, heads * HD :] = jnp.where(valid, v_ref[...], none)


def gradients(token_refs, w_ref, k_all, t_all, staged, deltas):
    tokens = token_refs[0].shape[0]
    padded = -(-tokens // 16) * 16
    width = k_all.shape[0]
    filled = len(token_refs) * padded
    for i, ref in enumerate(token_refs):
        for part, rows in enumerate((k_all, t_all)):
            rows[(i + 1) * padded - 16 : (i + 1) * padded] = jnp.zeros((16, HD), bf16)
            rows[i * padded : i * padded + tokens] = ref[:, part * HD : (part + 1) * HD]
    if width > filled:
        k_all[filled:] = jnp.zeros((width - filled, HD), bf16)
        t_all[filled:] = jnp.zeros((width - filled, HD), bf16)
    hidden = deltas.shape[1]
    w1, w3, w2 = (weight_rows(w_ref, m, 0, hidden) for m in range(3))
    tall = 64
    for left in range(0, width, staged.shape[3]):
        right = min(left + staged.shape[3], width)
        cols, used = slice(left, right), slice(0, right - left)
        stage = staged.at[(left // staged.shape[3]) % staged.shape[0]]
        stage[0, :, used] = dot(w1, k_all[cols], (1, 1))
        stage[1, :, used] = dot(w3, k_all[cols], (1, 1))
        stage[2, :, used] = dot(w2, t_all[cols], (1, 1))
        for start in range(0, hidden, tall):
            rows = slice(start, start + tall)
            pre_one, pre_three, back = (stage[i, rows, used] for i in range(3))
            sig = sigmoid(pre_one)
            gate = pre_one * sig
            deltas[2, rows, cols] = (gate * pre_three).astype(bf16)
            deltas[1, rows, cols] = (back * gate).astype(bf16)
            deltas[0, rows, cols] = (
                (back * pre_three) * (sig * (1.0 + pre_one * (1.0 - sig)))
            ).astype(bf16)
    return (
        dot(deltas[0], k_all[...], (1, 0)),
        dot(deltas[1], k_all[...], (1, 0)),
        dot(deltas[2], t_all[...], (1, 0)),
    )


def gradient_scratch(slots, padded, hidden):
    width = -(-slots * padded // 128) * 128
    return [
        pltpu.VMEM((width, HD), bf16),
        pltpu.VMEM((width, HD), bf16),
        pltpu.VMEM((2, 3, hidden, 256), f32),
        pltpu.VMEM((3, hidden, width), bf16),
    ]


def apply_tokens(token_ref, w_ref, stage, act, held):
    hidden = act.shape[1]
    tall = 16
    w1, w3, w2 = (weight_rows(w_ref, m, 0, hidden) for m in range(3))
    held[held.shape[0] - 16 :] = jnp.zeros((16, HD), bf16)
    held[: token_ref.shape[0]] = token_ref[:, 2 * HD :]
    query = held[...]
    stage[0] = dot(query, w1, (1, 1))
    stage[1] = dot(query, w3, (1, 1))
    for start in range(0, query.shape[0], tall):
        rows = slice(start, start + tall)
        proj = stage[0, rows]
        act[rows] = (proj * sigmoid(proj) * stage[1, rows]).astype(bf16)
    return dot(act[...], w2, (1, 0)).astype(bf16)


def apply_scratch(padded, hidden):
    return [
        pltpu.VMEM((2, 2, padded, hidden), f32),
        pltpu.VMEM((2, padded, hidden), bf16),
        pltpu.VMEM((2, padded, HD), bf16),
    ]


def early_body(count, *refs):
    token_refs, w_ref = refs[:count], refs[count]
    grads, fast = refs[count + 1 : count + 3]
    scratch, (staged, acts, held) = refs[count + 3 : -3], refs[-3:]
    for m, grad in enumerate(gradients(token_refs, w_ref, *scratch)):
        grads[m] = grad
    for i, ref in enumerate(token_refs):
        fast[i] = apply_tokens(ref, w_ref, *(buffer.at[i % 2] for buffer in (staged, acts, held)))


def late_body(group, slots, token_ref, w_ref, early, *refs):
    place = position()
    outs, sums, scratch = refs[:slots], refs[slots], refs[slots + 1 :]
    for m, grad in enumerate(gradients([token_ref], w_ref, *scratch)):
        sums[m] = (early[m] + grad).astype(bf16)
    for d in range(slots):
        matrix = lax.rem((place[0] ^ d) - first_owner(place[1]) + slots, slots)
        chosen = sums[jnp.minimum(matrix, 2)]
        outs[d][...] = jnp.where(matrix < 3, chosen, jnp.zeros_like(chosen))


def late_apply_body(early_slots, last, token_ref, w_ref, early, out, staged, acts, held):
    place = position()
    for i, d in enumerate(early_slots):
        out[place[1] ^ d] = early[i]
    out[place[1] ^ last] = apply_tokens(
        token_ref, w_ref, staged.at[0], acts.at[0], held.at[0]
    )


def weight_rows(w_ref, m, start, block):
    if len(w_ref.shape) == 3:
        return w_ref[m, start : start + block]
    rows = w_ref.shape[2]
    return w_ref[start // rows : (start + block) // rows, m].reshape(block, HD)


def parts_of(x):
    high = x.astype(bf16)
    return high, (x - high.astype(f32)).astype(bf16)


def left_of(x):
    high, low = parts_of(x)
    return jnp.concatenate([high, high, low], axis=1)


def right_of(x):
    high, low = parts_of(x)
    return jnp.concatenate([high, low, high], axis=0)


def ortho_body(heads, slots, *refs):
    place = position()
    matrix = lax.rem(place[0] - first_owner(place[1]) + slots, slots)
    owner = (place[1] < heads) & (matrix < 3)

    @pl.when(owner)
    def _():
        orthogonalize(refs[:-1], refs[-1])

    @pl.when(jnp.logical_not(owner))
    def _():
        refs[-1][...] = jnp.zeros(refs[-1].shape, refs[-1].dtype)


def orthogonalize(parts, out):
    grads = parts[0][...].astype(f32)
    for part in parts[1:]:
        grads = grads + part[...].astype(f32)
    eye = (
        lax.broadcasted_iota(jnp.int32, (HD, HD), 0) == lax.broadcasted_iota(jnp.int32, (HD, HD), 1)
    ).astype(f32)
    both = jnp.concatenate(parts_of(grads), axis=1)
    blocks = dot(both, both, (0, 0))
    raw = (blocks[:HD, HD:] + blocks[HD:, :HD]) + blocks[:HD, :HD]
    square = jnp.sum(jnp.sum(raw * eye, axis=0, keepdims=True), axis=1, keepdims=True)
    scale = lax.rsqrt(square + epsilon)
    gram = raw * scale * scale
    total = None
    for step in range(NS_STEPS):
        square_gram = dot(left_of(gram), right_of(gram), (1, 0))
        mix = quintic_a * eye + quintic_b * gram + quintic_c * square_gram
        right = right_of(mix)
        if step < NS_STEPS - 1:
            gram = dot(left_of(dot(left_of(gram), right, (1, 0))), right, (1, 0))
            total = mix if total is None else dot(left_of(total), right, (1, 0))
    ortho = dot(left_of(grads * scale), right_of(total), (1, 0))
    out[...] = dot(left_of(ortho), right, (1, 0)).astype(out.dtype)


def finish_body(slots, group, w_ref, rows_ref, out):
    heads = w_ref.shape[1]
    for m in range(3):
        for h in range(heads):
            weights = w_ref[m, h]
            summed = weights + rows_ref[index_of((m + first_owner(h)) % slots, h, slots)].astype(f32)
            old = jnp.sqrt(jnp.sum(weights * weights, axis=1, keepdims=True))
            new = lax.rsqrt(jnp.sum(summed * summed, axis=1, keepdims=True) + epsilon)
            out[m, h] = summed * (old * new)


def attend_body(heads, tokens, q_ref, own_ref, back_ref, out):
    padded = own_ref.shape[0]
    span = heads * HD
    column = lax.broadcasted_iota(jnp.int32, (1, 2 * padded), 1)
    place = position()
    first = (place[0] == 0) & (place[1] == 0)
    stop = jnp.where(first, padded, padded + tokens)
    live = (column < tokens) | ((column >= padded) & (column < stop))
    for h in range(heads):
        cols = slice(h * HD, (h + 1) * HD)
        key = jnp.concatenate([own_ref[:, cols], back_ref[:, cols]], axis=0)
        vcols = slice(span + h * HD, span + (h + 1) * HD)
        value = jnp.concatenate([own_ref[:, vcols], back_ref[:, vcols]], axis=0)
        scores = dot(q_ref[:, cols], key, (1, 1)) * (HD ** (-0.5))
        scores = jnp.where(live, scores, -1e30)
        weights = jnp.exp(scores - jnp.max(scores, axis=1, keepdims=True))
        probs = (weights / jnp.sum(weights, axis=1, keepdims=True)).astype(bf16)
        out[:, cols] = dot(probs, value, (1, 0))


def assemble_body(heads, slots, out, squares):
    for h in range(heads):
        out[:, h * HD : (h + 1) * HD] = slots[h]
    fast = out[...].astype(f32)
    squares[...] = dot(jnp.ones((8, heads * HD), f32), fast * fast, (1, 1), highest)


def block_body(features, gain_ref, attended_ref, fast_ref, *refs):
    squares, out = refs[:-1], refs[-1]
    total = squares[0][...]
    for other in squares[1:]:
        total = total + other[...]
    pick = (lax.broadcasted_iota(jnp.int32, (8, HD), 0) == 0).astype(f32)
    spread = dot(total, pick, (0, 0), highest) * (1.0 / features)
    scale = lax.rsqrt(spread + epsilon)
    for h in range(fast_ref.shape[1] // HD):
        cols = slice(h * HD, (h + 1) * HD)
        out[:, cols] = (
            attended_ref[:, cols] + fast_ref[:, cols].astype(f32) * gain_ref[:, cols] * scale
        ).astype(bf16)


def on_device(queries, keys, values, rates, frame_update, fast_weights, gain):
    tokens = queries.shape[0]
    heads = queries.shape[1] // HD
    rows_local = fast_weights.shape[2]
    nz, nh = lax.axis_size("z"), lax.axis_size("head")
    group = lax.axis_size("x") * lax.axis_size("core")
    count = nz * group
    hidden = count * rows_local
    padded = -(-tokens // 16) * 16
    span = heads * HD

    def whole(*shape):
        return pl.BlockSpec(shape, lambda i: (0,) * len(shape))

    low_shape = (count, 3, rows_local, HD)
    low = call(
        functools.partial(cast_body, heads, group), sds(low_shape, bf16), flops=1e6
    )(fast_weights)
    prepared = pl.pallas_call(
        functools.partial(prep_body, heads, group, tokens),
        grid=(1,),
        out_shape=[sds((padded, 2 * span), bf16)]
        + [sds((tokens, 3 * HD), bf16)] * group,
        in_specs=[pl.BlockSpec(memory_space=pl.ANY), whole(1, 1)]
        + [whole(heads, -(-padded // 128) * 128)]
        + [whole(padded, span)] * 3,
        out_specs=[whole(padded, 2 * span)] + [whole(tokens, 3 * HD)] * group,
        scratch_shapes=[pltpu.VMEM((padded, span), bf16)],
        compiler_params=pltpu.CompilerParams(vmem_limit_bytes=VMEM_LIMIT),
    )(low, frame_update.reshape(1, 1), rates.T, keys, values, queries)
    kv_own, *token_slots = prepared

    weights = lax.all_to_all(low, ORDER, 0, 0, tiled=True)
    if rows_local % 16:
        weights = weights.transpose(1, 0, 2, 3).reshape(3, hidden, HD)
    for d in served(group)[1:]:
        pairs = [(s, s ^ d) for s in range(group) if s ^ d < heads]
        token_slots[d] = lax.ppermute(token_slots[d], GROUP, pairs)

    last = group // 2
    early_slots = [d for d in served(group) if d != last]
    early_grads, early_fast = call(
        functools.partial(early_body, len(early_slots)),
        [sds((3, hidden, HD), f32), sds((len(early_slots), padded, HD), bf16)],
        scratch=gradient_scratch(len(early_slots), padded, hidden) + apply_scratch(padded, hidden),
        flops=1e9,
    )(*(token_slots[d] for d in early_slots), weights)
    partials = list(
        call(
            functools.partial(late_body, group, nz),
            [sds((hidden, HD), bf16)] * nz,
            scratch=[pltpu.VMEM((3, hidden, HD), bf16)] + gradient_scratch(1, padded, hidden),
            flops=5e8,
        )(token_slots[last], weights, early_grads)
    )
    weights, partials[0] = lax.optimization_barrier((weights, partials[0]))
    for d in served(nz)[1:]:
        pairs = []
        for z in range(nz):
            pairs += [
                (z * group + j, (z ^ d) * group + j)
                for j in range(heads)
                if ((z ^ d) - first_owner(j)) % nz < 3
            ]
        partials[d] = lax.ppermute(partials[d], ("z", *GROUP), pairs)

    fast_slots = call(
        functools.partial(late_apply_body, early_slots, last),
        sds((group, padded, HD), bf16),
        scratch=apply_scratch(padded, hidden),
        flops=1e3,
        moved=1024,
    )(token_slots[last], weights, early_fast)
    kv_own, partials[0], fast_slots = lax.optimization_barrier((kv_own, partials[0], fast_slots))
    fast_slots = lax.all_to_all(fast_slots, GROUP, 0, 0, tiled=True)

    ring = [(i, i + 1) for i in range(count - 1)]
    kv_back = lax.ppermute(kv_own, ("z", *GROUP), ring)

    ortho = call(functools.partial(ortho_body, heads, nz), sds((hidden, HD), bf16), flops=1e9)(
        *(partials[d] for d in served(nz))
    )
    queries, ortho = lax.optimization_barrier((queries, ortho))
    rows = lax.all_to_all(
        ortho.reshape(count, rows_local, HD), ORDER, 0, 0, tiled=True
    )
    new_weights = call(
        functools.partial(finish_body, nz, group), sds(fast_weights.shape, f32), flops=1e6
    )(fast_weights, rows)

    attended = pl.pallas_call(
        functools.partial(attend_body, heads, tokens),
        grid=(1,),
        out_shape=sds((padded, span), f32),
        in_specs=[whole(padded, span)] + [whole(padded, 2 * span)] * 2,
        out_specs=whole(padded, span),
        compiler_params=pltpu.CompilerParams(vmem_limit_bytes=VMEM_LIMIT),
    )(queries, kv_own, kv_back)
    fast, squares = call(
        functools.partial(assemble_body, heads),
        [sds((padded, span), bf16), sds((8, padded), f32)],
        flops=1e7,
    )(fast_slots)
    all_squares = [squares] + [
        lax.ppermute(squares, "head", [(s, (s + d) % nh) for s in range(nh)]) for d in range(1, nh)
    ]
    block_out = pl.pallas_call(
        functools.partial(block_body, span * nh),
        grid=(1,),
        out_shape=sds((tokens, span), bf16),
        in_specs=[whole(1, span), whole(padded, span), whole(padded, span)]
        + [whole(8, padded)] * nh,
        out_specs=whole(padded, span),
        compiler_params=pltpu.CompilerParams(vmem_limit_bytes=VMEM_LIMIT),
    )(gain.reshape(1, span), attended, fast, *all_squares)
    return (block_out, new_weights)


def solution(mesh):
    nh = mesh.shape["head"]
    inner = Mesh(
        np.asarray(mesh.devices).reshape(mesh.shape["ctx"] // 4, 2, 2, nh),
        ("z", *GROUP, "head"),
    )
    ctx = ("z", *GROUP)
    placed = (
        P(ctx, "head"),
        P(ctx, "head"),
        P(ctx, "head"),
        P(ctx, "head"),
        P(ctx),
        P(None, "head", ctx, None),
        P("head"),
    )
    return jax.shard_map(
        on_device,
        mesh=inner,
        in_specs=placed,
        out_specs=(P(ctx, "head"), P(None, "head", ctx, None)),
        check_vma=False,
    )
```

```python
import functools

import jax
import jax.numpy as jnp
import numpy as np
from jax import lax
from jax.experimental import pallas as pl
from jax.experimental.pallas import tpu as pltpu
from jax.sharding import Mesh, PartitionSpec as P

HD = 128
NS_STEPS = 5

epsilon = 1e-06
quintic_a = 3.4445
quintic_b = -4.775
quintic_c = 2.0315
highest = lax.Precision.HIGHEST
f32 = jnp.float32
bf16 = jnp.bfloat16
VMEM_LIMIT = 24 * 1024 * 1024


def dot(a, b, contract, precision=None):
    return lax.dot_general(
        a, b, ((contract[:1], contract[1:]), ((), ())),
        precision=precision, preferred_element_type=f32,
    )


def call(body, outs, scratch=(), in_specs=None, flops=1e8, moved=1 << 20, **kw):
    given = {} if in_specs is None else {"in_specs": in_specs}
    return pl.pallas_call(
        body,
        out_shape=outs,
        **given,
        scratch_shapes=list(scratch),
        compiler_params=pltpu.CompilerParams(vmem_limit_bytes=VMEM_LIMIT),
        cost_estimate=pl.CostEstimate(flops=int(flops), bytes_accessed=moved, transcendentals=0),
        **kw,
    )


def sds(shape, dtype):
    return jax.ShapeDtypeStruct(shape, dtype)


def served(n):
    return [0] + list(range(n - 1, 0, -1))


def first_owner(h):
    return h & 1


GROUP = ("x", "core")
ORDER = ("x", "z", "core")


def position():
    return lax.axis_index("z"), lax.axis_index("x") * 2 + lax.axis_index("core")


def index_of(z, j, slots):
    index = 0
    for name in ORDER:
        size, at = {"z": (slots, z), "x": (2, j // 2), "core": (2, j % 2)}[name]
        index = index * size + at
    return index


def sigmoid(x):
    return 0.5 * jnp.tanh(0.5 * x) + 0.5


def cast_body(heads, group, w_ref, w_out):
    slots = w_out.shape[0] // group
    for j in range(group):
        for m in range(3):
            low = w_ref[m, min(j, heads - 1)].astype(bf16)
            for z in range(slots):
                w_out[index_of(z, j, slots), m] = low


def prep_body(
    heads, group, tokens, after, update, rate_ref, k_ref, v_ref, q_ref, kv_out, *outs
):
    token_outs, targets = outs[:-1], outs[-1]
    padded = kv_out.shape[0]
    place = position()
    valid = lax.broadcasted_iota(jnp.int32, (padded, 1), 0) < tokens
    none = jnp.zeros((), bf16)
    keep = update[...].astype(f32)
    lane_head = lax.broadcasted_iota(jnp.int32, (heads, heads * HD), 1) // HD
    row = lax.broadcasted_iota(jnp.int32, (heads, heads * HD), 0)
    rate = dot(rate_ref[...], (row == lane_head).astype(f32), (0, 0), highest)[:padded]
    targets[...] = ((rate * keep) * v_ref[...].astype(f32)).astype(bf16)
    for d in range(group):
        head = jnp.minimum(place[1] ^ d, heads - 1)
        cols = pl.ds(pl.multiple_of(head * HD, HD), HD)
        for i, source in enumerate((k_ref, targets, q_ref)):
            token_outs[d][:, i * HD : (i + 1) * HD] = source[:tokens, cols]
    kv_out[:, : heads * HD] = jnp.where(valid, k_ref[...], none)
    kv_out[:, heads * HD :] = jnp.where(valid, v_ref[...], none)


def gradients(token_refs, w_ref, k_all, t_all, staged, deltas):
    tokens = token_refs[0].shape[0]
    padded = -(-tokens // 16) * 16
    width = k_all.shape[0]
    filled = len(token_refs) * padded
    for i, ref in enumerate(token_refs):
        for part, rows in enumerate((k_all, t_all)):
            rows[(i + 1) * padded - 16 : (i + 1) * padded] = jnp.zeros((16, HD), bf16)
            rows[i * padded : i * padded + tokens] = ref[:, part * HD : (part + 1) * HD]
    if width > filled:
        k_all[filled:] = jnp.zeros((width - filled, HD), bf16)
        t_all[filled:] = jnp.zeros((width - filled, HD), bf16)
    hidden = deltas.shape[1]
    w1, w3, w2 = (weight_rows(w_ref, m, 0, hidden) for m in range(3))
    tall = 64
    for left in range(0, width, staged.shape[3]):
        right = min(left + staged.shape[3], width)
        cols, used = slice(left, right), slice(0, right - left)
        stage = staged.at[(left // staged.shape[3]) % staged.shape[0]]
        stage[0, :, used] = dot(w1, k_all[cols], (1, 1))
        stage[1, :, used] = dot(w3, k_all[cols], (1, 1))
        stage[2, :, used] = dot(w2, t_all[cols], (1, 1))
        for start in range(0, hidden, tall):
            rows = slice(start, start + tall)
            pre_one, pre_three, back = (stage[i, rows, used] for i in range(3))
            sig = sigmoid(pre_one)
            gate = pre_one * sig
            deltas[2, rows, cols] = (gate * pre_three).astype(bf16)
            deltas[1, rows, cols] = (back * gate).astype(bf16)
            deltas[0, rows, cols] = (
                (back * pre_three) * (sig * (1.0 + pre_one * (1.0 - sig)))
            ).astype(bf16)
    return (
        dot(deltas[0], k_all[...], (1, 0)),
        dot(deltas[1], k_all[...], (1, 0)),
        dot(deltas[2], t_all[...], (1, 0)),
    )


def gradient_scratch(slots, padded, hidden):
    width = -(-slots * padded // 128) * 128
    return [
        pltpu.VMEM((width, HD), bf16),
        pltpu.VMEM((width, HD), bf16),
        pltpu.VMEM((2, 3, hidden, 256), f32),
        pltpu.VMEM((3, hidden, width), bf16),
    ]


def apply_tokens(token_ref, w_ref, stage, act, held):
    hidden = act.shape[1]
    tall = 16
    w1, w3, w2 = (weight_rows(w_ref, m, 0, hidden) for m in range(3))
    held[held.shape[0] - 16 :] = jnp.zeros((16, HD), bf16)
    held[: token_ref.shape[0]] = token_ref[:, 2 * HD :]
    query = held[...]
    stage[0] = dot(query, w1, (1, 1))
    stage[1] = dot(query, w3, (1, 1))
    for start in range(0, query.shape[0], tall):
        rows = slice(start, start + tall)
        proj = stage[0, rows]
        act[rows] = (proj * sigmoid(proj) * stage[1, rows]).astype(bf16)
    return dot(act[...], w2, (1, 0)).astype(bf16)


def apply_scratch(padded, hidden):
    return [
        pltpu.VMEM((2, 2, padded, hidden), f32),
        pltpu.VMEM((2, padded, hidden), bf16),
        pltpu.VMEM((2, padded, HD), bf16),
    ]


def early_body(count, *refs):
    token_refs, w_ref = refs[:count], refs[count]
    grads, fast = refs[count + 1 : count + 3]
    scratch, (staged, acts, held) = refs[count + 3 : -3], refs[-3:]
    for m, grad in enumerate(gradients(token_refs, w_ref, *scratch)):
        grads[m] = grad
    for i, ref in enumerate(token_refs):
        fast[i] = apply_tokens(ref, w_ref, *(buffer.at[i % 2] for buffer in (staged, acts, held)))


def late_body(group, slots, token_ref, w_ref, early, *refs):
    place = position()
    outs, sums, scratch = refs[:slots], refs[slots], refs[slots + 1 :]
    for m, grad in enumerate(gradients([token_ref], w_ref, *scratch)):
        sums[m] = (early[m] + grad).astype(bf16)
    for d in range(slots):
        matrix = lax.rem((place[0] ^ d) - first_owner(place[1]) + slots, slots)
        chosen = sums[jnp.minimum(matrix, 2)]
        outs[d][...] = jnp.where(matrix < 3, chosen, jnp.zeros_like(chosen))


def late_apply_body(early_slots, last, token_ref, w_ref, early, out, staged, acts, held):
    place = position()
    for i, d in enumerate(early_slots):
        out[place[1] ^ d] = early[i]
    out[place[1] ^ last] = apply_tokens(
        token_ref, w_ref, staged.at[0], acts.at[0], held.at[0]
    )


def weight_rows(w_ref, m, start, block):
    if len(w_ref.shape) == 3:
        return w_ref[m, start : start + block]
    rows = w_ref.shape[2]
    return w_ref[start // rows : (start + block) // rows, m].reshape(block, HD)


def parts_of(x):
    high = x.astype(bf16)
    return high, (x - high.astype(f32)).astype(bf16)


def left_of(x):
    high, low = parts_of(x)
    return jnp.concatenate([high, high, low], axis=1)


def right_of(x):
    high, low = parts_of(x)
    return jnp.concatenate([high, low, high], axis=0)


def ortho_body(heads, slots, *refs):
    place = position()
    matrix = lax.rem(place[0] - first_owner(place[1]) + slots, slots)
    owner = (place[1] < heads) & (matrix < 3)

    @pl.when(owner)
    def _():
        orthogonalize(refs[:-1], refs[-1])

    @pl.when(jnp.logical_not(owner))
    def _():
        refs[-1][...] = jnp.zeros(refs[-1].shape, refs[-1].dtype)


def orthogonalize(parts, out):
    grads = parts[0][...].astype(f32)
    for part in parts[1:]:
        grads = grads + part[...].astype(f32)
    eye = (
        lax.broadcasted_iota(jnp.int32, (HD, HD), 0) == lax.broadcasted_iota(jnp.int32, (HD, HD), 1)
    ).astype(f32)
    both = jnp.concatenate(parts_of(grads), axis=1)
    blocks = dot(both, both, (0, 0))
    raw = (blocks[:HD, HD:] + blocks[HD:, :HD]) + blocks[:HD, :HD]
    square = jnp.sum(jnp.sum(raw * eye, axis=0, keepdims=True), axis=1, keepdims=True)
    scale = lax.rsqrt(square + epsilon)
    gram = raw * scale * scale
    total = None
    for step in range(NS_STEPS):
        square_gram = dot(left_of(gram), right_of(gram), (1, 0))
        mix = quintic_a * eye + quintic_b * gram + quintic_c * square_gram
        right = right_of(mix)
        if step < NS_STEPS - 1:
            gram = dot(left_of(dot(left_of(gram), right, (1, 0))), right, (1, 0))
            total = mix if total is None else dot(left_of(total), right, (1, 0))
    ortho = dot(left_of(grads * scale), right_of(total), (1, 0))
    out[...] = dot(left_of(ortho), right, (1, 0)).astype(out.dtype)


def finish_body(slots, group, w_ref, rows_ref, out):
    heads = w_ref.shape[1]
    for m in range(3):
        for h in range(heads):
            weights = w_ref[m, h]
            summed = weights + rows_ref[index_of((m + first_owner(h)) % slots, h, slots)].astype(f32)
            old = jnp.sqrt(jnp.sum(weights * weights, axis=1, keepdims=True))
            new = lax.rsqrt(jnp.sum(summed * summed, axis=1, keepdims=True) + epsilon)
            out[m, h] = summed * (old * new)


def attend_body(heads, tokens, q_ref, own_ref, back_ref, out):
    padded = own_ref.shape[0]
    span = heads * HD
    column = lax.broadcasted_iota(jnp.int32, (1, 2 * padded), 1)
    place = position()
    first = (place[0] == 0) & (place[1] == 0)
    stop = jnp.where(first, padded, padded + tokens)
    live = (column < tokens) | ((column >= padded) & (column < stop))
    for h in range(heads):
        cols = slice(h * HD, (h + 1) * HD)
        key = jnp.concatenate([own_ref[:, cols], back_ref[:, cols]], axis=0)
        vcols = slice(span + h * HD, span + (h + 1) * HD)
        value = jnp.concatenate([own_ref[:, vcols], back_ref[:, vcols]], axis=0)
        scores = dot(q_ref[:, cols], key, (1, 1)) * (HD ** (-0.5))
        scores = jnp.where(live, scores, -1e30)
        weights = jnp.exp(scores - jnp.max(scores, axis=1, keepdims=True))
        probs = (weights / jnp.sum(weights, axis=1, keepdims=True)).astype(bf16)
        out[:, cols] = dot(probs, value, (1, 0))


def assemble_body(heads, slots, out, squares):
    for h in range(heads):
        out[:, h * HD : (h + 1) * HD] = slots[h]
    fast = out[...].astype(f32)
    squares[...] = dot(jnp.ones((8, heads * HD), f32), fast * fast, (1, 1), highest)


def block_body(features, gain_ref, attended_ref, fast_ref, *refs):
    squares, out = refs[:-1], refs[-1]
    total = squares[0][...]
    for other in squares[1:]:
        total = total + other[...]
    pick = (lax.broadcasted_iota(jnp.int32, (8, HD), 0) == 0).astype(f32)
    spread = dot(total, pick, (0, 0), highest) * (1.0 / features)
    scale = lax.rsqrt(spread + epsilon)
    for h in range(fast_ref.shape[1] // HD):
        cols = slice(h * HD, (h + 1) * HD)
        out[:, cols] = (
            attended_ref[:, cols] + fast_ref[:, cols].astype(f32) * gain_ref[:, cols] * scale
        ).astype(bf16)


def on_device(queries, keys, values, rates, frame_update, fast_weights, gain):
    tokens = queries.shape[0]
    heads = queries.shape[1] // HD
    rows_local = fast_weights.shape[2]
    nz, nh = lax.axis_size("z"), lax.axis_size("head")
    group = lax.axis_size("x") * lax.axis_size("core")
    count = nz * group
    hidden = count * rows_local
    padded = -(-tokens // 16) * 16
    span = heads * HD

    def whole(*shape):
        return pl.BlockSpec(shape, lambda i: (0,) * len(shape))

    low_shape = (count, 3, rows_local, HD)
    low = call(
        functools.partial(cast_body, heads, group), sds(low_shape, bf16), flops=1e6
    )(fast_weights)
    prepared = pl.pallas_call(
        functools.partial(prep_body, heads, group, tokens),
        grid=(1,),
        out_shape=[sds((padded, 2 * span), bf16)]
        + [sds((tokens, 3 * HD), bf16)] * group,
        in_specs=[pl.BlockSpec(memory_space=pl.ANY), whole(1, 1)]
        + [whole(heads, -(-padded // 128) * 128)]
        + [whole(padded, span)] * 3,
        out_specs=[whole(padded, 2 * span)] + [whole(tokens, 3 * HD)] * group,
        scratch_shapes=[pltpu.VMEM((padded, span), bf16)],
        compiler_params=pltpu.CompilerParams(vmem_limit_bytes=VMEM_LIMIT),
    )(low, frame_update.reshape(1, 1), rates.T, keys, values, queries)
    kv_own, *token_slots = prepared

    weights = lax.all_to_all(low, ORDER, 0, 0, tiled=True)
    if rows_local % 16:
        weights = weights.transpose(1, 0, 2, 3).reshape(3, hidden, HD)
    for d in served(group)[1:]:
        pairs = [(s, s ^ d) for s in range(group) if s ^ d < heads]
        token_slots[d] = lax.ppermute(token_slots[d], GROUP, pairs)

    last = group // 2
    early_slots = [d for d in served(group) if d != last]
    early_grads, early_fast = call(
        functools.partial(early_body, len(early_slots)),
        [sds((3, hidden, HD), f32), sds((len(early_slots), padded, HD), bf16)],
        scratch=gradient_scratch(len(early_slots), padded, hidden) + apply_scratch(padded, hidden),
        flops=1e9,
    )(*(token_slots[d] for d in early_slots), weights)
    partials = list(
        call(
            functools.partial(late_body, group, nz),
            [sds((hidden, HD), bf16)] * nz,
            scratch=[pltpu.VMEM((3, hidden, HD), bf16)] + gradient_scratch(1, padded, hidden),
            flops=5e8,
        )(token_slots[last], weights, early_grads)
    )
    weights, partials[0] = lax.optimization_barrier((weights, partials[0]))
    for d in served(nz)[1:]:
        pairs = []
        for z in range(nz):
            pairs += [
                (z * group + j, (z ^ d) * group + j)
                for j in range(heads)
                if ((z ^ d) - first_owner(j)) % nz < 3
            ]
        partials[d] = lax.ppermute(partials[d], ("z", *GROUP), pairs)

    fast_slots = call(
        functools.partial(late_apply_body, early_slots, last),
        sds((group, padded, HD), bf16),
        scratch=apply_scratch(padded, hidden),
        flops=1e3,
        moved=1024,
    )(token_slots[last], weights, early_fast)
    kv_own, partials[0], fast_slots = lax.optimization_barrier((kv_own, partials[0], fast_slots))
    fast_slots = lax.all_to_all(fast_slots, GROUP, 0, 0, tiled=True)

    ring = [(i, i + 1) for i in range(count - 1)]
    kv_back = lax.ppermute(kv_own, ("z", *GROUP), ring)

    ortho = call(functools.partial(ortho_body, heads, nz), sds((hidden, HD), bf16), flops=1e9)(
        *(partials[d] for d in served(nz))
    )
    queries, ortho = lax.optimization_barrier((queries, ortho))
    rows = lax.all_to_all(
        ortho.reshape(count, rows_local, HD), ORDER, 0, 0, tiled=True
    )
    new_weights = call(
        functools.partial(finish_body, nz, group), sds(fast_weights.shape, f32), flops=1e6
    )(fast_weights, rows)

    attended = pl.pallas_call(
        functools.partial(attend_body, heads, tokens),
        grid=(1,),
        out_shape=sds((padded, span), f32),
        in_specs=[whole(padded, span)] + [whole(padded, 2 * span)] * 2,
        out_specs=whole(padded, span),
        compiler_params=pltpu.CompilerParams(vmem_limit_bytes=VMEM_LIMIT),
    )(queries, kv_own, kv_back)
    fast, squares = call(
        functools.partial(assemble_body, heads),
        [sds((padded, span), bf16), sds((8, padded), f32)],
        flops=1e7,
    )(fast_slots)
    all_squares = [squares] + [
        lax.ppermute(squares, "head", [(s, (s + d) % nh) for s in range(nh)]) for d in range(1, nh)
    ]
    block_out = pl.pallas_call(
        functools.partial(block_body, span * nh),
        grid=(1,),
        out_shape=sds((tokens, span), bf16),
        in_specs=[whole(1, span), whole(padded, span), whole(padded, span)]
        + [whole(8, padded)] * nh,
        out_specs=whole(padded, span),
        compiler_params=pltpu.CompilerParams(vmem_limit_bytes=VMEM_LIMIT),
    )(gain.reshape(1, span), attended, fast, *all_squares)
    return (block_out, new_weights)


def solution(mesh):
    nh = mesh.shape["head"]
    inner = Mesh(
        np.asarray(mesh.devices).reshape(mesh.shape["ctx"] // 4, 2, 2, nh),
        ("z", *GROUP, "head"),
    )
    ctx = ("z", *GROUP)
    placed = (
        P(ctx, "head"),
        P(ctx, "head"),
        P(ctx, "head"),
        P(ctx, "head"),
        P(ctx),
        P(None, "head", ctx, None),
        P("head"),
    )
    return jax.shard_map(
        on_device,
        mesh=inner,
        in_specs=placed,
        out_specs=(P(ctx, "head"), P(None, "head", ctx, None)),
        check_vma=False,
    )
```

```python
import functools

import jax
import jax.numpy as jnp
from jax import lax
from jax.experimental import pallas as pl
from jax.experimental.pallas import tpu as pltpu
from jax.sharding import PartitionSpec as P

HD = 128
NS_STEPS = 5

epsilon = 1e-06
quintic_a = 3.4445
quintic_b = -4.775
quintic_c = 2.0315
highest = lax.Precision.HIGHEST
f32 = jnp.float32
bf16 = jnp.bfloat16
VMEM_LIMIT = 24 * 1024 * 1024


def dot(a, b, contract, precision=None):
    return lax.dot_general(
        a, b, ((contract[:1], contract[1:]), ((), ())),
        precision=precision, preferred_element_type=f32,
    )


def call(body, outs, scratch=(), in_specs=None, flops=1e8, moved=1 << 20, **kw):
    given = {} if in_specs is None else {"in_specs": in_specs}
    return pl.pallas_call(
        body,
        out_shape=outs,
        **given,
        scratch_shapes=list(scratch),
        compiler_params=pltpu.CompilerParams(vmem_limit_bytes=VMEM_LIMIT),
        cost_estimate=pl.CostEstimate(flops=int(flops), bytes_accessed=moved, transcendentals=0),
        **kw,
    )


def sds(shape, dtype):
    return jax.ShapeDtypeStruct(shape, dtype)


def served(n):
    return [0] + list(range(n - 1, 0, -1))


def first_owner(h):
    return h & 1


GROUP = 4


def position():
    return lax.axis_index("ctx") // GROUP, lax.axis_index("ctx") % GROUP


def index_of(z, j, slots):
    return (slots - 1 - z) * GROUP + j


def listed(slots):
    return [z * GROUP + j for z in reversed(range(slots)) for j in range(GROUP)]


def sigmoid(x):
    return 0.5 * jnp.tanh(0.5 * x) + 0.5


def cast_body(heads, group, w_ref, w_out):
    slots = w_out.shape[0] // group
    for j in range(group):
        for m in range(3):
            low = w_ref[m, min(j, heads - 1)].astype(bf16)
            for z in range(slots):
                w_out[index_of(z, j, slots), m] = low


def prep_body(
    heads, group, tokens, after, update, rate_ref, k_ref, v_ref, q_ref, kv_out, *outs
):
    token_outs, targets = outs[:-1], outs[-1]
    padded = kv_out.shape[0]
    place = position()
    valid = lax.broadcasted_iota(jnp.int32, (padded, 1), 0) < tokens
    none = jnp.zeros((), bf16)
    keep = update[...].astype(f32)
    lane_head = lax.broadcasted_iota(jnp.int32, (heads, heads * HD), 1) // HD
    row = lax.broadcasted_iota(jnp.int32, (heads, heads * HD), 0)
    rate = dot(rate_ref[...], (row == lane_head).astype(f32), (0, 0), highest)[:padded]
    targets[...] = ((rate * keep) * v_ref[...].astype(f32)).astype(bf16)
    for d in range(group):
        head = jnp.minimum(place[1] ^ d, heads - 1)
        cols = pl.ds(pl.multiple_of(head * HD, HD), HD)
        for i, source in enumerate((k_ref, targets, q_ref)):
            token_outs[d][:, i * HD : (i + 1) * HD] = source[:tokens, cols]
    kv_out[:, : heads * HD] = jnp.where(valid, k_ref[...], none)
    kv_out[:, heads * HD :] = jnp.where(valid, v_ref[...], none)


def gradients(token_refs, w_ref, k_all, t_all, staged, deltas):
    tokens = token_refs[0].shape[0]
    padded = -(-tokens // 16) * 16
    width = k_all.shape[0]
    filled = len(token_refs) * padded
    for i, ref in enumerate(token_refs):
        for part, rows in enumerate((k_all, t_all)):
            rows[(i + 1) * padded - 16 : (i + 1) * padded] = jnp.zeros((16, HD), bf16)
            rows[i * padded : i * padded + tokens] = ref[:, part * HD : (part + 1) * HD]
    if width > filled:
        k_all[filled:] = jnp.zeros((width - filled, HD), bf16)
        t_all[filled:] = jnp.zeros((width - filled, HD), bf16)
    hidden = deltas.shape[1]
    w1, w3, w2 = (weight_rows(w_ref, m, 0, hidden) for m in range(3))
    tall = 64
    for left in range(0, width, staged.shape[3]):
        right = min(left + staged.shape[3], width)
        cols, used = slice(left, right), slice(0, right - left)
        stage = staged.at[(left // staged.shape[3]) % staged.shape[0]]
        stage[0, :, used] = dot(w1, k_all[cols], (1, 1))
        stage[1, :, used] = dot(w3, k_all[cols], (1, 1))
        stage[2, :, used] = dot(w2, t_all[cols], (1, 1))
        for start in range(0, hidden, tall):
            rows = slice(start, start + tall)
            pre_one, pre_three, back = (stage[i, rows, used] for i in range(3))
            sig = sigmoid(pre_one)
            gate = pre_one * sig
            deltas[2, rows, cols] = (gate * pre_three).astype(bf16)
            deltas[1, rows, cols] = (back * gate).astype(bf16)
            deltas[0, rows, cols] = (
                (back * pre_three) * (sig * (1.0 + pre_one * (1.0 - sig)))
            ).astype(bf16)
    return (
        dot(deltas[0], k_all[...], (1, 0)),
        dot(deltas[1], k_all[...], (1, 0)),
        dot(deltas[2], t_all[...], (1, 0)),
    )


def gradient_scratch(slots, padded, hidden):
    width = -(-slots * padded // 128) * 128
    return [
        pltpu.VMEM((width, HD), bf16),
        pltpu.VMEM((width, HD), bf16),
        pltpu.VMEM((2, 3, hidden, 256), f32),
        pltpu.VMEM((3, hidden, width), bf16),
    ]


def apply_tokens(token_ref, w_ref, stage, act, held):
    hidden = act.shape[1]
    tall = 16
    w1, w3, w2 = (weight_rows(w_ref, m, 0, hidden) for m in range(3))
    held[held.shape[0] - 16 :] = jnp.zeros((16, HD), bf16)
    held[: token_ref.shape[0]] = token_ref[:, 2 * HD :]
    query = held[...]
    stage[0] = dot(query, w1, (1, 1))
    stage[1] = dot(query, w3, (1, 1))
    for start in range(0, query.shape[0], tall):
        rows = slice(start, start + tall)
        proj = stage[0, rows]
        act[rows] = (proj * sigmoid(proj) * stage[1, rows]).astype(bf16)
    return dot(act[...], w2, (1, 0)).astype(bf16)


def apply_scratch(padded, hidden):
    return [
        pltpu.VMEM((2, 2, padded, hidden), f32),
        pltpu.VMEM((2, padded, hidden), bf16),
        pltpu.VMEM((2, padded, HD), bf16),
    ]


def early_body(count, *refs):
    token_refs, w_ref = refs[:count], refs[count]
    grads, fast = refs[count + 1 : count + 3]
    scratch, (staged, acts, held) = refs[count + 3 : -3], refs[-3:]
    for m, grad in enumerate(gradients(token_refs, w_ref, *scratch)):
        grads[m] = grad
    for i, ref in enumerate(token_refs):
        fast[i] = apply_tokens(ref, w_ref, *(buffer.at[i % 2] for buffer in (staged, acts, held)))


def late_body(group, slots, token_ref, w_ref, early, *refs):
    place = position()
    outs, sums, scratch = refs[:slots], refs[slots], refs[slots + 1 :]
    for m, grad in enumerate(gradients([token_ref], w_ref, *scratch)):
        sums[m] = (early[m] + grad).astype(bf16)
    for d in range(slots):
        matrix = lax.rem((place[0] ^ d) - first_owner(place[1]) + slots, slots)
        chosen = sums[jnp.minimum(matrix, 2)]
        outs[d][...] = jnp.where(matrix < 3, chosen, jnp.zeros_like(chosen))


def late_apply_body(early_slots, last, token_ref, w_ref, early, out, staged, acts, held):
    place = position()
    for i, d in enumerate(early_slots):
        out[place[1] ^ d] = early[i]
    out[place[1] ^ last] = apply_tokens(
        token_ref, w_ref, staged.at[0], acts.at[0], held.at[0]
    )


def weight_rows(w_ref, m, start, block):
    if len(w_ref.shape) == 3:
        return w_ref[m, start : start + block]
    rows = w_ref.shape[2]
    return w_ref[start // rows : (start + block) // rows, m].reshape(block, HD)


def parts_of(x):
    high = x.astype(bf16)
    return high, (x - high.astype(f32)).astype(bf16)


def left_of(x):
    high, low = parts_of(x)
    return jnp.concatenate([high, high, low], axis=1)


def right_of(x):
    high, low = parts_of(x)
    return jnp.concatenate([high, low, high], axis=0)


def ortho_body(heads, slots, *refs):
    place = position()
    matrix = lax.rem(place[0] - first_owner(place[1]) + slots, slots)
    owner = (place[1] < heads) & (matrix < 3)

    @pl.when(owner)
    def _():
        orthogonalize(refs[:-1], refs[-1])

    @pl.when(jnp.logical_not(owner))
    def _():
        refs[-1][...] = jnp.zeros(refs[-1].shape, refs[-1].dtype)


def orthogonalize(parts, out):
    grads = parts[0][...].astype(f32)
    for part in parts[1:]:
        grads = grads + part[...].astype(f32)
    eye = (
        lax.broadcasted_iota(jnp.int32, (HD, HD), 0) == lax.broadcasted_iota(jnp.int32, (HD, HD), 1)
    ).astype(f32)
    both = jnp.concatenate(parts_of(grads), axis=1)
    blocks = dot(both, both, (0, 0))
    raw = (blocks[:HD, HD:] + blocks[HD:, :HD]) + blocks[:HD, :HD]
    square = jnp.sum(jnp.sum(raw * eye, axis=0, keepdims=True), axis=1, keepdims=True)
    scale = lax.rsqrt(square + epsilon)
    gram = raw * scale * scale
    total = None
    for step in range(NS_STEPS):
        square_gram = dot(left_of(gram), right_of(gram), (1, 0))
        mix = quintic_a * eye + quintic_b * gram + quintic_c * square_gram
        right = right_of(mix)
        if step < NS_STEPS - 1:
            gram = dot(left_of(dot(left_of(gram), right, (1, 0))), right, (1, 0))
            total = mix if total is None else dot(left_of(total), right, (1, 0))
    ortho = dot(left_of(grads * scale), right_of(total), (1, 0))
    out[...] = dot(left_of(ortho), right, (1, 0)).astype(out.dtype)


def finish_body(slots, group, w_ref, rows_ref, out):
    heads = w_ref.shape[1]
    for m in range(3):
        for h in range(heads):
            weights = w_ref[m, h]
            summed = weights + rows_ref[index_of((m + first_owner(h)) % slots, h, slots)].astype(f32)
            old = jnp.sqrt(jnp.sum(weights * weights, axis=1, keepdims=True))
            new = lax.rsqrt(jnp.sum(summed * summed, axis=1, keepdims=True) + epsilon)
            out[m, h] = summed * (old * new)


def attend_body(heads, tokens, q_ref, own_ref, back_ref, out):
    padded = own_ref.shape[0]
    span = heads * HD
    column = lax.broadcasted_iota(jnp.int32, (1, 2 * padded), 1)
    place = position()
    first = (place[0] == 0) & (place[1] == 0)
    stop = jnp.where(first, padded, padded + tokens)
    live = (column < tokens) | ((column >= padded) & (column < stop))
    for h in range(heads):
        cols = slice(h * HD, (h + 1) * HD)
        key = jnp.concatenate([own_ref[:, cols], back_ref[:, cols]], axis=0)
        vcols = slice(span + h * HD, span + (h + 1) * HD)
        value = jnp.concatenate([own_ref[:, vcols], back_ref[:, vcols]], axis=0)
        scores = dot(q_ref[:, cols], key, (1, 1)) * (HD ** (-0.5))
        scores = jnp.where(live, scores, -1e30)
        weights = jnp.exp(scores - jnp.max(scores, axis=1, keepdims=True))
        probs = (weights / jnp.sum(weights, axis=1, keepdims=True)).astype(bf16)
        out[:, cols] = dot(probs, value, (1, 0))


def assemble_body(heads, slots, out, squares):
    for h in range(heads):
        out[:, h * HD : (h + 1) * HD] = slots[h]
    fast = out[...].astype(f32)
    squares[...] = dot(jnp.ones((8, heads * HD), f32), fast * fast, (1, 1), highest)


def block_body(features, gain_ref, attended_ref, fast_ref, *refs):
    squares, out = refs[:-1], refs[-1]
    total = squares[0][...]
    for other in squares[1:]:
        total = total + other[...]
    pick = (lax.broadcasted_iota(jnp.int32, (8, HD), 0) == 0).astype(f32)
    spread = dot(total, pick, (0, 0), highest) * (1.0 / features)
    scale = lax.rsqrt(spread + epsilon)
    for h in range(fast_ref.shape[1] // HD):
        cols = slice(h * HD, (h + 1) * HD)
        out[:, cols] = (
            attended_ref[:, cols] + fast_ref[:, cols].astype(f32) * gain_ref[:, cols] * scale
        ).astype(bf16)


def on_device(queries, keys, values, rates, frame_update, fast_weights, gain):
    tokens = queries.shape[0]
    heads = queries.shape[1] // HD
    rows_local = fast_weights.shape[2]
    group, nh = GROUP, lax.axis_size("head")
    nz = lax.axis_size("ctx") // group
    count = nz * group
    hidden = count * rows_local
    padded = -(-tokens // 16) * 16
    span = heads * HD

    def whole(*shape):
        return pl.BlockSpec(shape, lambda i: (0,) * len(shape))

    low_shape = (count, 3, rows_local, HD)
    low = call(
        functools.partial(cast_body, heads, group), sds(low_shape, bf16), flops=1e6
    )(fast_weights)
    prepared = pl.pallas_call(
        functools.partial(prep_body, heads, group, tokens),
        grid=(1,),
        out_shape=[sds((padded, 2 * span), bf16)]
        + [sds((tokens, 3 * HD), bf16)] * group,
        in_specs=[pl.BlockSpec(memory_space=pl.ANY), whole(1, 1)]
        + [whole(heads, -(-padded // 128) * 128)]
        + [whole(padded, span)] * 3,
        out_specs=[whole(padded, 2 * span)] + [whole(tokens, 3 * HD)] * group,
        scratch_shapes=[pltpu.VMEM((padded, span), bf16)],
        compiler_params=pltpu.CompilerParams(vmem_limit_bytes=VMEM_LIMIT),
    )(low, frame_update.reshape(1, 1), rates.T, keys, values, queries)
    kv_own, *token_slots = prepared

    weights = lax.all_to_all(low, "ctx", 0, 0, tiled=True, axis_index_groups=[listed(nz)])
    if rows_local % 16:
        weights = weights.transpose(1, 0, 2, 3).reshape(3, hidden, HD)
    for d in served(group)[1:]:
        pairs = [(s, s ^ d) for s in range(count) if (s ^ d) % group < heads]
        token_slots[d] = lax.ppermute(token_slots[d], "ctx", pairs)

    last = group // 2
    early_slots = [d for d in served(group) if d != last]
    early_grads, early_fast = call(
        functools.partial(early_body, len(early_slots)),
        [sds((3, hidden, HD), f32), sds((len(early_slots), padded, HD), bf16)],
        scratch=gradient_scratch(len(early_slots), padded, hidden) + apply_scratch(padded, hidden),
        flops=1e9,
    )(*(token_slots[d] for d in early_slots), weights)
    partials = list(
        call(
            functools.partial(late_body, group, nz),
            [sds((hidden, HD), bf16)] * nz,
            scratch=[pltpu.VMEM((3, hidden, HD), bf16)] + gradient_scratch(1, padded, hidden),
            flops=5e8,
        )(token_slots[last], weights, early_grads)
    )
    weights, partials[0] = lax.optimization_barrier((weights, partials[0]))
    for d in served(nz)[1:]:
        pairs = []
        for z in range(nz):
            pairs += [
                (z * group + j, (z ^ d) * group + j)
                for j in range(heads)
                if ((z ^ d) - first_owner(j)) % nz < 3
            ]
        partials[d] = lax.ppermute(partials[d], "ctx", pairs)

    fast_slots = call(
        functools.partial(late_apply_body, early_slots, last),
        sds((group, padded, HD), bf16),
        scratch=apply_scratch(padded, hidden),
        flops=1e3,
        moved=1024,
    )(token_slots[last], weights, early_fast)
    kv_own, partials[0], fast_slots = lax.optimization_barrier((kv_own, partials[0], fast_slots))
    fast_slots = lax.all_to_all(
        fast_slots, "ctx", 0, 0, tiled=True,
        axis_index_groups=[[z * group + j for j in range(group)] for z in range(nz)],
    )

    ring = [(i, i + 1) for i in range(count - 1)]
    kv_back = lax.ppermute(kv_own, "ctx", ring)

    ortho = call(functools.partial(ortho_body, heads, nz), sds((hidden, HD), bf16), flops=1e9)(
        *(partials[d] for d in served(nz))
    )
    queries, ortho = lax.optimization_barrier((queries, ortho))
    rows = lax.all_to_all(
        ortho.reshape(count, rows_local, HD), "ctx", 0, 0, tiled=True,
        axis_index_groups=[listed(nz)],
    )
    new_weights = call(
        functools.partial(finish_body, nz, group), sds(fast_weights.shape, f32), flops=1e6
    )(fast_weights, rows)

    attended = pl.pallas_call(
        functools.partial(attend_body, heads, tokens),
        grid=(1,),
        out_shape=sds((padded, span), f32),
        in_specs=[whole(padded, span)] + [whole(padded, 2 * span)] * 2,
        out_specs=whole(padded, span),
        compiler_params=pltpu.CompilerParams(vmem_limit_bytes=VMEM_LIMIT),
    )(queries, kv_own, kv_back)
    fast, squares = call(
        functools.partial(assemble_body, heads),
        [sds((padded, span), bf16), sds((8, padded), f32)],
        flops=1e7,
    )(fast_slots)
    all_squares = [squares] + [
        lax.ppermute(squares, "head", [(s, (s + d) % nh) for s in range(nh)]) for d in range(1, nh)
    ]
    block_out = pl.pallas_call(
        functools.partial(block_body, span * nh),
        grid=(1,),
        out_shape=sds((tokens, span), bf16),
        in_specs=[whole(1, span), whole(padded, span), whole(padded, span)]
        + [whole(8, padded)] * nh,
        out_specs=whole(padded, span),
        compiler_params=pltpu.CompilerParams(vmem_limit_bytes=VMEM_LIMIT),
    )(gain.reshape(1, span), attended, fast, *all_squares)
    return (block_out, new_weights)


def solution(mesh):
    placed = (
        P("ctx", "head"),
        P("ctx", "head"),
        P("ctx", "head"),
        P("ctx", "head"),
        P("ctx"),
        P(None, "head", "ctx", None),
        P("head"),
    )
    return jax.shard_map(
        on_device,
        mesh=mesh,
        in_specs=placed,
        out_specs=(P("ctx", "head"), P(None, "head", "ctx", None)),
        check_vma=False,
    )
```

```python
import functools

import jax
import jax.numpy as jnp
from jax import lax
from jax.experimental import pallas as pl
from jax.experimental.pallas import tpu as pltpu
from jax.sharding import PartitionSpec as P

HD = 128
NS_STEPS = 5

epsilon = 1e-06
quintic_a = 3.4445
quintic_b = -4.775
quintic_c = 2.0315
highest = lax.Precision.HIGHEST
f32 = jnp.float32
bf16 = jnp.bfloat16
VMEM_LIMIT = 24 * 1024 * 1024


def dot(a, b, contract, precision=None):
    return lax.dot_general(
        a, b, ((contract[:1], contract[1:]), ((), ())),
        precision=precision, preferred_element_type=f32,
    )


def call(body, outs, scratch=(), in_specs=None, flops=1e8, moved=1 << 20, **kw):
    given = {} if in_specs is None else {"in_specs": in_specs}
    return pl.pallas_call(
        body,
        out_shape=outs,
        **given,
        scratch_shapes=list(scratch),
        compiler_params=pltpu.CompilerParams(vmem_limit_bytes=VMEM_LIMIT),
        cost_estimate=pl.CostEstimate(flops=int(flops), bytes_accessed=moved, transcendentals=0),
        **kw,
    )


def sds(shape, dtype):
    return jax.ShapeDtypeStruct(shape, dtype)


def served(n):
    return [0] + list(range(n - 1, 0, -1))


def first_owner(h):
    return h & 1


GROUP = 4


def position():
    return lax.axis_index("ctx") // GROUP, lax.axis_index("ctx") % GROUP


def index_of(z, j, slots):
    return (slots // 2 - 1 - z) % slots * GROUP + j


def listed(slots):
    return [(slots // 2 - 1 - i) % slots * GROUP + j for i in range(slots) for j in range(GROUP)]


def sigmoid(x):
    return 0.5 * jnp.tanh(0.5 * x) + 0.5


def cast_body(heads, group, w_ref, w_out):
    slots = w_out.shape[0] // group
    for j in range(group):
        for m in range(3):
            low = w_ref[m, min(j, heads - 1)].astype(bf16)
            for z in range(slots):
                w_out[index_of(z, j, slots), m] = low


def prep_body(
    heads, group, tokens, after, update, rate_ref, k_ref, v_ref, q_ref, kv_out, *outs
):
    token_outs, targets = outs[:-1], outs[-1]
    padded = kv_out.shape[0]
    place = position()
    valid = lax.broadcasted_iota(jnp.int32, (padded, 1), 0) < tokens
    none = jnp.zeros((), bf16)
    keep = update[...].astype(f32)
    lane_head = lax.broadcasted_iota(jnp.int32, (heads, heads * HD), 1) // HD
    row = lax.broadcasted_iota(jnp.int32, (heads, heads * HD), 0)
    rate = dot(rate_ref[...], (row == lane_head).astype(f32), (0, 0), highest)[:padded]
    targets[...] = ((rate * keep) * v_ref[...].astype(f32)).astype(bf16)
    for d in range(group):
        head = jnp.minimum(place[1] ^ d, heads - 1)
        cols = pl.ds(pl.multiple_of(head * HD, HD), HD)
        for i, source in enumerate((k_ref, targets, q_ref)):
            token_outs[d][:, i * HD : (i + 1) * HD] = source[:tokens, cols]
    kv_out[:, : heads * HD] = jnp.where(valid, k_ref[...], none)
    kv_out[:, heads * HD :] = jnp.where(valid, v_ref[...], none)


def gradients(token_refs, w_ref, k_all, t_all, staged, deltas):
    tokens = token_refs[0].shape[0]
    padded = -(-tokens // 16) * 16
    width = k_all.shape[0]
    filled = len(token_refs) * padded
    for i, ref in enumerate(token_refs):
        for part, rows in enumerate((k_all, t_all)):
            rows[(i + 1) * padded - 16 : (i + 1) * padded] = jnp.zeros((16, HD), bf16)
            rows[i * padded : i * padded + tokens] = ref[:, part * HD : (part + 1) * HD]
    if width > filled:
        k_all[filled:] = jnp.zeros((width - filled, HD), bf16)
        t_all[filled:] = jnp.zeros((width - filled, HD), bf16)
    hidden = deltas.shape[1]
    w1, w3, w2 = (weight_rows(w_ref, m, 0, hidden) for m in range(3))
    tall = 64
    for left in range(0, width, staged.shape[3]):
        right = min(left + staged.shape[3], width)
        cols, used = slice(left, right), slice(0, right - left)
        stage = staged.at[(left // staged.shape[3]) % staged.shape[0]]
        stage[0, :, used] = dot(w1, k_all[cols], (1, 1))
        stage[1, :, used] = dot(w3, k_all[cols], (1, 1))
        stage[2, :, used] = dot(w2, t_all[cols], (1, 1))
        for start in range(0, hidden, tall):
            rows = slice(start, start + tall)
            pre_one, pre_three, back = (stage[i, rows, used] for i in range(3))
            sig = sigmoid(pre_one)
            gate = pre_one * sig
            deltas[2, rows, cols] = (gate * pre_three).astype(bf16)
            deltas[1, rows, cols] = (back * gate).astype(bf16)
            deltas[0, rows, cols] = (
                (back * pre_three) * (sig * (1.0 + pre_one * (1.0 - sig)))
            ).astype(bf16)
    return (
        dot(deltas[0], k_all[...], (1, 0)),
        dot(deltas[1], k_all[...], (1, 0)),
        dot(deltas[2], t_all[...], (1, 0)),
    )


def gradient_scratch(slots, padded, hidden):
    width = -(-slots * padded // 128) * 128
    return [
        pltpu.VMEM((width, HD), bf16),
        pltpu.VMEM((width, HD), bf16),
        pltpu.VMEM((2, 3, hidden, 256), f32),
        pltpu.VMEM((3, hidden, width), bf16),
    ]


def apply_tokens(token_ref, w_ref, stage, act, held):
    hidden = act.shape[1]
    tall = 16
    w1, w3, w2 = (weight_rows(w_ref, m, 0, hidden) for m in range(3))
    held[held.shape[0] - 16 :] = jnp.zeros((16, HD), bf16)
    held[: token_ref.shape[0]] = token_ref[:, 2 * HD :]
    query = held[...]
    stage[0] = dot(query, w1, (1, 1))
    stage[1] = dot(query, w3, (1, 1))
    for start in range(0, query.shape[0], tall):
        rows = slice(start, start + tall)
        proj = stage[0, rows]
        act[rows] = (proj * sigmoid(proj) * stage[1, rows]).astype(bf16)
    return dot(act[...], w2, (1, 0)).astype(bf16)


def apply_scratch(padded, hidden):
    return [
        pltpu.VMEM((2, 2, padded, hidden), f32),
        pltpu.VMEM((2, padded, hidden), bf16),
        pltpu.VMEM((2, padded, HD), bf16),
    ]


def early_body(count, *refs):
    token_refs, w_ref = refs[:count], refs[count]
    grads, fast = refs[count + 1 : count + 3]
    scratch, (staged, acts, held) = refs[count + 3 : -3], refs[-3:]
    for m, grad in enumerate(gradients(token_refs, w_ref, *scratch)):
        grads[m] = grad
    for i, ref in enumerate(token_refs):
        fast[i] = apply_tokens(ref, w_ref, *(buffer.at[i % 2] for buffer in (staged, acts, held)))


def late_body(group, slots, token_ref, w_ref, early, *refs):
    place = position()
    outs, sums, scratch = refs[:slots], refs[slots], refs[slots + 1 :]
    for m, grad in enumerate(gradients([token_ref], w_ref, *scratch)):
        sums[m] = (early[m] + grad).astype(bf16)
    for d in range(slots):
        matrix = lax.rem((place[0] ^ d) - first_owner(place[1]) + slots, slots)
        chosen = sums[jnp.minimum(matrix, 2)]
        outs[d][...] = jnp.where(matrix < 3, chosen, jnp.zeros_like(chosen))


def late_apply_body(early_slots, last, token_ref, w_ref, early, out, staged, acts, held):
    place = position()
    for i, d in enumerate(early_slots):
        out[place[1] ^ d] = early[i]
    out[place[1] ^ last] = apply_tokens(
        token_ref, w_ref, staged.at[0], acts.at[0], held.at[0]
    )


def weight_rows(w_ref, m, start, block):
    if len(w_ref.shape) == 3:
        return w_ref[m, start : start + block]
    rows = w_ref.shape[2]
    return w_ref[start // rows : (start + block) // rows, m].reshape(block, HD)


def parts_of(x):
    high = x.astype(bf16)
    return high, (x - high.astype(f32)).astype(bf16)


def left_of(x):
    high, low = parts_of(x)
    return jnp.concatenate([high, high, low], axis=1)


def right_of(x):
    high, low = parts_of(x)
    return jnp.concatenate([high, low, high], axis=0)


def ortho_body(heads, slots, *refs):
    place = position()
    matrix = lax.rem(place[0] - first_owner(place[1]) + slots, slots)
    owner = (place[1] < heads) & (matrix < 3)

    @pl.when(owner)
    def _():
        orthogonalize(refs[:-1], refs[-1])

    @pl.when(jnp.logical_not(owner))
    def _():
        refs[-1][...] = jnp.zeros(refs[-1].shape, refs[-1].dtype)


def orthogonalize(parts, out):
    grads = parts[0][...].astype(f32)
    for part in parts[1:]:
        grads = grads + part[...].astype(f32)
    eye = (
        lax.broadcasted_iota(jnp.int32, (HD, HD), 0) == lax.broadcasted_iota(jnp.int32, (HD, HD), 1)
    ).astype(f32)
    both = jnp.concatenate(parts_of(grads), axis=1)
    blocks = dot(both, both, (0, 0))
    raw = (blocks[:HD, HD:] + blocks[HD:, :HD]) + blocks[:HD, :HD]
    square = jnp.sum(jnp.sum(raw * eye, axis=0, keepdims=True), axis=1, keepdims=True)
    scale = lax.rsqrt(square + epsilon)
    gram = raw * scale * scale
    total = None
    for step in range(NS_STEPS):
        square_gram = dot(left_of(gram), right_of(gram), (1, 0))
        mix = quintic_a * eye + quintic_b * gram + quintic_c * square_gram
        right = right_of(mix)
        if step < NS_STEPS - 1:
            gram = dot(left_of(dot(left_of(gram), right, (1, 0))), right, (1, 0))
            total = mix if total is None else dot(left_of(total), right, (1, 0))
    ortho = dot(left_of(grads * scale), right_of(total), (1, 0))
    out[...] = dot(left_of(ortho), right, (1, 0)).astype(out.dtype)


def finish_body(slots, group, w_ref, rows_ref, out):
    heads = w_ref.shape[1]
    for m in range(3):
        for h in range(heads):
            weights = w_ref[m, h]
            summed = weights + rows_ref[index_of((m + first_owner(h)) % slots, h, slots)].astype(f32)
            old = jnp.sqrt(jnp.sum(weights * weights, axis=1, keepdims=True))
            new = lax.rsqrt(jnp.sum(summed * summed, axis=1, keepdims=True) + epsilon)
            out[m, h] = summed * (old * new)


def attend_body(heads, tokens, q_ref, own_ref, back_ref, out):
    padded = own_ref.shape[0]
    span = heads * HD
    column = lax.broadcasted_iota(jnp.int32, (1, 2 * padded), 1)
    place = position()
    first = (place[0] == 0) & (place[1] == 0)
    stop = jnp.where(first, padded, padded + tokens)
    live = (column < tokens) | ((column >= padded) & (column < stop))
    for h in range(heads):
        cols = slice(h * HD, (h + 1) * HD)
        key = jnp.concatenate([own_ref[:, cols], back_ref[:, cols]], axis=0)
        vcols = slice(span + h * HD, span + (h + 1) * HD)
        value = jnp.concatenate([own_ref[:, vcols], back_ref[:, vcols]], axis=0)
        scores = dot(q_ref[:, cols], key, (1, 1)) * (HD ** (-0.5))
        scores = jnp.where(live, scores, -1e30)
        weights = jnp.exp(scores - jnp.max(scores, axis=1, keepdims=True))
        probs = (weights / jnp.sum(weights, axis=1, keepdims=True)).astype(bf16)
        out[:, cols] = dot(probs, value, (1, 0))


def assemble_body(heads, slots, out, squares):
    for h in range(heads):
        out[:, h * HD : (h + 1) * HD] = slots[h]
    fast = out[...].astype(f32)
    squares[...] = dot(jnp.ones((8, heads * HD), f32), fast * fast, (1, 1), highest)


def block_body(features, gain_ref, attended_ref, fast_ref, *refs):
    squares, out = refs[:-1], refs[-1]
    total = squares[0][...]
    for other in squares[1:]:
        total = total + other[...]
    pick = (lax.broadcasted_iota(jnp.int32, (8, HD), 0) == 0).astype(f32)
    spread = dot(total, pick, (0, 0), highest) * (1.0 / features)
    scale = lax.rsqrt(spread + epsilon)
    for h in range(fast_ref.shape[1] // HD):
        cols = slice(h * HD, (h + 1) * HD)
        out[:, cols] = (
            attended_ref[:, cols] + fast_ref[:, cols].astype(f32) * gain_ref[:, cols] * scale
        ).astype(bf16)


def on_device(queries, keys, values, rates, frame_update, fast_weights, gain):
    tokens = queries.shape[0]
    heads = queries.shape[1] // HD
    rows_local = fast_weights.shape[2]
    group, nh = GROUP, lax.axis_size("head")
    nz = lax.axis_size("ctx") // group
    count = nz * group
    hidden = count * rows_local
    padded = -(-tokens // 16) * 16
    span = heads * HD

    def whole(*shape):
        return pl.BlockSpec(shape, lambda i: (0,) * len(shape))

    low_shape = (count, 3, rows_local, HD)
    low = call(
        functools.partial(cast_body, heads, group), sds(low_shape, bf16), flops=1e6
    )(fast_weights)
    prepared = pl.pallas_call(
        functools.partial(prep_body, heads, group, tokens),
        grid=(1,),
        out_shape=[sds((padded, 2 * span), bf16)]
        + [sds((tokens, 3 * HD), bf16)] * group,
        in_specs=[pl.BlockSpec(memory_space=pl.ANY), whole(1, 1)]
        + [whole(heads, -(-padded // 128) * 128)]
        + [whole(padded, span)] * 3,
        out_specs=[whole(padded, 2 * span)] + [whole(tokens, 3 * HD)] * group,
        scratch_shapes=[pltpu.VMEM((padded, span), bf16)],
        compiler_params=pltpu.CompilerParams(vmem_limit_bytes=VMEM_LIMIT),
    )(low, frame_update.reshape(1, 1), rates.T, keys, values, queries)
    kv_own, *token_slots = prepared

    weights = lax.all_to_all(low, "ctx", 0, 0, tiled=True, axis_index_groups=[listed(nz)])
    if rows_local % 16:
        weights = weights.transpose(1, 0, 2, 3).reshape(3, hidden, HD)
    for d in served(group)[1:]:
        pairs = [(s, s ^ d) for s in range(count) if (s ^ d) % group < heads]
        token_slots[d] = lax.ppermute(token_slots[d], "ctx", pairs)

    last = group // 2
    early_slots = [d for d in served(group) if d != last]
    early_grads, early_fast = call(
        functools.partial(early_body, len(early_slots)),
        [sds((3, hidden, HD), f32), sds((len(early_slots), padded, HD), bf16)],
        scratch=gradient_scratch(len(early_slots), padded, hidden) + apply_scratch(padded, hidden),
        flops=1e9,
    )(*(token_slots[d] for d in early_slots), weights)
    partials = list(
        call(
            functools.partial(late_body, group, nz),
            [sds((hidden, HD), bf16)] * nz,
            scratch=[pltpu.VMEM((3, hidden, HD), bf16)] + gradient_scratch(1, padded, hidden),
            flops=5e8,
        )(token_slots[last], weights, early_grads)
    )
    weights, partials[0] = lax.optimization_barrier((weights, partials[0]))
    for d in served(nz)[1:]:
        pairs = []
        for z in range(nz):
            pairs += [
                (z * group + j, (z ^ d) * group + j)
                for j in range(heads)
                if ((z ^ d) - first_owner(j)) % nz < 3
            ]
        partials[d] = lax.ppermute(partials[d], "ctx", pairs)

    fast_slots = call(
        functools.partial(late_apply_body, early_slots, last),
        sds((group, padded, HD), bf16),
        scratch=apply_scratch(padded, hidden),
        flops=1e3,
        moved=1024,
    )(token_slots[last], weights, early_fast)
    kv_own, partials[0], fast_slots = lax.optimization_barrier((kv_own, partials[0], fast_slots))
    fast_slots = lax.all_to_all(
        fast_slots, "ctx", 0, 0, tiled=True,
        axis_index_groups=[[z * group + j for j in range(group)] for z in range(nz)],
    )

    ring = [(i, i + 1) for i in range(count - 1)]
    kv_back = lax.ppermute(kv_own, "ctx", ring)

    ortho = call(functools.partial(ortho_body, heads, nz), sds((hidden, HD), bf16), flops=1e9)(
        *(partials[d] for d in served(nz))
    )
    queries, ortho = lax.optimization_barrier((queries, ortho))
    rows = lax.all_to_all(
        ortho.reshape(count, rows_local, HD), "ctx", 0, 0, tiled=True,
        axis_index_groups=[listed(nz)],
    )
    new_weights = call(
        functools.partial(finish_body, nz, group), sds(fast_weights.shape, f32), flops=1e6
    )(fast_weights, rows)

    attended = pl.pallas_call(
        functools.partial(attend_body, heads, tokens),
        grid=(1,),
        out_shape=sds((padded, span), f32),
        in_specs=[whole(padded, span)] + [whole(padded, 2 * span)] * 2,
        out_specs=whole(padded, span),
        compiler_params=pltpu.CompilerParams(vmem_limit_bytes=VMEM_LIMIT),
    )(queries, kv_own, kv_back)
    fast, squares = call(
        functools.partial(assemble_body, heads),
        [sds((padded, span), bf16), sds((8, padded), f32)],
        flops=1e7,
    )(fast_slots)
    all_squares = [squares] + [
        lax.ppermute(squares, "head", [(s, (s + d) % nh) for s in range(nh)]) for d in range(1, nh)
    ]
    block_out = pl.pallas_call(
        functools.partial(block_body, span * nh),
        grid=(1,),
        out_shape=sds((tokens, span), bf16),
        in_specs=[whole(1, span), whole(padded, span), whole(padded, span)]
        + [whole(8, padded)] * nh,
        out_specs=whole(padded, span),
        compiler_params=pltpu.CompilerParams(vmem_limit_bytes=VMEM_LIMIT),
    )(gain.reshape(1, span), attended, fast, *all_squares)
    return (block_out, new_weights)


def solution(mesh):
    placed = (
        P("ctx", "head"),
        P("ctx", "head"),
        P("ctx", "head"),
        P("ctx", "head"),
        P("ctx"),
        P(None, "head", "ctx", None),
        P("head"),
    )
    return jax.shard_map(
        on_device,
        mesh=mesh,
        in_specs=placed,
        out_specs=(P("ctx", "head"), P(None, "head", "ctx", None)),
        check_vma=False,
    )
```

```python
import functools

import jax
import jax.numpy as jnp
from jax import lax
from jax.experimental import pallas as pl
from jax.experimental.pallas import tpu as pltpu
from jax.sharding import PartitionSpec as P

HD = 128
NS_STEPS = 5

epsilon = 1e-06
quintic_a = 3.4445
quintic_b = -4.775
quintic_c = 2.0315
highest = lax.Precision.HIGHEST
f32 = jnp.float32
bf16 = jnp.bfloat16
VMEM_LIMIT = 24 * 1024 * 1024


def dot(a, b, contract, precision=None):
    return lax.dot_general(
        a, b, ((contract[:1], contract[1:]), ((), ())),
        precision=precision, preferred_element_type=f32,
    )


def call(body, outs, scratch=(), in_specs=None, flops=1e8, moved=1 << 20, **kw):
    given = {} if in_specs is None else {"in_specs": in_specs}
    return pl.pallas_call(
        body,
        out_shape=outs,
        **given,
        scratch_shapes=list(scratch),
        compiler_params=pltpu.CompilerParams(vmem_limit_bytes=VMEM_LIMIT),
        cost_estimate=pl.CostEstimate(flops=int(flops), bytes_accessed=moved, transcendentals=0),
        **kw,
    )


def sds(shape, dtype):
    return jax.ShapeDtypeStruct(shape, dtype)


def served(n):
    return [0] + list(range(n - 1, 0, -1))


def owner(m, h):
    return m + (h & 1) * min(m, 1)


def owned(z, h):
    odd = h & 1
    return jnp.where((odd == 1) & (z == 1), 3, z - odd * jnp.minimum(z, 1))


GROUP = 4


def position():
    return lax.axis_index("ctx") // GROUP, lax.axis_index("ctx") % GROUP


def index_of(z, j, slots):
    return (slots // 2 - 1 - z) % slots * GROUP + j


def listed(slots):
    return [(slots // 2 - 1 - i) % slots * GROUP + j for i in range(slots) for j in range(GROUP)]


def sigmoid(x):
    return 0.5 * jnp.tanh(0.5 * x) + 0.5


def cast_body(heads, group, w_ref, w_out):
    slots = w_out.shape[0] // group
    for j in range(group):
        for m in range(3):
            low = w_ref[m, min(j, heads - 1)].astype(bf16)
            for z in range(slots):
                w_out[index_of(z, j, slots), m] = low


def prep_body(
    heads, group, tokens, after, update, rate_ref, k_ref, v_ref, q_ref, kv_out, *outs
):
    token_outs, targets = outs[:-1], outs[-1]
    padded = kv_out.shape[0]
    place = position()
    valid = lax.broadcasted_iota(jnp.int32, (padded, 1), 0) < tokens
    none = jnp.zeros((), bf16)
    keep = update[...].astype(f32)
    lane_head = lax.broadcasted_iota(jnp.int32, (heads, heads * HD), 1) // HD
    row = lax.broadcasted_iota(jnp.int32, (heads, heads * HD), 0)
    rate = dot(rate_ref[...], (row == lane_head).astype(f32), (0, 0), highest)[:padded]
    targets[...] = ((rate * keep) * v_ref[...].astype(f32)).astype(bf16)
    for d in range(group):
        head = jnp.minimum(place[1] ^ d, heads - 1)
        cols = pl.ds(pl.multiple_of(head * HD, HD), HD)
        for i, source in enumerate((k_ref, targets, q_ref)):
            token_outs[d][:, i * HD : (i + 1) * HD] = source[:tokens, cols]
    kv_out[:, : heads * HD] = jnp.where(valid, k_ref[...], none)
    kv_out[:, heads * HD :] = jnp.where(valid, v_ref[...], none)


def gradients(token_refs, w_ref, k_all, t_all, staged, deltas):
    tokens = token_refs[0].shape[0]
    padded = -(-tokens // 16) * 16
    width = k_all.shape[0]
    filled = len(token_refs) * padded
    for i, ref in enumerate(token_refs):
        for part, rows in enumerate((k_all, t_all)):
            rows[(i + 1) * padded - 16 : (i + 1) * padded] = jnp.zeros((16, HD), bf16)
            rows[i * padded : i * padded + tokens] = ref[:, part * HD : (part + 1) * HD]
    if width > filled:
        k_all[filled:] = jnp.zeros((width - filled, HD), bf16)
        t_all[filled:] = jnp.zeros((width - filled, HD), bf16)
    hidden = deltas.shape[1]
    w1, w3, w2 = (weight_rows(w_ref, m, 0, hidden) for m in range(3))
    tall = 64
    for left in range(0, width, staged.shape[3]):
        right = min(left + staged.shape[3], width)
        cols, used = slice(left, right), slice(0, right - left)
        stage = staged.at[(left // staged.shape[3]) % staged.shape[0]]
        stage[0, :, used] = dot(w1, k_all[cols], (1, 1))
        stage[1, :, used] = dot(w3, k_all[cols], (1, 1))
        stage[2, :, used] = dot(w2, t_all[cols], (1, 1))
        for start in range(0, hidden, tall):
            rows = slice(start, start + tall)
            pre_one, pre_three, back = (stage[i, rows, used] for i in range(3))
            sig = sigmoid(pre_one)
            gate = pre_one * sig
            deltas[2, rows, cols] = (gate * pre_three).astype(bf16)
            deltas[1, rows, cols] = (back * gate).astype(bf16)
            deltas[0, rows, cols] = (
                (back * pre_three) * (sig * (1.0 + pre_one * (1.0 - sig)))
            ).astype(bf16)
    return (
        dot(deltas[0], k_all[...], (1, 0)),
        dot(deltas[1], k_all[...], (1, 0)),
        dot(deltas[2], t_all[...], (1, 0)),
    )


def gradient_scratch(slots, padded, hidden):
    width = -(-slots * padded // 128) * 128
    return [
        pltpu.VMEM((width, HD), bf16),
        pltpu.VMEM((width, HD), bf16),
        pltpu.VMEM((2, 3, hidden, 256), f32),
        pltpu.VMEM((3, hidden, width), bf16),
    ]


def apply_tokens(token_ref, w_ref, stage, act, held):
    hidden = act.shape[1]
    tall = 16
    w1, w3, w2 = (weight_rows(w_ref, m, 0, hidden) for m in range(3))
    held[held.shape[0] - 16 :] = jnp.zeros((16, HD), bf16)
    held[: token_ref.shape[0]] = token_ref[:, 2 * HD :]
    query = held[...]
    stage[0] = dot(query, w1, (1, 1))
    stage[1] = dot(query, w3, (1, 1))
    for start in range(0, query.shape[0], tall):
        rows = slice(start, start + tall)
        proj = stage[0, rows]
        act[rows] = (proj * sigmoid(proj) * stage[1, rows]).astype(bf16)
    return dot(act[...], w2, (1, 0)).astype(bf16)


def apply_scratch(padded, hidden):
    return [
        pltpu.VMEM((2, 2, padded, hidden), f32),
        pltpu.VMEM((2, padded, hidden), bf16),
        pltpu.VMEM((2, padded, HD), bf16),
    ]


def early_body(count, *refs):
    token_refs, w_ref = refs[:count], refs[count]
    grads, fast = refs[count + 1 : count + 3]
    scratch, (staged, acts, held) = refs[count + 3 : -3], refs[-3:]
    for m, grad in enumerate(gradients(token_refs, w_ref, *scratch)):
        grads[m] = grad
    for i, ref in enumerate(token_refs):
        fast[i] = apply_tokens(ref, w_ref, *(buffer.at[i % 2] for buffer in (staged, acts, held)))


def late_body(group, slots, token_ref, w_ref, early, *refs):
    place = position()
    outs, sums, scratch = refs[:slots], refs[slots], refs[slots + 1 :]
    for m, grad in enumerate(gradients([token_ref], w_ref, *scratch)):
        sums[m] = (early[m] + grad).astype(bf16)
    for d in range(slots):
        matrix = owned(place[0] ^ d, place[1])
        chosen = sums[jnp.minimum(matrix, 2)]
        outs[d][...] = jnp.where(matrix < 3, chosen, jnp.zeros_like(chosen))


def late_apply_body(early_slots, last, token_ref, w_ref, early, out, staged, acts, held):
    place = position()
    for i, d in enumerate(early_slots):
        out[place[1] ^ d] = early[i]
    out[place[1] ^ last] = apply_tokens(
        token_ref, w_ref, staged.at[0], acts.at[0], held.at[0]
    )


def weight_rows(w_ref, m, start, block):
    if len(w_ref.shape) == 3:
        return w_ref[m, start : start + block]
    rows = w_ref.shape[2]
    return w_ref[start // rows : (start + block) // rows, m].reshape(block, HD)


def parts_of(x):
    high = x.astype(bf16)
    return high, (x - high.astype(f32)).astype(bf16)


def left_of(x):
    high, low = parts_of(x)
    return jnp.concatenate([high, high, low], axis=1)


def right_of(x):
    high, low = parts_of(x)
    return jnp.concatenate([high, low, high], axis=0)


def ortho_body(heads, *refs):
    place = position()
    busy = (place[1] < heads) & (owned(*place) < 3)

    @pl.when(busy)
    def _():
        orthogonalize(refs[:-1], refs[-1])

    @pl.when(jnp.logical_not(busy))
    def _():
        refs[-1][...] = jnp.zeros(refs[-1].shape, refs[-1].dtype)


def orthogonalize(parts, out):
    grads = parts[0][...].astype(f32)
    for part in parts[1:]:
        grads = grads + part[...].astype(f32)
    eye = (
        lax.broadcasted_iota(jnp.int32, (HD, HD), 0) == lax.broadcasted_iota(jnp.int32, (HD, HD), 1)
    ).astype(f32)
    both = jnp.concatenate(parts_of(grads), axis=1)
    blocks = dot(both, both, (0, 0))
    raw = (blocks[:HD, HD:] + blocks[HD:, :HD]) + blocks[:HD, :HD]
    square = jnp.sum(jnp.sum(raw * eye, axis=0, keepdims=True), axis=1, keepdims=True)
    scale = lax.rsqrt(square + epsilon)
    gram = raw * scale * scale
    total = None
    for step in range(NS_STEPS):
        square_gram = dot(left_of(gram), right_of(gram), (1, 0))
        mix = quintic_a * eye + quintic_b * gram + quintic_c * square_gram
        right = right_of(mix)
        if step < NS_STEPS - 1:
            gram = dot(left_of(dot(left_of(gram), right, (1, 0))), right, (1, 0))
            total = mix if total is None else dot(left_of(total), right, (1, 0))
    ortho = dot(left_of(grads * scale), right_of(total), (1, 0))
    out[...] = dot(left_of(ortho), right, (1, 0)).astype(out.dtype)


def finish_body(slots, group, w_ref, rows_ref, out):
    heads = w_ref.shape[1]
    for m in range(3):
        for h in range(heads):
            weights = w_ref[m, h]
            summed = weights + rows_ref[index_of(owner(m, h), h, slots)].astype(f32)
            old = jnp.sqrt(jnp.sum(weights * weights, axis=1, keepdims=True))
            new = lax.rsqrt(jnp.sum(summed * summed, axis=1, keepdims=True) + epsilon)
            out[m, h] = summed * (old * new)


def attend_body(heads, tokens, q_ref, own_ref, back_ref, out):
    padded = own_ref.shape[0]
    span = heads * HD
    column = lax.broadcasted_iota(jnp.int32, (1, 2 * padded), 1)
    place = position()
    first = (place[0] == 0) & (place[1] == 0)
    stop = jnp.where(first, padded, padded + tokens)
    live = (column < tokens) | ((column >= padded) & (column < stop))
    for h in range(heads):
        cols = slice(h * HD, (h + 1) * HD)
        key = jnp.concatenate([own_ref[:, cols], back_ref[:, cols]], axis=0)
        vcols = slice(span + h * HD, span + (h + 1) * HD)
        value = jnp.concatenate([own_ref[:, vcols], back_ref[:, vcols]], axis=0)
        scores = dot(q_ref[:, cols], key, (1, 1)) * (HD ** (-0.5))
        scores = jnp.where(live, scores, -1e30)
        weights = jnp.exp(scores - jnp.max(scores, axis=1, keepdims=True))
        probs = (weights / jnp.sum(weights, axis=1, keepdims=True)).astype(bf16)
        out[:, cols] = dot(probs, value, (1, 0))


def assemble_body(heads, slots, out, squares):
    for h in range(heads):
        out[:, h * HD : (h + 1) * HD] = slots[h]
    fast = out[...].astype(f32)
    squares[...] = dot(jnp.ones((8, heads * HD), f32), fast * fast, (1, 1), highest)


def block_body(features, gain_ref, attended_ref, fast_ref, *refs):
    squares, out = refs[:-1], refs[-1]
    total = squares[0][...]
    for other in squares[1:]:
        total = total + other[...]
    pick = (lax.broadcasted_iota(jnp.int32, (8, HD), 0) == 0).astype(f32)
    spread = dot(total, pick, (0, 0), highest) * (1.0 / features)
    scale = lax.rsqrt(spread + epsilon)
    for h in range(fast_ref.shape[1] // HD):
        cols = slice(h * HD, (h + 1) * HD)
        out[:, cols] = (
            attended_ref[:, cols] + fast_ref[:, cols].astype(f32) * gain_ref[:, cols] * scale
        ).astype(bf16)


def on_device(queries, keys, values, rates, frame_update, fast_weights, gain):
    tokens = queries.shape[0]
    heads = queries.shape[1] // HD
    rows_local = fast_weights.shape[2]
    group, nh = GROUP, lax.axis_size("head")
    nz = lax.axis_size("ctx") // group
    count = nz * group
    hidden = count * rows_local
    padded = -(-tokens // 16) * 16
    span = heads * HD

    def whole(*shape):
        return pl.BlockSpec(shape, lambda i: (0,) * len(shape))

    low_shape = (count, 3, rows_local, HD)
    low = call(
        functools.partial(cast_body, heads, group), sds(low_shape, bf16), flops=1e6
    )(fast_weights)
    prepared = pl.pallas_call(
        functools.partial(prep_body, heads, group, tokens),
        grid=(1,),
        out_shape=[sds((padded, 2 * span), bf16)]
        + [sds((tokens, 3 * HD), bf16)] * group,
        in_specs=[pl.BlockSpec(memory_space=pl.ANY), whole(1, 1)]
        + [whole(heads, -(-padded // 128) * 128)]
        + [whole(padded, span)] * 3,
        out_specs=[whole(padded, 2 * span)] + [whole(tokens, 3 * HD)] * group,
        scratch_shapes=[pltpu.VMEM((padded, span), bf16)],
        compiler_params=pltpu.CompilerParams(vmem_limit_bytes=VMEM_LIMIT),
    )(low, frame_update.reshape(1, 1), rates.T, keys, values, queries)
    kv_own, *token_slots = prepared

    weights = lax.all_to_all(low, "ctx", 0, 0, tiled=True, axis_index_groups=[listed(nz)])
    if rows_local % 16:
        weights = weights.transpose(1, 0, 2, 3).reshape(3, hidden, HD)
    for d in served(group)[1:]:
        pairs = [(s, s ^ d) for s in range(count) if (s ^ d) % group < heads]
        token_slots[d] = lax.ppermute(token_slots[d], "ctx", pairs)

    last = group // 2
    early_slots = [d for d in served(group) if d != last]
    early_grads, early_fast = call(
        functools.partial(early_body, len(early_slots)),
        [sds((3, hidden, HD), f32), sds((len(early_slots), padded, HD), bf16)],
        scratch=gradient_scratch(len(early_slots), padded, hidden) + apply_scratch(padded, hidden),
        flops=1e9,
    )(*(token_slots[d] for d in early_slots), weights)
    partials = list(
        call(
            functools.partial(late_body, group, nz),
            [sds((hidden, HD), bf16)] * nz,
            scratch=[pltpu.VMEM((3, hidden, HD), bf16)] + gradient_scratch(1, padded, hidden),
            flops=5e8,
        )(token_slots[last], weights, early_grads)
    )
    weights, partials[0] = lax.optimization_barrier((weights, partials[0]))
    for d in served(nz)[1:]:
        pairs = []
        for z in range(nz):
            pairs += [
                (z * group + j, (z ^ d) * group + j)
                for j in range(heads)
                if (z ^ d) in [owner(m, j) for m in range(3)]
            ]
        partials[d] = lax.ppermute(partials[d], "ctx", pairs)

    fast_slots = call(
        functools.partial(late_apply_body, early_slots, last),
        sds((group, padded, HD), bf16),
        scratch=apply_scratch(padded, hidden),
        flops=1e3,
        moved=1024,
    )(token_slots[last], weights, early_fast)
    kv_own, partials[0], fast_slots = lax.optimization_barrier((kv_own, partials[0], fast_slots))
    fast_slots = lax.all_to_all(
        fast_slots, "ctx", 0, 0, tiled=True,
        axis_index_groups=[[z * group + j for j in range(group)] for z in range(nz)],
    )

    ring = [(i, i + 1) for i in range(count - 1)]
    kv_back = lax.ppermute(kv_own, "ctx", ring)

    ortho = call(functools.partial(ortho_body, heads), sds((hidden, HD), bf16), flops=1e9)(
        *(partials[d] for d in served(nz))
    )
    queries, ortho = lax.optimization_barrier((queries, ortho))
    rows = lax.all_to_all(
        ortho.reshape(count, rows_local, HD), "ctx", 0, 0, tiled=True,
        axis_index_groups=[listed(nz)],
    )
    new_weights = call(
        functools.partial(finish_body, nz, group), sds(fast_weights.shape, f32), flops=1e6
    )(fast_weights, rows)

    attended = pl.pallas_call(
        functools.partial(attend_body, heads, tokens),
        grid=(1,),
        out_shape=sds((padded, span), f32),
        in_specs=[whole(padded, span)] + [whole(padded, 2 * span)] * 2,
        out_specs=whole(padded, span),
        compiler_params=pltpu.CompilerParams(vmem_limit_bytes=VMEM_LIMIT),
    )(queries, kv_own, kv_back)
    fast, squares = call(
        functools.partial(assemble_body, heads),
        [sds((padded, span), bf16), sds((8, padded), f32)],
        flops=1e7,
    )(fast_slots)
    all_squares = [squares] + [
        lax.ppermute(squares, "head", [(s, (s + d) % nh) for s in range(nh)]) for d in range(1, nh)
    ]
    block_out = pl.pallas_call(
        functools.partial(block_body, span * nh),
        grid=(1,),
        out_shape=sds((tokens, span), bf16),
        in_specs=[whole(1, span), whole(padded, span), whole(padded, span)]
        + [whole(8, padded)] * nh,
        out_specs=whole(padded, span),
        compiler_params=pltpu.CompilerParams(vmem_limit_bytes=VMEM_LIMIT),
    )(gain.reshape(1, span), attended, fast, *all_squares)
    return (block_out, new_weights)


def solution(mesh):
    placed = (
        P("ctx", "head"),
        P("ctx", "head"),
        P("ctx", "head"),
        P("ctx", "head"),
        P("ctx"),
        P(None, "head", "ctx", None),
        P("head"),
    )
    return jax.shard_map(
        on_device,
        mesh=mesh,
        in_specs=placed,
        out_specs=(P("ctx", "head"), P(None, "head", "ctx", None)),
        check_vma=False,
    )
```

```python
import functools

import jax
import jax.numpy as jnp
from jax import lax
from jax.experimental import pallas as pl
from jax.experimental.pallas import tpu as pltpu
from jax.sharding import PartitionSpec as P

HD = 128
NS_STEPS = 5

epsilon = 1e-06
quintic_a = 3.4445
quintic_b = -4.775
quintic_c = 2.0315
highest = lax.Precision.HIGHEST
f32 = jnp.float32
bf16 = jnp.bfloat16
VMEM_LIMIT = 24 * 1024 * 1024


def dot(a, b, contract, precision=None):
    return lax.dot_general(
        a, b, ((contract[:1], contract[1:]), ((), ())),
        precision=precision, preferred_element_type=f32,
    )


def call(body, outs, scratch=(), in_specs=None, flops=1e8, moved=1 << 20, **kw):
    given = {} if in_specs is None else {"in_specs": in_specs}
    return pl.pallas_call(
        body,
        out_shape=outs,
        **given,
        scratch_shapes=list(scratch),
        compiler_params=pltpu.CompilerParams(vmem_limit_bytes=VMEM_LIMIT),
        cost_estimate=pl.CostEstimate(flops=int(flops), bytes_accessed=moved, transcendentals=0),
        **kw,
    )


def sds(shape, dtype):
    return jax.ShapeDtypeStruct(shape, dtype)


def served(n):
    return [0] + list(range(n - 1, 0, -1))


def first_owner(h):
    return h & 1


GROUP = 4


def position():
    return lax.axis_index("ctx") // GROUP, lax.axis_index("ctx") % GROUP


def index_of(z, j, slots):
    return (slots // 2 - z) % slots * GROUP + j


def listed(slots):
    return [(slots // 2 - i) % slots * GROUP + j for i in range(slots) for j in range(GROUP)]


def sigmoid(x):
    return 0.5 * jnp.tanh(0.5 * x) + 0.5


def cast_body(heads, group, w_ref, w_out):
    slots = w_out.shape[0] // group
    for j in range(group):
        for m in range(3):
            low = w_ref[m, min(j, heads - 1)].astype(bf16)
            for z in range(slots):
                w_out[index_of(z, j, slots), m] = low


def prep_body(
    heads, group, tokens, after, update, rate_ref, k_ref, v_ref, q_ref, kv_out, *outs
):
    token_outs, targets = outs[:-1], outs[-1]
    padded = kv_out.shape[0]
    place = position()
    valid = lax.broadcasted_iota(jnp.int32, (padded, 1), 0) < tokens
    none = jnp.zeros((), bf16)
    keep = update[...].astype(f32)
    lane_head = lax.broadcasted_iota(jnp.int32, (heads, heads * HD), 1) // HD
    row = lax.broadcasted_iota(jnp.int32, (heads, heads * HD), 0)
    rate = dot(rate_ref[...], (row == lane_head).astype(f32), (0, 0), highest)[:padded]
    targets[...] = ((rate * keep) * v_ref[...].astype(f32)).astype(bf16)
    for d in range(group):
        head = jnp.minimum(place[1] ^ d, heads - 1)
        cols = pl.ds(pl.multiple_of(head * HD, HD), HD)
        for i, source in enumerate((k_ref, targets, q_ref)):
            token_outs[d][:, i * HD : (i + 1) * HD] = source[:tokens, cols]
    kv_out[:, : heads * HD] = jnp.where(valid, k_ref[...], none)
    kv_out[:, heads * HD :] = jnp.where(valid, v_ref[...], none)


def gradients(token_refs, w_ref, k_all, t_all, staged, deltas):
    tokens = token_refs[0].shape[0]
    padded = -(-tokens // 16) * 16
    width = k_all.shape[0]
    filled = len(token_refs) * padded
    for i, ref in enumerate(token_refs):
        for part, rows in enumerate((k_all, t_all)):
            rows[(i + 1) * padded - 16 : (i + 1) * padded] = jnp.zeros((16, HD), bf16)
            rows[i * padded : i * padded + tokens] = ref[:, part * HD : (part + 1) * HD]
    if width > filled:
        k_all[filled:] = jnp.zeros((width - filled, HD), bf16)
        t_all[filled:] = jnp.zeros((width - filled, HD), bf16)
    hidden = deltas.shape[1]
    w1, w3, w2 = (weight_rows(w_ref, m, 0, hidden) for m in range(3))
    tall = 64
    for left in range(0, width, staged.shape[3]):
        right = min(left + staged.shape[3], width)
        cols, used = slice(left, right), slice(0, right - left)
        stage = staged.at[(left // staged.shape[3]) % staged.shape[0]]
        stage[0, :, used] = dot(w1, k_all[cols], (1, 1))
        stage[1, :, used] = dot(w3, k_all[cols], (1, 1))
        stage[2, :, used] = dot(w2, t_all[cols], (1, 1))
        for start in range(0, hidden, tall):
            rows = slice(start, start + tall)
            pre_one, pre_three, back = (stage[i, rows, used] for i in range(3))
            sig = sigmoid(pre_one)
            gate = pre_one * sig
            deltas[2, rows, cols] = (gate * pre_three).astype(bf16)
            deltas[1, rows, cols] = (back * gate).astype(bf16)
            deltas[0, rows, cols] = (
                (back * pre_three) * (sig * (1.0 + pre_one * (1.0 - sig)))
            ).astype(bf16)
    return (
        dot(deltas[0], k_all[...], (1, 0)),
        dot(deltas[1], k_all[...], (1, 0)),
        dot(deltas[2], t_all[...], (1, 0)),
    )


def gradient_scratch(slots, padded, hidden):
    width = -(-slots * padded // 128) * 128
    return [
        pltpu.VMEM((width, HD), bf16),
        pltpu.VMEM((width, HD), bf16),
        pltpu.VMEM((2, 3, hidden, 256), f32),
        pltpu.VMEM((3, hidden, width), bf16),
    ]


def apply_tokens(token_ref, w_ref, stage, act, held):
    hidden = act.shape[1]
    tall = 16
    w1, w3, w2 = (weight_rows(w_ref, m, 0, hidden) for m in range(3))
    held[held.shape[0] - 16 :] = jnp.zeros((16, HD), bf16)
    held[: token_ref.shape[0]] = token_ref[:, 2 * HD :]
    query = held[...]
    stage[0] = dot(query, w1, (1, 1))
    stage[1] = dot(query, w3, (1, 1))
    for start in range(0, query.shape[0], tall):
        rows = slice(start, start + tall)
        proj = stage[0, rows]
        act[rows] = (proj * sigmoid(proj) * stage[1, rows]).astype(bf16)
    return dot(act[...], w2, (1, 0)).astype(bf16)


def apply_scratch(padded, hidden):
    return [
        pltpu.VMEM((2, 2, padded, hidden), f32),
        pltpu.VMEM((2, padded, hidden), bf16),
        pltpu.VMEM((2, padded, HD), bf16),
    ]


def early_body(count, *refs):
    token_refs, w_ref = refs[:count], refs[count]
    grads, fast = refs[count + 1 : count + 3]
    scratch, (staged, acts, held) = refs[count + 3 : -3], refs[-3:]
    for m, grad in enumerate(gradients(token_refs, w_ref, *scratch)):
        grads[m] = grad
    for i, ref in enumerate(token_refs):
        fast[i] = apply_tokens(ref, w_ref, *(buffer.at[i % 2] for buffer in (staged, acts, held)))


def late_body(group, slots, token_ref, w_ref, early, *refs):
    place = position()
    outs, sums, scratch = refs[:slots], refs[slots], refs[slots + 1 :]
    for m, grad in enumerate(gradients([token_ref], w_ref, *scratch)):
        sums[m] = (early[m] + grad).astype(bf16)
    for d in range(slots):
        matrix = lax.rem((place[0] ^ d) - first_owner(place[1]) + slots, slots)
        chosen = sums[jnp.minimum(matrix, 2)]
        outs[d][...] = jnp.where(matrix < 3, chosen, jnp.zeros_like(chosen))


def late_apply_body(early_slots, last, token_ref, w_ref, early, out, staged, acts, held):
    place = position()
    for i, d in enumerate(early_slots):
        out[place[1] ^ d] = early[i]
    out[place[1] ^ last] = apply_tokens(
        token_ref, w_ref, staged.at[0], acts.at[0], held.at[0]
    )


def weight_rows(w_ref, m, start, block):
    if len(w_ref.shape) == 3:
        return w_ref[m, start : start + block]
    rows = w_ref.shape[2]
    return w_ref[start // rows : (start + block) // rows, m].reshape(block, HD)


def parts_of(x):
    high = x.astype(bf16)
    return high, (x - high.astype(f32)).astype(bf16)


def left_of(x):
    high, low = parts_of(x)
    return jnp.concatenate([high, high, low], axis=1)


def right_of(x):
    high, low = parts_of(x)
    return jnp.concatenate([high, low, high], axis=0)


def ortho_body(heads, slots, *refs):
    place = position()
    matrix = lax.rem(place[0] - first_owner(place[1]) + slots, slots)
    owner = (place[1] < heads) & (matrix < 3)

    @pl.when(owner)
    def _():
        orthogonalize(refs[:-1], refs[-1])

    @pl.when(jnp.logical_not(owner))
    def _():
        refs[-1][...] = jnp.zeros(refs[-1].shape, refs[-1].dtype)


def orthogonalize(parts, out):
    grads = parts[0][...].astype(f32)
    for part in parts[1:]:
        grads = grads + part[...].astype(f32)
    eye = (
        lax.broadcasted_iota(jnp.int32, (HD, HD), 0) == lax.broadcasted_iota(jnp.int32, (HD, HD), 1)
    ).astype(f32)
    both = jnp.concatenate(parts_of(grads), axis=1)
    blocks = dot(both, both, (0, 0))
    raw = (blocks[:HD, HD:] + blocks[HD:, :HD]) + blocks[:HD, :HD]
    square = jnp.sum(jnp.sum(raw * eye, axis=0, keepdims=True), axis=1, keepdims=True)
    scale = lax.rsqrt(square + epsilon)
    gram = raw * scale * scale
    total = None
    for step in range(NS_STEPS):
        square_gram = dot(left_of(gram), right_of(gram), (1, 0))
        mix = quintic_a * eye + quintic_b * gram + quintic_c * square_gram
        right = right_of(mix)
        if step < NS_STEPS - 1:
            gram = dot(left_of(dot(left_of(gram), right, (1, 0))), right, (1, 0))
            total = mix if total is None else dot(left_of(total), right, (1, 0))
    ortho = dot(left_of(grads * scale), right_of(total), (1, 0))
    out[...] = dot(left_of(ortho), right, (1, 0)).astype(out.dtype)


def finish_body(slots, group, w_ref, rows_ref, out):
    heads = w_ref.shape[1]
    for m in range(3):
        for h in range(heads):
            weights = w_ref[m, h]
            summed = weights + rows_ref[index_of((m + first_owner(h)) % slots, h, slots)].astype(f32)
            old = jnp.sqrt(jnp.sum(weights * weights, axis=1, keepdims=True))
            new = lax.rsqrt(jnp.sum(summed * summed, axis=1, keepdims=True) + epsilon)
            out[m, h] = summed * (old * new)


def attend_body(heads, tokens, q_ref, own_ref, back_ref, out):
    padded = own_ref.shape[0]
    span = heads * HD
    column = lax.broadcasted_iota(jnp.int32, (1, 2 * padded), 1)
    place = position()
    first = (place[0] == 0) & (place[1] == 0)
    stop = jnp.where(first, padded, padded + tokens)
    live = (column < tokens) | ((column >= padded) & (column < stop))
    for h in range(heads):
        cols = slice(h * HD, (h + 1) * HD)
        key = jnp.concatenate([own_ref[:, cols], back_ref[:, cols]], axis=0)
        vcols = slice(span + h * HD, span + (h + 1) * HD)
        value = jnp.concatenate([own_ref[:, vcols], back_ref[:, vcols]], axis=0)
        scores = dot(q_ref[:, cols], key, (1, 1)) * (HD ** (-0.5))
        scores = jnp.where(live, scores, -1e30)
        weights = jnp.exp(scores - jnp.max(scores, axis=1, keepdims=True))
        probs = (weights / jnp.sum(weights, axis=1, keepdims=True)).astype(bf16)
        out[:, cols] = dot(probs, value, (1, 0))


def assemble_body(heads, slots, out, squares):
    for h in range(heads):
        out[:, h * HD : (h + 1) * HD] = slots[h]
    fast = out[...].astype(f32)
    squares[...] = dot(jnp.ones((8, heads * HD), f32), fast * fast, (1, 1), highest)


def block_body(features, gain_ref, attended_ref, fast_ref, *refs):
    squares, out = refs[:-1], refs[-1]
    total = squares[0][...]
    for other in squares[1:]:
        total = total + other[...]
    pick = (lax.broadcasted_iota(jnp.int32, (8, HD), 0) == 0).astype(f32)
    spread = dot(total, pick, (0, 0), highest) * (1.0 / features)
    scale = lax.rsqrt(spread + epsilon)
    for h in range(fast_ref.shape[1] // HD):
        cols = slice(h * HD, (h + 1) * HD)
        out[:, cols] = (
            attended_ref[:, cols] + fast_ref[:, cols].astype(f32) * gain_ref[:, cols] * scale
        ).astype(bf16)


def on_device(queries, keys, values, rates, frame_update, fast_weights, gain):
    tokens = queries.shape[0]
    heads = queries.shape[1] // HD
    rows_local = fast_weights.shape[2]
    group, nh = GROUP, lax.axis_size("head")
    nz = lax.axis_size("ctx") // group
    count = nz * group
    hidden = count * rows_local
    padded = -(-tokens // 16) * 16
    span = heads * HD

    def whole(*shape):
        return pl.BlockSpec(shape, lambda i: (0,) * len(shape))

    low_shape = (count, 3, rows_local, HD)
    low = call(
        functools.partial(cast_body, heads, group), sds(low_shape, bf16), flops=1e6
    )(fast_weights)
    prepared = pl.pallas_call(
        functools.partial(prep_body, heads, group, tokens),
        grid=(1,),
        out_shape=[sds((padded, 2 * span), bf16)]
        + [sds((tokens, 3 * HD), bf16)] * group,
        in_specs=[pl.BlockSpec(memory_space=pl.ANY), whole(1, 1)]
        + [whole(heads, -(-padded // 128) * 128)]
        + [whole(padded, span)] * 3,
        out_specs=[whole(padded, 2 * span)] + [whole(tokens, 3 * HD)] * group,
        scratch_shapes=[pltpu.VMEM((padded, span), bf16)],
        compiler_params=pltpu.CompilerParams(vmem_limit_bytes=VMEM_LIMIT),
    )(low, frame_update.reshape(1, 1), rates.T, keys, values, queries)
    kv_own, *token_slots = prepared

    weights = lax.all_to_all(low, "ctx", 0, 0, tiled=True, axis_index_groups=[listed(nz)])
    if rows_local % 16:
        weights = weights.transpose(1, 0, 2, 3).reshape(3, hidden, HD)
    for d in served(group)[1:]:
        pairs = [(s, s ^ d) for s in range(count) if (s ^ d) % group < heads]
        token_slots[d] = lax.ppermute(token_slots[d], "ctx", pairs)

    last = group // 2
    early_slots = [d for d in served(group) if d != last]
    early_grads, early_fast = call(
        functools.partial(early_body, len(early_slots)),
        [sds((3, hidden, HD), f32), sds((len(early_slots), padded, HD), bf16)],
        scratch=gradient_scratch(len(early_slots), padded, hidden) + apply_scratch(padded, hidden),
        flops=1e9,
    )(*(token_slots[d] for d in early_slots), weights)
    partials = list(
        call(
            functools.partial(late_body, group, nz),
            [sds((hidden, HD), bf16)] * nz,
            scratch=[pltpu.VMEM((3, hidden, HD), bf16)] + gradient_scratch(1, padded, hidden),
            flops=5e8,
        )(token_slots[last], weights, early_grads)
    )
    weights, partials[0] = lax.optimization_barrier((weights, partials[0]))
    for d in served(nz)[1:]:
        pairs = []
        for z in range(nz):
            pairs += [
                (z * group + j, (z ^ d) * group + j)
                for j in range(heads)
                if ((z ^ d) - first_owner(j)) % nz < 3
            ]
        partials[d] = lax.ppermute(partials[d], "ctx", pairs)

    fast_slots = call(
        functools.partial(late_apply_body, early_slots, last),
        sds((group, padded, HD), bf16),
        scratch=apply_scratch(padded, hidden),
        flops=1e3,
        moved=1024,
    )(token_slots[last], weights, early_fast)
    kv_own, partials[0], fast_slots = lax.optimization_barrier((kv_own, partials[0], fast_slots))
    fast_slots = lax.all_to_all(
        fast_slots, "ctx", 0, 0, tiled=True,
        axis_index_groups=[[z * group + j for j in range(group)] for z in range(nz)],
    )

    ring = [(i, i + 1) for i in range(count - 1)]
    kv_back = lax.ppermute(kv_own, "ctx", ring)

    ortho = call(functools.partial(ortho_body, heads, nz), sds((hidden, HD), bf16), flops=1e9)(
        *(partials[d] for d in served(nz))
    )
    queries, ortho = lax.optimization_barrier((queries, ortho))
    rows = lax.all_to_all(
        ortho.reshape(count, rows_local, HD), "ctx", 0, 0, tiled=True,
        axis_index_groups=[listed(nz)],
    )
    new_weights = call(
        functools.partial(finish_body, nz, group), sds(fast_weights.shape, f32), flops=1e6
    )(fast_weights, rows)

    attended = pl.pallas_call(
        functools.partial(attend_body, heads, tokens),
        grid=(1,),
        out_shape=sds((padded, span), f32),
        in_specs=[whole(padded, span)] + [whole(padded, 2 * span)] * 2,
        out_specs=whole(padded, span),
        compiler_params=pltpu.CompilerParams(vmem_limit_bytes=VMEM_LIMIT),
    )(queries, kv_own, kv_back)
    fast, squares = call(
        functools.partial(assemble_body, heads),
        [sds((padded, span), bf16), sds((8, padded), f32)],
        flops=1e7,
    )(fast_slots)
    all_squares = [squares] + [
        lax.ppermute(squares, "head", [(s, (s + d) % nh) for s in range(nh)]) for d in range(1, nh)
    ]
    block_out = pl.pallas_call(
        functools.partial(block_body, span * nh),
        grid=(1,),
        out_shape=sds((tokens, span), bf16),
        in_specs=[whole(1, span), whole(padded, span), whole(padded, span)]
        + [whole(8, padded)] * nh,
        out_specs=whole(padded, span),
        compiler_params=pltpu.CompilerParams(vmem_limit_bytes=VMEM_LIMIT),
    )(gain.reshape(1, span), attended, fast, *all_squares)
    return (block_out, new_weights)


def solution(mesh):
    placed = (
        P("ctx", "head"),
        P("ctx", "head"),
        P("ctx", "head"),
        P("ctx", "head"),
        P("ctx"),
        P(None, "head", "ctx", None),
        P("head"),
    )
    return jax.shard_map(
        on_device,
        mesh=mesh,
        in_specs=placed,
        out_specs=(P("ctx", "head"), P(None, "head", "ctx", None)),
        check_vma=False,
    )
```

```python
import functools

import jax
import jax.numpy as jnp
from jax import lax
from jax.experimental import pallas as pl
from jax.experimental.pallas import tpu as pltpu
from jax.sharding import PartitionSpec as P

HD = 128
NS_STEPS = 5

epsilon = 1e-06
quintic_a = 3.4445
quintic_b = -4.775
quintic_c = 2.0315
highest = lax.Precision.HIGHEST
f32 = jnp.float32
bf16 = jnp.bfloat16
VMEM_LIMIT = 24 * 1024 * 1024


def dot(a, b, contract, precision=None):
    return lax.dot_general(
        a, b, ((contract[:1], contract[1:]), ((), ())),
        precision=precision, preferred_element_type=f32,
    )


def call(body, outs, scratch=(), in_specs=None, flops=1e8, moved=1 << 20, **kw):
    given = {} if in_specs is None else {"in_specs": in_specs}
    return pl.pallas_call(
        body,
        out_shape=outs,
        **given,
        scratch_shapes=list(scratch),
        compiler_params=pltpu.CompilerParams(vmem_limit_bytes=VMEM_LIMIT),
        cost_estimate=pl.CostEstimate(flops=int(flops), bytes_accessed=moved, transcendentals=0),
        **kw,
    )


def sds(shape, dtype):
    return jax.ShapeDtypeStruct(shape, dtype)


def served(n):
    return [0] + list(range(n - 1, 0, -1))


def owner(m, h):
    return m + (h & 1) * min(m, 1)


def owned(z, h):
    odd = h & 1
    return jnp.where((odd == 1) & (z == 1), 3, z - odd * jnp.minimum(z, 1))


GROUP = 4


def position():
    return lax.axis_index("ctx") // GROUP, lax.axis_index("ctx") % GROUP


def index_of(z, j, slots):
    return (slots // 2 - z) % slots * GROUP + j


def listed(slots):
    return [(slots // 2 - i) % slots * GROUP + j for i in range(slots) for j in range(GROUP)]


def sigmoid(x):
    return 0.5 * jnp.tanh(0.5 * x) + 0.5


def cast_body(heads, group, w_ref, w_out):
    slots = w_out.shape[0] // group
    for j in range(group):
        for m in range(3):
            low = w_ref[m, min(j, heads - 1)].astype(bf16)
            for z in range(slots):
                w_out[index_of(z, j, slots), m] = low


def prep_body(
    heads, group, tokens, after, update, rate_ref, k_ref, v_ref, q_ref, kv_out, *outs
):
    token_outs, targets = outs[:-1], outs[-1]
    padded = kv_out.shape[0]
    place = position()
    valid = lax.broadcasted_iota(jnp.int32, (padded, 1), 0) < tokens
    none = jnp.zeros((), bf16)
    keep = update[...].astype(f32)
    lane_head = lax.broadcasted_iota(jnp.int32, (heads, heads * HD), 1) // HD
    row = lax.broadcasted_iota(jnp.int32, (heads, heads * HD), 0)
    rate = dot(rate_ref[...], (row == lane_head).astype(f32), (0, 0), highest)[:padded]
    targets[...] = ((rate * keep) * v_ref[...].astype(f32)).astype(bf16)
    for d in range(group):
        head = jnp.minimum(place[1] ^ d, heads - 1)
        cols = pl.ds(pl.multiple_of(head * HD, HD), HD)
        for i, source in enumerate((k_ref, targets, q_ref)):
            token_outs[d][:, i * HD : (i + 1) * HD] = source[:tokens, cols]
    kv_out[:, : heads * HD] = jnp.where(valid, k_ref[...], none)
    kv_out[:, heads * HD :] = jnp.where(valid, v_ref[...], none)


def gradients(token_refs, w_ref, k_all, t_all, staged, deltas):
    tokens = token_refs[0].shape[0]
    padded = -(-tokens // 16) * 16
    width = k_all.shape[0]
    filled = len(token_refs) * padded
    for i, ref in enumerate(token_refs):
        for part, rows in enumerate((k_all, t_all)):
            rows[(i + 1) * padded - 16 : (i + 1) * padded] = jnp.zeros((16, HD), bf16)
            rows[i * padded : i * padded + tokens] = ref[:, part * HD : (part + 1) * HD]
    if width > filled:
        k_all[filled:] = jnp.zeros((width - filled, HD), bf16)
        t_all[filled:] = jnp.zeros((width - filled, HD), bf16)
    hidden = deltas.shape[1]
    w1, w3, w2 = (weight_rows(w_ref, m, 0, hidden) for m in range(3))
    tall = 64
    for left in range(0, width, staged.shape[3]):
        right = min(left + staged.shape[3], width)
        cols, used = slice(left, right), slice(0, right - left)
        stage = staged.at[(left // staged.shape[3]) % staged.shape[0]]
        stage[0, :, used] = dot(w1, k_all[cols], (1, 1))
        stage[1, :, used] = dot(w3, k_all[cols], (1, 1))
        stage[2, :, used] = dot(w2, t_all[cols], (1, 1))
        for start in range(0, hidden, tall):
            rows = slice(start, start + tall)
            pre_one, pre_three, back = (stage[i, rows, used] for i in range(3))
            sig = sigmoid(pre_one)
            gate = pre_one * sig
            deltas[2, rows, cols] = (gate * pre_three).astype(bf16)
            deltas[1, rows, cols] = (back * gate).astype(bf16)
            deltas[0, rows, cols] = (
                (back * pre_three) * (sig * (1.0 + pre_one * (1.0 - sig)))
            ).astype(bf16)
    return (
        dot(deltas[0], k_all[...], (1, 0)),
        dot(deltas[1], k_all[...], (1, 0)),
        dot(deltas[2], t_all[...], (1, 0)),
    )


def gradient_scratch(slots, padded, hidden):
    width = -(-slots * padded // 128) * 128
    return [
        pltpu.VMEM((width, HD), bf16),
        pltpu.VMEM((width, HD), bf16),
        pltpu.VMEM((2, 3, hidden, 256), f32),
        pltpu.VMEM((3, hidden, width), bf16),
    ]


def apply_tokens(token_ref, w_ref, stage, act, held):
    hidden = act.shape[1]
    tall = 16
    w1, w3, w2 = (weight_rows(w_ref, m, 0, hidden) for m in range(3))
    held[held.shape[0] - 16 :] = jnp.zeros((16, HD), bf16)
    held[: token_ref.shape[0]] = token_ref[:, 2 * HD :]
    query = held[...]
    stage[0] = dot(query, w1, (1, 1))
    stage[1] = dot(query, w3, (1, 1))
    for start in range(0, query.shape[0], tall):
        rows = slice(start, start + tall)
        proj = stage[0, rows]
        act[rows] = (proj * sigmoid(proj) * stage[1, rows]).astype(bf16)
    return dot(act[...], w2, (1, 0)).astype(bf16)


def apply_scratch(padded, hidden):
    return [
        pltpu.VMEM((2, 2, padded, hidden), f32),
        pltpu.VMEM((2, padded, hidden), bf16),
        pltpu.VMEM((2, padded, HD), bf16),
    ]


def early_body(count, *refs):
    token_refs, w_ref = refs[:count], refs[count]
    grads, fast = refs[count + 1 : count + 3]
    scratch, (staged, acts, held) = refs[count + 3 : -3], refs[-3:]
    for m, grad in enumerate(gradients(token_refs, w_ref, *scratch)):
        grads[m] = grad
    for i, ref in enumerate(token_refs):
        fast[i] = apply_tokens(ref, w_ref, *(buffer.at[i % 2] for buffer in (staged, acts, held)))


def late_body(group, slots, token_ref, w_ref, early, *refs):
    place = position()
    outs, sums, scratch = refs[:slots], refs[slots], refs[slots + 1 :]
    for m, grad in enumerate(gradients([token_ref], w_ref, *scratch)):
        sums[m] = (early[m] + grad).astype(bf16)
    for d in range(slots):
        matrix = owned(place[0] ^ d, place[1])
        chosen = sums[jnp.minimum(matrix, 2)]
        outs[d][...] = jnp.where(matrix < 3, chosen, jnp.zeros_like(chosen))


def late_apply_body(early_slots, last, token_ref, w_ref, early, out, staged, acts, held):
    place = position()
    for i, d in enumerate(early_slots):
        out[place[1] ^ d] = early[i]
    out[place[1] ^ last] = apply_tokens(
        token_ref, w_ref, staged.at[0], acts.at[0], held.at[0]
    )


def weight_rows(w_ref, m, start, block):
    if len(w_ref.shape) == 3:
        return w_ref[m, start : start + block]
    rows = w_ref.shape[2]
    return w_ref[start // rows : (start + block) // rows, m].reshape(block, HD)


def parts_of(x):
    high = x.astype(bf16)
    return high, (x - high.astype(f32)).astype(bf16)


def left_of(x):
    high, low = parts_of(x)
    return jnp.concatenate([high, high, low], axis=1)


def right_of(x):
    high, low = parts_of(x)
    return jnp.concatenate([high, low, high], axis=0)


def ortho_body(heads, *refs):
    place = position()
    busy = (place[1] < heads) & (owned(*place) < 3)

    @pl.when(busy)
    def _():
        orthogonalize(refs[:-1], refs[-1])

    @pl.when(jnp.logical_not(busy))
    def _():
        refs[-1][...] = jnp.zeros(refs[-1].shape, refs[-1].dtype)


def orthogonalize(parts, out):
    grads = parts[0][...].astype(f32)
    for part in parts[1:]:
        grads = grads + part[...].astype(f32)
    eye = (
        lax.broadcasted_iota(jnp.int32, (HD, HD), 0) == lax.broadcasted_iota(jnp.int32, (HD, HD), 1)
    ).astype(f32)
    both = jnp.concatenate(parts_of(grads), axis=1)
    blocks = dot(both, both, (0, 0))
    raw = (blocks[:HD, HD:] + blocks[HD:, :HD]) + blocks[:HD, :HD]
    square = jnp.sum(jnp.sum(raw * eye, axis=0, keepdims=True), axis=1, keepdims=True)
    scale = lax.rsqrt(square + epsilon)
    gram = raw * scale * scale
    total = None
    for step in range(NS_STEPS):
        square_gram = dot(left_of(gram), right_of(gram), (1, 0))
        mix = quintic_a * eye + quintic_b * gram + quintic_c * square_gram
        right = right_of(mix)
        if step < NS_STEPS - 1:
            gram = dot(left_of(dot(left_of(gram), right, (1, 0))), right, (1, 0))
            total = mix if total is None else dot(left_of(total), right, (1, 0))
    ortho = dot(left_of(grads * scale), right_of(total), (1, 0))
    out[...] = dot(left_of(ortho), right, (1, 0)).astype(out.dtype)


def finish_body(slots, group, w_ref, rows_ref, out):
    heads = w_ref.shape[1]
    for m in range(3):
        for h in range(heads):
            weights = w_ref[m, h]
            summed = weights + rows_ref[index_of(owner(m, h), h, slots)].astype(f32)
            old = jnp.sqrt(jnp.sum(weights * weights, axis=1, keepdims=True))
            new = lax.rsqrt(jnp.sum(summed * summed, axis=1, keepdims=True) + epsilon)
            out[m, h] = summed * (old * new)


def attend_body(heads, tokens, q_ref, own_ref, back_ref, out):
    padded = own_ref.shape[0]
    span = heads * HD
    column = lax.broadcasted_iota(jnp.int32, (1, 2 * padded), 1)
    place = position()
    first = (place[0] == 0) & (place[1] == 0)
    stop = jnp.where(first, padded, padded + tokens)
    live = (column < tokens) | ((column >= padded) & (column < stop))
    for h in range(heads):
        cols = slice(h * HD, (h + 1) * HD)
        key = jnp.concatenate([own_ref[:, cols], back_ref[:, cols]], axis=0)
        vcols = slice(span + h * HD, span + (h + 1) * HD)
        value = jnp.concatenate([own_ref[:, vcols], back_ref[:, vcols]], axis=0)
        scores = dot(q_ref[:, cols], key, (1, 1)) * (HD ** (-0.5))
        scores = jnp.where(live, scores, -1e30)
        weights = jnp.exp(scores - jnp.max(scores, axis=1, keepdims=True))
        probs = (weights / jnp.sum(weights, axis=1, keepdims=True)).astype(bf16)
        out[:, cols] = dot(probs, value, (1, 0))


def assemble_body(heads, slots, out, squares):
    for h in range(heads):
        out[:, h * HD : (h + 1) * HD] = slots[h]
    fast = out[...].astype(f32)
    squares[...] = dot(jnp.ones((8, heads * HD), f32), fast * fast, (1, 1), highest)


def block_body(features, gain_ref, attended_ref, fast_ref, *refs):
    squares, out = refs[:-1], refs[-1]
    total = squares[0][...]
    for other in squares[1:]:
        total = total + other[...]
    pick = (lax.broadcasted_iota(jnp.int32, (8, HD), 0) == 0).astype(f32)
    spread = dot(total, pick, (0, 0), highest) * (1.0 / features)
    scale = lax.rsqrt(spread + epsilon)
    for h in range(fast_ref.shape[1] // HD):
        cols = slice(h * HD, (h + 1) * HD)
        out[:, cols] = (
            attended_ref[:, cols] + fast_ref[:, cols].astype(f32) * gain_ref[:, cols] * scale
        ).astype(bf16)


def on_device(queries, keys, values, rates, frame_update, fast_weights, gain):
    tokens = queries.shape[0]
    heads = queries.shape[1] // HD
    rows_local = fast_weights.shape[2]
    group, nh = GROUP, lax.axis_size("head")
    nz = lax.axis_size("ctx") // group
    count = nz * group
    hidden = count * rows_local
    padded = -(-tokens // 16) * 16
    span = heads * HD

    def whole(*shape):
        return pl.BlockSpec(shape, lambda i: (0,) * len(shape))

    low_shape = (count, 3, rows_local, HD)
    low = call(
        functools.partial(cast_body, heads, group), sds(low_shape, bf16), flops=1e6
    )(fast_weights)
    prepared = pl.pallas_call(
        functools.partial(prep_body, heads, group, tokens),
        grid=(1,),
        out_shape=[sds((padded, 2 * span), bf16)]
        + [sds((tokens, 3 * HD), bf16)] * group,
        in_specs=[pl.BlockSpec(memory_space=pl.ANY), whole(1, 1)]
        + [whole(heads, -(-padded // 128) * 128)]
        + [whole(padded, span)] * 3,
        out_specs=[whole(padded, 2 * span)] + [whole(tokens, 3 * HD)] * group,
        scratch_shapes=[pltpu.VMEM((padded, span), bf16)],
        compiler_params=pltpu.CompilerParams(vmem_limit_bytes=VMEM_LIMIT),
    )(low, frame_update.reshape(1, 1), rates.T, keys, values, queries)
    kv_own, *token_slots = prepared

    weights = lax.all_to_all(low, "ctx", 0, 0, tiled=True, axis_index_groups=[listed(nz)])
    if rows_local % 16:
        weights = weights.transpose(1, 0, 2, 3).reshape(3, hidden, HD)
    for d in served(group)[1:]:
        pairs = [(s, s ^ d) for s in range(count) if (s ^ d) % group < heads]
        token_slots[d] = lax.ppermute(token_slots[d], "ctx", pairs)

    last = group // 2
    early_slots = [d for d in served(group) if d != last]
    early_grads, early_fast = call(
        functools.partial(early_body, len(early_slots)),
        [sds((3, hidden, HD), f32), sds((len(early_slots), padded, HD), bf16)],
        scratch=gradient_scratch(len(early_slots), padded, hidden) + apply_scratch(padded, hidden),
        flops=1e9,
    )(*(token_slots[d] for d in early_slots), weights)
    partials = list(
        call(
            functools.partial(late_body, group, nz),
            [sds((hidden, HD), bf16)] * nz,
            scratch=[pltpu.VMEM((3, hidden, HD), bf16)] + gradient_scratch(1, padded, hidden),
            flops=5e8,
        )(token_slots[last], weights, early_grads)
    )
    weights, partials[0] = lax.optimization_barrier((weights, partials[0]))
    for d in served(nz)[1:]:
        pairs = []
        for z in range(nz):
            pairs += [
                (z * group + j, (z ^ d) * group + j)
                for j in range(heads)
                if (z ^ d) in [owner(m, j) for m in range(3)]
            ]
        partials[d] = lax.ppermute(partials[d], "ctx", pairs)

    fast_slots = call(
        functools.partial(late_apply_body, early_slots, last),
        sds((group, padded, HD), bf16),
        scratch=apply_scratch(padded, hidden),
        flops=1e3,
        moved=1024,
    )(token_slots[last], weights, early_fast)
    kv_own, partials[0], fast_slots = lax.optimization_barrier((kv_own, partials[0], fast_slots))
    fast_slots = lax.all_to_all(
        fast_slots, "ctx", 0, 0, tiled=True,
        axis_index_groups=[[z * group + j for j in range(group)] for z in range(nz)],
    )

    ring = [(i, i + 1) for i in range(count - 1)]
    kv_back = lax.ppermute(kv_own, "ctx", ring)

    ortho = call(functools.partial(ortho_body, heads), sds((hidden, HD), bf16), flops=1e9)(
        *(partials[d] for d in served(nz))
    )
    queries, ortho = lax.optimization_barrier((queries, ortho))
    rows = lax.all_to_all(
        ortho.reshape(count, rows_local, HD), "ctx", 0, 0, tiled=True,
        axis_index_groups=[listed(nz)],
    )
    new_weights = call(
        functools.partial(finish_body, nz, group), sds(fast_weights.shape, f32), flops=1e6
    )(fast_weights, rows)

    attended = pl.pallas_call(
        functools.partial(attend_body, heads, tokens),
        grid=(1,),
        out_shape=sds((padded, span), f32),
        in_specs=[whole(padded, span)] + [whole(padded, 2 * span)] * 2,
        out_specs=whole(padded, span),
        compiler_params=pltpu.CompilerParams(vmem_limit_bytes=VMEM_LIMIT),
    )(queries, kv_own, kv_back)
    fast, squares = call(
        functools.partial(assemble_body, heads),
        [sds((padded, span), bf16), sds((8, padded), f32)],
        flops=1e7,
    )(fast_slots)
    all_squares = [squares] + [
        lax.ppermute(squares, "head", [(s, (s + d) % nh) for s in range(nh)]) for d in range(1, nh)
    ]
    block_out = pl.pallas_call(
        functools.partial(block_body, span * nh),
        grid=(1,),
        out_shape=sds((tokens, span), bf16),
        in_specs=[whole(1, span), whole(padded, span), whole(padded, span)]
        + [whole(8, padded)] * nh,
        out_specs=whole(padded, span),
        compiler_params=pltpu.CompilerParams(vmem_limit_bytes=VMEM_LIMIT),
    )(gain.reshape(1, span), attended, fast, *all_squares)
    return (block_out, new_weights)


def solution(mesh):
    placed = (
        P("ctx", "head"),
        P("ctx", "head"),
        P("ctx", "head"),
        P("ctx", "head"),
        P("ctx"),
        P(None, "head", "ctx", None),
        P("head"),
    )
    return jax.shard_map(
        on_device,
        mesh=mesh,
        in_specs=placed,
        out_specs=(P("ctx", "head"), P(None, "head", "ctx", None)),
        check_vma=False,
    )
```

```python
import functools

import jax
import jax.numpy as jnp
from jax import lax
from jax.experimental import pallas as pl
from jax.experimental.pallas import tpu as pltpu
from jax.sharding import PartitionSpec as P

HD = 128
NS_STEPS = 5

epsilon = 1e-06
quintic_a = 3.4445
quintic_b = -4.775
quintic_c = 2.0315
highest = lax.Precision.HIGHEST
f32 = jnp.float32
bf16 = jnp.bfloat16
VMEM_LIMIT = 24 * 1024 * 1024


def dot(a, b, contract, precision=None):
    return lax.dot_general(
        a, b, ((contract[:1], contract[1:]), ((), ())),
        precision=precision, preferred_element_type=f32,
    )


def call(body, outs, scratch=(), in_specs=None, flops=1e8, moved=1 << 20, **kw):
    given = {} if in_specs is None else {"in_specs": in_specs}
    return pl.pallas_call(
        body,
        out_shape=outs,
        **given,
        scratch_shapes=list(scratch),
        compiler_params=pltpu.CompilerParams(vmem_limit_bytes=VMEM_LIMIT),
        cost_estimate=pl.CostEstimate(flops=int(flops), bytes_accessed=moved, transcendentals=0),
        **kw,
    )


def sds(shape, dtype):
    return jax.ShapeDtypeStruct(shape, dtype)


def served(n):
    return [0] + list(range(n - 1, 0, -1))


def first_owner(h):
    return h & 1


GROUP = 4


def position():
    return lax.axis_index("ctx") // GROUP, lax.axis_index("ctx") % GROUP


def index_of(z, j, slots):
    return (slots // 2 - z) % slots * GROUP + GROUP - 1 - j


def listed(slots):
    return [(slots // 2 - i) % slots * GROUP + j for i in range(slots) for j in range(GROUP)[::-1]]


def sigmoid(x):
    return 0.5 * jnp.tanh(0.5 * x) + 0.5


def cast_body(heads, group, w_ref, w_out):
    slots = w_out.shape[0] // group
    for j in range(group):
        for m in range(3):
            low = w_ref[m, min(j, heads - 1)].astype(bf16)
            for z in range(slots):
                w_out[index_of(z, j, slots), m] = low


def prep_body(
    heads, group, tokens, after, update, rate_ref, k_ref, v_ref, q_ref, kv_out, *outs
):
    token_outs, targets = outs[:-1], outs[-1]
    padded = kv_out.shape[0]
    place = position()
    valid = lax.broadcasted_iota(jnp.int32, (padded, 1), 0) < tokens
    none = jnp.zeros((), bf16)
    keep = update[...].astype(f32)
    lane_head = lax.broadcasted_iota(jnp.int32, (heads, heads * HD), 1) // HD
    row = lax.broadcasted_iota(jnp.int32, (heads, heads * HD), 0)
    rate = dot(rate_ref[...], (row == lane_head).astype(f32), (0, 0), highest)[:padded]
    targets[...] = ((rate * keep) * v_ref[...].astype(f32)).astype(bf16)
    for d in range(group):
        head = jnp.minimum(place[1] ^ d, heads - 1)
        cols = pl.ds(pl.multiple_of(head * HD, HD), HD)
        for i, source in enumerate((k_ref, targets, q_ref)):
            token_outs[d][:, i * HD : (i + 1) * HD] = source[:tokens, cols]
    kv_out[:, : heads * HD] = jnp.where(valid, k_ref[...], none)
    kv_out[:, heads * HD :] = jnp.where(valid, v_ref[...], none)


def gradients(token_refs, w_ref, k_all, t_all, staged, deltas):
    tokens = token_refs[0].shape[0]
    padded = -(-tokens // 16) * 16
    width = k_all.shape[0]
    filled = len(token_refs) * padded
    for i, ref in enumerate(token_refs):
        for part, rows in enumerate((k_all, t_all)):
            rows[(i + 1) * padded - 16 : (i + 1) * padded] = jnp.zeros((16, HD), bf16)
            rows[i * padded : i * padded + tokens] = ref[:, part * HD : (part + 1) * HD]
    if width > filled:
        k_all[filled:] = jnp.zeros((width - filled, HD), bf16)
        t_all[filled:] = jnp.zeros((width - filled, HD), bf16)
    hidden = deltas.shape[1]
    w1, w3, w2 = (weight_rows(w_ref, m, 0, hidden) for m in range(3))
    tall = 64
    for left in range(0, width, staged.shape[3]):
        right = min(left + staged.shape[3], width)
        cols, used = slice(left, right), slice(0, right - left)
        stage = staged.at[(left // staged.shape[3]) % staged.shape[0]]
        stage[0, :, used] = dot(w1, k_all[cols], (1, 1))
        stage[1, :, used] = dot(w3, k_all[cols], (1, 1))
        stage[2, :, used] = dot(w2, t_all[cols], (1, 1))
        for start in range(0, hidden, tall):
            rows = slice(start, start + tall)
            pre_one, pre_three, back = (stage[i, rows, used] for i in range(3))
            sig = sigmoid(pre_one)
            gate = pre_one * sig
            deltas[2, rows, cols] = (gate * pre_three).astype(bf16)
            deltas[1, rows, cols] = (back * gate).astype(bf16)
            deltas[0, rows, cols] = (
                (back * pre_three) * (sig * (1.0 + pre_one * (1.0 - sig)))
            ).astype(bf16)
    return (
        dot(deltas[0], k_all[...], (1, 0)),
        dot(deltas[1], k_all[...], (1, 0)),
        dot(deltas[2], t_all[...], (1, 0)),
    )


def gradient_scratch(slots, padded, hidden):
    width = -(-slots * padded // 128) * 128
    return [
        pltpu.VMEM((width, HD), bf16),
        pltpu.VMEM((width, HD), bf16),
        pltpu.VMEM((2, 3, hidden, 256), f32),
        pltpu.VMEM((3, hidden, width), bf16),
    ]


def apply_tokens(token_ref, w_ref, stage, act, held):
    hidden = act.shape[1]
    tall = 16
    w1, w3, w2 = (weight_rows(w_ref, m, 0, hidden) for m in range(3))
    held[held.shape[0] - 16 :] = jnp.zeros((16, HD), bf16)
    held[: token_ref.shape[0]] = token_ref[:, 2 * HD :]
    query = held[...]
    stage[0] = dot(query, w1, (1, 1))
    stage[1] = dot(query, w3, (1, 1))
    for start in range(0, query.shape[0], tall):
        rows = slice(start, start + tall)
        proj = stage[0, rows]
        act[rows] = (proj * sigmoid(proj) * stage[1, rows]).astype(bf16)
    return dot(act[...], w2, (1, 0)).astype(bf16)


def apply_scratch(padded, hidden):
    return [
        pltpu.VMEM((2, 2, padded, hidden), f32),
        pltpu.VMEM((2, padded, hidden), bf16),
        pltpu.VMEM((2, padded, HD), bf16),
    ]


def early_body(count, *refs):
    token_refs, w_ref = refs[:count], refs[count]
    grads, fast = refs[count + 1 : count + 3]
    scratch, (staged, acts, held) = refs[count + 3 : -3], refs[-3:]
    for m, grad in enumerate(gradients(token_refs, w_ref, *scratch)):
        grads[m] = grad
    for i, ref in enumerate(token_refs):
        fast[i] = apply_tokens(ref, w_ref, *(buffer.at[i % 2] for buffer in (staged, acts, held)))


def late_body(group, slots, token_ref, w_ref, early, *refs):
    place = position()
    outs, sums, scratch = refs[:slots], refs[slots], refs[slots + 1 :]
    for m, grad in enumerate(gradients([token_ref], w_ref, *scratch)):
        sums[m] = (early[m] + grad).astype(bf16)
    for d in range(slots):
        matrix = lax.rem((place[0] ^ d) - first_owner(place[1]) + slots, slots)
        chosen = sums[jnp.minimum(matrix, 2)]
        outs[d][...] = jnp.where(matrix < 3, chosen, jnp.zeros_like(chosen))


def late_apply_body(early_slots, last, token_ref, w_ref, early, out, staged, acts, held):
    place = position()
    for i, d in enumerate(early_slots):
        out[place[1] ^ d] = early[i]
    out[place[1] ^ last] = apply_tokens(
        token_ref, w_ref, staged.at[0], acts.at[0], held.at[0]
    )


def weight_rows(w_ref, m, start, block):
    if len(w_ref.shape) == 3:
        return w_ref[m, start : start + block]
    rows = w_ref.shape[2]
    return w_ref[start // rows : (start + block) // rows, m].reshape(block, HD)


def parts_of(x):
    high = x.astype(bf16)
    return high, (x - high.astype(f32)).astype(bf16)


def left_of(x):
    high, low = parts_of(x)
    return jnp.concatenate([high, high, low], axis=1)


def right_of(x):
    high, low = parts_of(x)
    return jnp.concatenate([high, low, high], axis=0)


def ortho_body(heads, slots, *refs):
    place = position()
    matrix = lax.rem(place[0] - first_owner(place[1]) + slots, slots)
    owner = (place[1] < heads) & (matrix < 3)

    @pl.when(owner)
    def _():
        orthogonalize(refs[:-1], refs[-1])

    @pl.when(jnp.logical_not(owner))
    def _():
        refs[-1][...] = jnp.zeros(refs[-1].shape, refs[-1].dtype)


def orthogonalize(parts, out):
    grads = parts[0][...].astype(f32)
    for part in parts[1:]:
        grads = grads + part[...].astype(f32)
    eye = (
        lax.broadcasted_iota(jnp.int32, (HD, HD), 0) == lax.broadcasted_iota(jnp.int32, (HD, HD), 1)
    ).astype(f32)
    both = jnp.concatenate(parts_of(grads), axis=1)
    blocks = dot(both, both, (0, 0))
    raw = (blocks[:HD, HD:] + blocks[HD:, :HD]) + blocks[:HD, :HD]
    square = jnp.sum(jnp.sum(raw * eye, axis=0, keepdims=True), axis=1, keepdims=True)
    scale = lax.rsqrt(square + epsilon)
    gram = raw * scale * scale
    total = None
    for step in range(NS_STEPS):
        square_gram = dot(left_of(gram), right_of(gram), (1, 0))
        mix = quintic_a * eye + quintic_b * gram + quintic_c * square_gram
        right = right_of(mix)
        if step < NS_STEPS - 1:
            gram = dot(left_of(dot(left_of(gram), right, (1, 0))), right, (1, 0))
            total = mix if total is None else dot(left_of(total), right, (1, 0))
    ortho = dot(left_of(grads * scale), right_of(total), (1, 0))
    out[...] = dot(left_of(ortho), right, (1, 0)).astype(out.dtype)


def finish_body(slots, group, w_ref, rows_ref, out):
    heads = w_ref.shape[1]
    for m in range(3):
        for h in range(heads):
            weights = w_ref[m, h]
            summed = weights + rows_ref[index_of((m + first_owner(h)) % slots, h, slots)].astype(f32)
            old = jnp.sqrt(jnp.sum(weights * weights, axis=1, keepdims=True))
            new = lax.rsqrt(jnp.sum(summed * summed, axis=1, keepdims=True) + epsilon)
            out[m, h] = summed * (old * new)


def attend_body(heads, tokens, q_ref, own_ref, back_ref, out):
    padded = own_ref.shape[0]
    span = heads * HD
    column = lax.broadcasted_iota(jnp.int32, (1, 2 * padded), 1)
    place = position()
    first = (place[0] == 0) & (place[1] == 0)
    stop = jnp.where(first, padded, padded + tokens)
    live = (column < tokens) | ((column >= padded) & (column < stop))
    for h in range(heads):
        cols = slice(h * HD, (h + 1) * HD)
        key = jnp.concatenate([own_ref[:, cols], back_ref[:, cols]], axis=0)
        vcols = slice(span + h * HD, span + (h + 1) * HD)
        value = jnp.concatenate([own_ref[:, vcols], back_ref[:, vcols]], axis=0)
        scores = dot(q_ref[:, cols], key, (1, 1)) * (HD ** (-0.5))
        scores = jnp.where(live, scores, -1e30)
        weights = jnp.exp(scores - jnp.max(scores, axis=1, keepdims=True))
        probs = (weights / jnp.sum(weights, axis=1, keepdims=True)).astype(bf16)
        out[:, cols] = dot(probs, value, (1, 0))


def assemble_body(heads, slots, out, squares):
    for h in range(heads):
        out[:, h * HD : (h + 1) * HD] = slots[h]
    fast = out[...].astype(f32)
    squares[...] = dot(jnp.ones((8, heads * HD), f32), fast * fast, (1, 1), highest)


def block_body(features, gain_ref, attended_ref, fast_ref, *refs):
    squares, out = refs[:-1], refs[-1]
    total = squares[0][...]
    for other in squares[1:]:
        total = total + other[...]
    pick = (lax.broadcasted_iota(jnp.int32, (8, HD), 0) == 0).astype(f32)
    spread = dot(total, pick, (0, 0), highest) * (1.0 / features)
    scale = lax.rsqrt(spread + epsilon)
    for h in range(fast_ref.shape[1] // HD):
        cols = slice(h * HD, (h + 1) * HD)
        out[:, cols] = (
            attended_ref[:, cols] + fast_ref[:, cols].astype(f32) * gain_ref[:, cols] * scale
        ).astype(bf16)


def on_device(queries, keys, values, rates, frame_update, fast_weights, gain):
    tokens = queries.shape[0]
    heads = queries.shape[1] // HD
    rows_local = fast_weights.shape[2]
    group, nh = GROUP, lax.axis_size("head")
    nz = lax.axis_size("ctx") // group
    count = nz * group
    hidden = count * rows_local
    padded = -(-tokens // 16) * 16
    span = heads * HD

    def whole(*shape):
        return pl.BlockSpec(shape, lambda i: (0,) * len(shape))

    low_shape = (count, 3, rows_local, HD)
    low = call(
        functools.partial(cast_body, heads, group), sds(low_shape, bf16), flops=1e6
    )(fast_weights)
    prepared = pl.pallas_call(
        functools.partial(prep_body, heads, group, tokens),
        grid=(1,),
        out_shape=[sds((padded, 2 * span), bf16)]
        + [sds((tokens, 3 * HD), bf16)] * group,
        in_specs=[pl.BlockSpec(memory_space=pl.ANY), whole(1, 1)]
        + [whole(heads, -(-padded // 128) * 128)]
        + [whole(padded, span)] * 3,
        out_specs=[whole(padded, 2 * span)] + [whole(tokens, 3 * HD)] * group,
        scratch_shapes=[pltpu.VMEM((padded, span), bf16)],
        compiler_params=pltpu.CompilerParams(vmem_limit_bytes=VMEM_LIMIT),
    )(low, frame_update.reshape(1, 1), rates.T, keys, values, queries)
    kv_own, *token_slots = prepared

    weights = lax.all_to_all(low, "ctx", 0, 0, tiled=True, axis_index_groups=[listed(nz)])
    if rows_local % 16:
        weights = weights.transpose(1, 0, 2, 3).reshape(3, hidden, HD)
    for d in served(group)[1:]:
        pairs = [(s, s ^ d) for s in range(count) if (s ^ d) % group < heads]
        token_slots[d] = lax.ppermute(token_slots[d], "ctx", pairs)

    last = group // 2
    early_slots = [d for d in served(group) if d != last]
    early_grads, early_fast = call(
        functools.partial(early_body, len(early_slots)),
        [sds((3, hidden, HD), f32), sds((len(early_slots), padded, HD), bf16)],
        scratch=gradient_scratch(len(early_slots), padded, hidden) + apply_scratch(padded, hidden),
        flops=1e9,
    )(*(token_slots[d] for d in early_slots), weights)
    partials = list(
        call(
            functools.partial(late_body, group, nz),
            [sds((hidden, HD), bf16)] * nz,
            scratch=[pltpu.VMEM((3, hidden, HD), bf16)] + gradient_scratch(1, padded, hidden),
            flops=5e8,
        )(token_slots[last], weights, early_grads)
    )
    weights, partials[0] = lax.optimization_barrier((weights, partials[0]))
    for d in served(nz)[1:]:
        pairs = []
        for z in range(nz):
            pairs += [
                (z * group + j, (z ^ d) * group + j)
                for j in range(heads)
                if ((z ^ d) - first_owner(j)) % nz < 3
            ]
        partials[d] = lax.ppermute(partials[d], "ctx", pairs)

    fast_slots = call(
        functools.partial(late_apply_body, early_slots, last),
        sds((group, padded, HD), bf16),
        scratch=apply_scratch(padded, hidden),
        flops=1e3,
        moved=1024,
    )(token_slots[last], weights, early_fast)
    kv_own, partials[0], fast_slots = lax.optimization_barrier((kv_own, partials[0], fast_slots))
    fast_slots = lax.all_to_all(
        fast_slots, "ctx", 0, 0, tiled=True,
        axis_index_groups=[[z * group + j for j in range(group)] for z in range(nz)],
    )

    ring = [(i, i + 1) for i in range(count - 1)]
    kv_back = lax.ppermute(kv_own, "ctx", ring)

    ortho = call(functools.partial(ortho_body, heads, nz), sds((hidden, HD), bf16), flops=1e9)(
        *(partials[d] for d in served(nz))
    )
    queries, ortho = lax.optimization_barrier((queries, ortho))
    rows = lax.all_to_all(
        ortho.reshape(count, rows_local, HD), "ctx", 0, 0, tiled=True,
        axis_index_groups=[listed(nz)],
    )
    new_weights = call(
        functools.partial(finish_body, nz, group), sds(fast_weights.shape, f32), flops=1e6
    )(fast_weights, rows)

    attended = pl.pallas_call(
        functools.partial(attend_body, heads, tokens),
        grid=(1,),
        out_shape=sds((padded, span), f32),
        in_specs=[whole(padded, span)] + [whole(padded, 2 * span)] * 2,
        out_specs=whole(padded, span),
        compiler_params=pltpu.CompilerParams(vmem_limit_bytes=VMEM_LIMIT),
    )(queries, kv_own, kv_back)
    fast, squares = call(
        functools.partial(assemble_body, heads),
        [sds((padded, span), bf16), sds((8, padded), f32)],
        flops=1e7,
    )(fast_slots)
    all_squares = [squares] + [
        lax.ppermute(squares, "head", [(s, (s + d) % nh) for s in range(nh)]) for d in range(1, nh)
    ]
    block_out = pl.pallas_call(
        functools.partial(block_body, span * nh),
        grid=(1,),
        out_shape=sds((tokens, span), bf16),
        in_specs=[whole(1, span), whole(padded, span), whole(padded, span)]
        + [whole(8, padded)] * nh,
        out_specs=whole(padded, span),
        compiler_params=pltpu.CompilerParams(vmem_limit_bytes=VMEM_LIMIT),
    )(gain.reshape(1, span), attended, fast, *all_squares)
    return (block_out, new_weights)


def solution(mesh):
    placed = (
        P("ctx", "head"),
        P("ctx", "head"),
        P("ctx", "head"),
        P("ctx", "head"),
        P("ctx"),
        P(None, "head", "ctx", None),
        P("head"),
    )
    return jax.shard_map(
        on_device,
        mesh=mesh,
        in_specs=placed,
        out_specs=(P("ctx", "head"), P(None, "head", "ctx", None)),
        check_vma=False,
    )
```
